32 devices in a mesh: dp: 4 (over x, core), fsdp: 8 (over z, y).
Axes of the slice: x: 2, y: 2, z: 4, core: 2. Of those that a mesh axis runs over, the one named last changes fastest.
Arguments:
- block_input: bfloat16 [16384, 1024], P(('dp', 'fsdp')), may hold values from -6 to 6
- in_weight: float32 [1024, 3072], P(('dp', 'fsdp')), may hold values from -0.1875 to 0.1875
- out_weight: float32 [1024, 1024], P(('dp', 'fsdp')), may hold values from -0.1875 to 0.1875
- gate_weight: float32 [1024, 4608], P(('dp', 'fsdp')), may hold values from -0.1875 to 0.1875
- up_weight: float32 [1024, 4608], P(('dp', 'fsdp')), may hold values from -0.1875 to 0.1875
- down_weight: float32 [4608, 1024], P(('dp', 'fsdp')), may hold values from -0.09375 to 0.09375
- norm_gain: float32 [1024], P(('dp', 'fsdp')), may hold values from 0.5 to 1.5
- ffn_gain: float32 [1024], P(('dp', 'fsdp')), may hold values from 0.5 to 1.5
- conv_weight: float32 [1024, 3], P(('dp', 'fsdp')), may hold values from -3 to 3
- seq_starts: int32 [4, 4], P('dp'), may hold values from 0 to 3072, as said below
- cotangent: bfloat16 [16384, 1024], P(('dp', 'fsdp')), may hold values from -6 to 6
Outputs:
- block_output: bfloat16 [16384, 1024], P(('dp', 'fsdp'))
- grad_input: bfloat16 [16384, 1024], P(('dp', 'fsdp'))
- grad_in_weight: float32 [1024, 3072], P(('dp', 'fsdp'))
- grad_out_weight: float32 [1024, 1024], P(('dp', 'fsdp'))
- grad_gate_weight: float32 [1024, 4608], P(('dp', 'fsdp'))
- grad_up_weight: float32 [1024, 4608], P(('dp', 'fsdp'))
- grad_down_weight: float32 [4608, 1024], P(('dp', 'fsdp'))
- grad_norm_gain: float32 [1024], P(('dp', 'fsdp'))
- grad_ffn_gain: float32 [1024], P(('dp', 'fsdp'))
- grad_conv_weight: float32 [1024, 3], P(('dp', 'fsdp'))
The draws below stay inside these ranges and needn't reach their ends.
Inputs may be any that keep to these rules, and one draw needn't show every extreme that they name: `seq_starts`: row g holds the offsets within group g of the sequences packed there, in rising order, each sequence 1024, 2048 or 4096 tokens long, the first at 0; a row with fewer than 4 sequences repeats its last start. Some row holds four sequences.
All inputs are finite; a program needn't handle non-finite values.
Results may differ from the reference program's by a relative error of at most 0.012.
The reference program's roundings to bfloat16 on the way count: a program that leaves them out, or rounds other values in their place, can miss the bound.
Values may be sent and summed in bfloat16 or wider, within the bound.
No kernel may reach another device: no remote copies, remote signals or barrier semaphores. Data moves between devices by JAX's collectives and lax.ppermute only.
A program may use at most 320 MiB of HBM per device.

```python
import jax
import jax.numpy as jnp
from jax import lax

D = 1024
FF = 4608
KERNEL = 3
GROUP = 4096
TOKENS = 16384
N_DP = 4


def draw_seq_starts(key, part):
    key = jax.random.fold_in(key, 7)
    first_key, second_key = jax.random.split(key)
    layouts = jnp.array([[0, 0, 0, 0], [0, 2, 2, 2], [0, 2, 3, 3], [0, 1, 3, 3], [0, 1, 2, 2], [0, 1, 2, 3]], jnp.int32)
    picked = jax.random.randint(first_key, (N_DP,), 0, 6)
    forced = jax.random.randint(second_key, (), 0, N_DP)
    picked = jnp.where(jnp.arange(N_DP) == forced, 5, picked)
    return layouts[picked] * (GROUP // 4)


def block_scale(stream_key, extent, shards, least, high):
    factor_of, own = 1.0, jax.random.fold_in(stream_key, 6)
    for axis_at, parts in shards:
        heights = jnp.exp(jax.random.uniform(jax.random.fold_in(own, axis_at), (parts,), jnp.float32, least / len(shards), high / len(shards)))
        factor_of = factor_of * jnp.repeat(heights, extent[axis_at] // parts).reshape([-1 if axis == axis_at else 1 for axis in range(len(extent))])
    return factor_of


def noise(rng, dims, scale, reach, cuts=(), kind=jnp.bfloat16):
    values = scale * jax.random.normal(rng, dims, jnp.float32)
    if cuts:
        values = values * block_scale(rng, dims, cuts, -0.22, 0.18)
    return jnp.clip(values, -reach, reach).astype(kind)


def setup_inputs(seed: int = 0) -> dict:
    key_list = jax.random.split(jax.random.key(seed), 12)
    return {
        "block_input": noise(key_list[0], (TOKENS, D), 1.0, 6.0, ((0, 32),)),
        "in_weight": noise(key_list[1], (D, 3 * D), D ** -0.5, 0.1875, ((0, 32),), jnp.float32),
        "out_weight": noise(key_list[2], (D, D), D ** -0.5, 0.1875, ((0, 32),), jnp.float32),
        "gate_weight": noise(key_list[3], (D, FF), D ** -0.5, 0.1875, ((0, 32),), jnp.float32),
        "up_weight": noise(key_list[4], (D, FF), D ** -0.5, 0.1875, ((0, 32),), jnp.float32),
        "down_weight": noise(key_list[5], (FF, D), FF ** -0.5, 0.09375, ((0, 32),), jnp.float32),
        "norm_gain": jnp.clip(1.0 + 0.1 * jax.random.normal(key_list[6], (D,), jnp.float32), 0.5, 1.5),
        "ffn_gain": jnp.clip(1.0 + 0.1 * jax.random.normal(key_list[7], (D,), jnp.float32), 0.5, 1.5),
        "conv_weight": noise(key_list[8], (D, KERNEL), 0.6, 3.0, ((0, 32),), jnp.float32),
        "seq_starts": draw_seq_starts(jax.random.fold_in(key_list[11], 71), 0),
        "cotangent": noise(key_list[10], (TOKENS, D), 1.0, 6.0, ((0, 32),)),
    }


@jax.custom_vjp
def low(v):
    return lax.optimization_barrier(v.astype(jnp.bfloat16)).astype(jnp.float32)

@jax.custom_vjp
def low_back(v):
    return v

def low_keep(v):
    return (low(v), None)

def low_pass(kept, grad):
    return (grad,)

def back_keep(v):
    return (v, None)

def back_low(kept, grad):
    return (low(grad),)
low.defvjp(low_keep, low_pass)
low_back.defvjp(back_keep, back_low)
EPS = 1e-05

def matmul(left, right):
    return jnp.dot(left, right, precision=lax.Precision.HIGHEST)

def rms_norm(values, gain):
    scale = lax.rsqrt(lax.optimization_barrier(jnp.mean(values * values, axis=1, keepdims=True)) + EPS)
    return values * scale * gain[None, :]

def reference(block_input, in_weight, out_weight, gate_weight, up_weight, down_weight, norm_gain, ffn_gain, conv_weight, seq_starts, cotangent):

    def forward(inputs, mix_in, mix_out, ffn_gate, ffn_up, ffn_down, gain_mix, gain_ffn, conv_taps):
        mix_in = low(mix_in)
        mix_out = low(mix_out)
        ffn_gate = low(ffn_gate)
        ffn_up = low(ffn_up)
        ffn_down = low(ffn_down)
        gain_mix = low(gain_mix)
        gain_ffn = low(gain_ffn)
        conv_taps = low(conv_taps)

        def one_group(pair):
            rows, starts = pair
            normed = low(rms_norm(rows, gain_mix))
            projected = low_back(matmul(normed, mix_in))
            b_branch = projected[:, :D]
            c_branch = projected[:, D:2 * D]
            x_branch = projected[:, 2 * D:]
            product = b_branch * x_branch
            position = jnp.arange(GROUP, dtype=jnp.int32)
            begin = lax.optimization_barrier(jnp.max(jnp.where(starts[None, :] <= position[:, None], starts[None, :], 0), axis=1))
            offset = position - begin
            mixed = jnp.zeros((GROUP, D), jnp.float32)
            for lag in range(KERNEL):
                if lag > 0:
                    moved = jnp.concatenate([jnp.zeros((lag, D), jnp.float32), product[:GROUP - lag]], 0)
                else:
                    moved = product
                valid = (offset >= lag).astype(jnp.float32)[:, None]
                mixed = mixed + valid * conv_taps[:, KERNEL - 1 - lag][None, :] * moved
            gated = low(c_branch * mixed)
            hidden = rows + low_back(matmul(gated, mix_out))
            normed_ffn = low(rms_norm(hidden, gain_ffn))
            gate_pre = low_back(matmul(normed_ffn, ffn_gate))
            rise_pre = low_back(matmul(normed_ffn, ffn_up))
            swiglu = low(jax.nn.silu(gate_pre) * rise_pre)
            return hidden + matmul(swiglu, ffn_down)
        grouped = lax.map(jax.checkpoint(one_group), (inputs.reshape(N_DP, GROUP, D), seq_starts))
        return grouped.reshape(TOKENS, D)
    result, pull = jax.vjp(forward, block_input.astype(jnp.float32), in_weight, out_weight, gate_weight, up_weight, down_weight, norm_gain, ffn_gain, conv_weight)
    grads = pull(cotangent.astype(jnp.float32))
    return (result.astype(jnp.bfloat16), grads[0].astype(jnp.bfloat16), grads[1], grads[2], grads[3], grads[4], grads[5], grads[6], grads[7], grads[8])
```

```python
import functools

import jax
import jax.numpy as jnp
from jax import lax
from jax.experimental import pallas as pl
from jax.experimental.pallas import tpu as pltpu
from jax.sharding import PartitionSpec as P

EPS = 1e-05
BF = jnp.bfloat16
F32 = jnp.float32


class Axis:
    def __init__(self, name, stride, size):
        self.name, self.stride, self.size = name, stride, size
        self.here = (lax.axis_index(name) // stride) % size

    def shift(self, value, by):
        total = lax.axis_size(self.name)
        pairs = []
        for i in range(total):
            at = (i // self.stride) % self.size
            pairs.append((i, i + ((at + by) % self.size - at) * self.stride))
        return lax.ppermute(value, self.name, pairs)


def passed_along(shard, axis, by):
    peers = lax.axis_size(axis)
    pairs = [(i, i + by) for i in range(peers) if 0 <= i + by < peers]
    return lax.ppermute(shard, axis, pairs)


def contract_rows(left, right):
    return lax.dot_general(
        left, right, (((0,), (0,)), ((), ())), preferred_element_type=F32
    )


def contract_cols(left, right):
    return lax.dot_general(
        left, right, (((1,), (1,)), ((), ())), preferred_element_type=F32
    )


def times(left, right):
    return jnp.dot(left, right, preferred_element_type=F32)


def spread(buffer, axis):
    return jnp.stack([buffer] + [axis.shift(buffer, by) for by in range(1, axis.size)])


def place_body(plan, nz, ny, nx, kept, here_ref, *refs):
    sources, (out_ref, sems) = refs[:-2], refs[-2:]
    x, y, z = here_ref[0], here_ref[1], here_ref[2]
    copies = []
    for source, (order, first_z, count_z) in zip(sources, plan, strict=True):
        for dx in range(nx):
            for dy in range(ny):
                for dz in range(count_z):
                    at_x = lax.rem(x + nx - dx, nx)
                    at_y = lax.rem(y + ny - dy, ny)
                    at_z = lax.rem(z + nz - (first_z + dz), nz)
                    lead = (dx, dy, dz) if order == "xy" else (dy, dx, dz)
                    if kept == 2:
                        target = out_ref.at[at_x, :, at_z, at_y]
                    else:
                        target = out_ref.at[at_x, 0, at_z, at_y]
                    copies.append((source.at[lead], target))
    started = []
    for i, (source, target) in enumerate(copies):
        copy = pltpu.make_async_copy(source, target, sems.at[i])
        copy.start()
        started.append(copy)
    for copy in started:
        copy.wait()


def place(here, sources, plan, sizes, kept, rows, columns):
    nx, ny, nz = sizes
    count = nx * ny * nz
    out = pl.pallas_call(
        functools.partial(place_body, plan, nz, ny, nx, kept),
        out_shape=jax.ShapeDtypeStruct((nx, kept, nz, ny, rows, columns), sources[0].dtype),
        in_specs=[pl.BlockSpec(memory_space=pltpu.SMEM)]
        + [pl.BlockSpec(memory_space=pl.ANY)] * len(sources),
        out_specs=pl.BlockSpec(memory_space=pl.ANY),
        scratch_shapes=[pltpu.SemaphoreType.DMA((count,))],
        cost_estimate=pl.CostEstimate(
            flops=0, bytes_accessed=4 * count * kept * rows * columns, transcendentals=0
        ),
    )(here, *sources)
    return out.reshape(nx * kept * nz * ny * rows, columns)


def gather(block, here, ax, ay, az):
    kept, rows, columns = block.shape
    lower = az.size // 2
    parts = [block] + [az.shift(block, by) for by in range(1, az.size)]
    first, second = jnp.stack(parts[:lower]), jnp.stack(parts[lower:])
    first = spread(spread(first, ax), ay)
    second = spread(spread(second, ay), ax)
    shape = (rows, columns) if kept == 1 else (kept, rows, columns)
    first = first.reshape(first.shape[:3] + shape)
    second = second.reshape(second.shape[:3] + shape)
    plan = (("yx", 0, lower), ("xy", lower, az.size - lower))
    return place(here, (first, second), plan, (ax.size, ay.size, az.size), kept, rows, columns)


def folded(value, axis, dim):
    own = lax.dynamic_index_in_dim(value, axis.here, dim, keepdims=False).astype(F32)
    for by in range(1, axis.size):
        there = lax.rem(axis.here + by, axis.size)
        own = own + axis.shift(
            lax.dynamic_index_in_dim(value, there, dim, keepdims=False), by
        ).astype(F32)
    return own


def scatter(whole, kept, ax, ay, az):
    columns = whole.shape[1]
    rows = whole.shape[0] // (ax.size * kept * az.size * ay.size)
    whole = whole.reshape(ax.size, kept, az.size, ay.size, rows, columns)
    lower = az.size // 2
    first, second = whole[:, :, :lower], whole[:, :, lower:]
    first = folded(folded(first, ay, 3).astype(BF), ax, 0).astype(BF)
    second = folded(folded(second, ax, 0).astype(BF), ay, 2).astype(BF)
    return folded(jnp.concatenate([first, second], 1), az, 1)


def core_columns(matrix, groups, which):
    rows, columns = matrix.shape
    blocks = matrix.reshape(rows, groups, 2, columns // (2 * groups))
    return lax.dynamic_index_in_dim(blocks, which, 2, keepdims=False).reshape(rows, columns // 2)


def both_columns(mine, other, groups, core):
    rows, half = mine.shape
    mine = mine.reshape(rows, groups, half // groups)
    other = other.reshape(rows, groups, half // groups)
    low = jnp.where(core == 0, mine, other)
    high = jnp.where(core == 0, other, mine)
    return jnp.stack([low, high], 2).reshape(rows, 2 * half)


def per_device(
    block_input,
    in_weight,
    out_weight,
    gate_weight,
    up_weight,
    down_weight,
    norm_gain,
    ffn_gain,
    conv_weight,
    seq_starts,
    cotangent,
):
    nd, nf = lax.axis_size("dp"), lax.axis_size("fsdp")
    ny = 1
    while (2 * ny) ** 2 <= nf:
        ny *= 2
    nx, nz = nd // 2, nf // ny
    ac, ax = Axis("dp", 1, 2), Axis("dp", 2, nx)
    ay, az = Axis("fsdp", 1, ny), Axis("fsdp", ny, nz)
    core = ac.here
    here = jnp.stack([ax.here, ay.here, az.here]).astype(jnp.int32)

    def swap(value):
        return ac.shift(value, 1)

    tokens, width = block_input.shape
    rows = in_weight.shape[0]
    hidden = gate_weight.shape[1] // 2
    feats = width // 2

    small = jnp.concatenate(
        [norm_gain[:, None], ffn_gain[:, None], conv_weight, jnp.zeros((rows, 123), F32)], 1
    ).astype(BF)
    in_low, gate_low, up_low = (w.astype(BF) for w in (in_weight, gate_weight, up_weight))

    def halves(which):
        return jnp.concatenate(
            [
                core_columns(in_low, 3 * nx, which),
                small,
                core_columns(gate_low, nx, which),
                core_columns(up_low, nx, which),
            ],
            1,
        )

    mine, theirs = halves(core), swap(halves(1 - core))
    pair = jnp.stack([jnp.where(core == 0, mine, theirs), jnp.where(core == 0, theirs, mine)])
    cut = 3 * feats + 128
    x_all = jnp.concatenate([block_input, swap(block_input)], 0)
    dy_all = jnp.concatenate([cotangent, swap(cotangent)], 0)
    starts = jnp.concatenate([seq_starts, swap(seq_starts)], 0)

    in_full = gather(pair[:, :, :cut], here, ax, ay, az)
    mix_out = gather(out_weight.astype(BF)[None], here, ax, ay, az)
    ffn_gate = gather(pair[:, :, cut : cut + hidden], here, ax, ay, az)
    ffn_up = gather(pair[:, :, cut + hidden :], here, ax, ay, az)
    ffn_down = gather(down_weight.astype(BF)[None], here, ax, ay, az)
    mix_in = in_full[:, : 3 * feats]
    tiny = in_full[:, 3 * feats : 3 * feats + 8].astype(F32)
    gain_mix, gain_ffn = tiny[:, 0], tiny[:, 1]
    taps = lax.dynamic_index_in_dim(
        tiny[:, 2:5].reshape(nx, 2, feats // nx, 3), core, 1, keepdims=False
    ).reshape(feats, 3)

    inputs = x_all.astype(F32)
    scale_mix = lax.rsqrt(jnp.mean(inputs * inputs, axis=1, keepdims=True) + EPS)
    normed_mix = (inputs * scale_mix * gain_mix[None, :]).astype(BF)
    projected = times(normed_mix, mix_in)
    b_branch = projected[:, :feats]
    c_branch = projected[:, feats : 2 * feats]
    x_branch = projected[:, 2 * feats :]
    product = (b_branch * x_branch).reshape(2, tokens, feats)
    earlier = passed_along(product[:, tokens - 2 :], "fsdp", 1)
    padded = jnp.concatenate([earlier, product], 1)
    position = lax.axis_index("fsdp") * tokens + jnp.arange(tokens + 2, dtype=jnp.int32)

    def offsets(at):
        reached = starts[:, None, :] <= at[None, :, None]
        return at[None, :] - jnp.max(jnp.where(reached, starts[:, None, :], 0), axis=2)

    own_offset = offsets(position[:tokens])
    mixed = jnp.zeros((2, tokens, feats), F32)
    for lag in range(3):
        valid = (own_offset >= lag).astype(F32)[:, :, None]
        mixed = mixed + valid * taps[:, 2 - lag] * padded[:, 2 - lag : 2 - lag + tokens]
    mixed = mixed.reshape(2 * tokens, feats)
    gated = (c_branch * mixed).astype(BF)
    mixer = times(gated, mix_out)
    own_inputs = inputs[:tokens]
    h = own_inputs + (mixer[:tokens] + swap(mixer[tokens:]))

    scale_ffn = lax.rsqrt(jnp.mean(h * h, axis=1, keepdims=True) + EPS)
    normed_own = (h * scale_ffn * gain_ffn[None, :]).astype(BF)
    normed_ffn = jnp.concatenate([normed_own, swap(normed_own)], 0)
    gate_pre = times(normed_ffn, ffn_gate)
    rise_pre = times(normed_ffn, ffn_up)
    sigma = jax.nn.sigmoid(gate_pre)
    swiglu = (gate_pre * sigma * rise_pre).astype(BF)
    grad_down = contract_rows(swiglu, dy_all).astype(BF)
    fed = times(swiglu, ffn_down)
    block_output = (h + (fed[:tokens] + swap(fed[tokens:]))).astype(BF)
    part_down = scatter(grad_down, 1, ax, ay, az)[0]

    grad_swiglu = contract_cols(dy_all, ffn_down)
    grad_gate = (grad_swiglu * rise_pre * sigma * (1.0 + gate_pre * (1.0 - sigma))).astype(BF)
    grad_rise = (grad_swiglu * gate_pre * sigma).astype(BF)
    part_gate = scatter(contract_rows(normed_ffn, grad_gate).astype(BF), 2, ax, ay, az)
    part_rise = scatter(contract_rows(normed_ffn, grad_rise).astype(BF), 2, ax, ay, az)
    grad_normed = contract_cols(grad_gate, ffn_gate) + contract_cols(grad_rise, ffn_up)
    grad_normed = grad_normed[:tokens] + swap(grad_normed[tokens:])
    grad_gain_ffn = jnp.sum(grad_normed * h * scale_ffn, axis=0)
    weighted = grad_normed * gain_ffn[None, :]
    grad_hidden = (
        cotangent.astype(F32)
        + scale_ffn * weighted
        - h * scale_ffn**3 * jnp.mean(weighted * h, axis=1, keepdims=True)
    )

    hidden_low = grad_hidden.astype(BF)
    hidden_low = jnp.concatenate([hidden_low, swap(hidden_low)], 0)
    part_out = scatter(contract_rows(gated, hidden_low).astype(BF), 1, ax, ay, az)[0]
    grad_gated = contract_cols(hidden_low, mix_out)
    grad_c = grad_gated * mixed
    grad_mixed = (grad_gated * c_branch).reshape(2, tokens, feats)
    later = passed_along(grad_mixed[:, :2], "fsdp", -1)
    trailing = jnp.concatenate([grad_mixed, later], 1)
    next_offset = offsets(position)
    grad_product = jnp.zeros((2, tokens, feats), F32)
    tap_grads = []
    for lag in range(3):
        ahead = (next_offset[:, lag : lag + tokens] >= lag).astype(F32)[:, :, None]
        grad_product = grad_product + ahead * taps[:, 2 - lag] * trailing[:, lag : lag + tokens]
    for column in range(3):
        valid = (own_offset >= 2 - column).astype(F32)[:, :, None]
        tap_grads.append(
            jnp.sum(valid * grad_mixed * padded[:, column : column + tokens], axis=(0, 1))
        )
    grad_product = grad_product.reshape(2 * tokens, feats)
    grad_projected = jnp.concatenate(
        [grad_product * x_branch, grad_c, grad_product * b_branch], 1
    ).astype(BF)
    part_in = scatter(contract_rows(normed_mix, grad_projected).astype(BF), 2, ax, ay, az)
    grad_normed_mix = contract_cols(grad_projected, mix_in)
    grad_normed_mix = grad_normed_mix[:tokens] + swap(grad_normed_mix[tokens:])
    own_scale = scale_mix[:tokens]
    grad_gain_mix = jnp.sum(grad_normed_mix * own_inputs * own_scale, axis=0)
    weighted_mix = grad_normed_mix * gain_mix[None, :]
    grad_inputs = (
        grad_hidden
        + own_scale * weighted_mix
        - own_inputs * own_scale**3 * jnp.mean(weighted_mix * own_inputs, axis=1, keepdims=True)
    )

    tap_rows = jnp.stack(tap_grads).reshape(3, nx, 1, feats // nx)
    on_core = (jnp.arange(2) == core).astype(F32)[None, None, :, None]
    tap_rows = (tap_rows * on_core).reshape(3, width)
    terms = jnp.concatenate([grad_gain_mix[None], grad_gain_ffn[None], tap_rows], 0)
    for axis in (ac, ax, ay, az):
        gone = terms
        for by in range(1, axis.size):
            terms = terms + axis.shift(gone, by)
    at = (lax.axis_index("dp") * nf + lax.axis_index("fsdp")) * rows
    own_terms = lax.dynamic_slice_in_dim(terms, at, rows, 1)

    wide = jnp.concatenate([part_in, part_gate, part_rise], 2)
    own_wide = lax.dynamic_index_in_dim(wide, core, 0, keepdims=False)
    got = swap(lax.dynamic_index_in_dim(wide, 1 - core, 0, keepdims=False))
    ends = (0, 3 * feats, 3 * feats + hidden, 3 * feats + 2 * hidden)
    full = [
        both_columns(own_wide[:, a:b], got[:, a:b], groups, core)
        for a, b, groups in zip(ends[:-1], ends[1:], (3 * nx, nx, nx), strict=True)
    ]
    return (
        block_output,
        grad_inputs.astype(BF),
        full[0],
        part_out,
        full[1],
        full[2],
        part_down,
        own_terms[0],
        own_terms[1],
        own_terms[2:].T,
    )


def solution(mesh):
    rows = P(("dp", "fsdp"), None)
    line = P(("dp", "fsdp"))
    return jax.shard_map(
        per_device,
        mesh=mesh,
        in_specs=(rows,) * 6 + (line, line, rows, P("dp", None), rows),
        out_specs=(rows,) * 7 + (line, line, rows),
        check_vma=False,
    )
```

```python
import functools

import jax
import jax.numpy as jnp
from jax import lax
from jax.experimental import pallas as pl
from jax.experimental.pallas import tpu as pltpu
from jax.sharding import Mesh
from jax.sharding import PartitionSpec as P

EPS = 1e-05
AXES = ("x", "core", "z", "y")
BF = jnp.bfloat16
F32 = jnp.float32


class Axis:
    def __init__(self, name):
        self.name, self.size = name, lax.axis_size(name)
        self.here = lax.axis_index(name)
        near = sorted(range(1, self.size), key=lambda by: (min(by, self.size - by), by))
        self.steps = tuple(near)

    def shift(self, value, by=1):
        return lax.ppermute(value, self.name, [(i, (i + by) % self.size) for i in range(self.size)])

    def at(self, by):
        return lax.rem(self.here + by, self.size)


def passed_along(shard, by):
    peers = lax.axis_size(("z", "y"))
    pairs = [(i, i + by) for i in range(peers) if 0 <= i + by < peers]
    return lax.ppermute(shard, ("z", "y"), pairs)


def fence(*values):
    return lax.optimization_barrier(values)


def contract_rows(left, right):
    return lax.dot_general(
        left, right, (((0,), (0,)), ((), ())), preferred_element_type=F32
    )


def contract_cols(left, right):
    return lax.dot_general(
        left, right, (((1,), (1,)), ((), ())), preferred_element_type=F32
    )


def times(left, right):
    return jnp.dot(left, right, preferred_element_type=F32)


def pick(value, at, dim):
    return lax.dynamic_index_in_dim(value, at, dim, keepdims=False)


def ordered(mine, other, here, dim):
    low = jnp.where(here == 0, mine, other)
    high = jnp.where(here == 0, other, mine)
    return jnp.stack([low, high], dim)


def sent(value, axis, dim):
    own = pick(value, axis.here, dim)
    return own, [axis.shift(pick(value, axis.at(by), dim), by) for by in axis.steps]


def summed(own, others):
    total = own.astype(F32)
    for other in others:
        total = total + other.astype(F32)
    return total


def place_body(moves, here_ref, *refs):
    sems = refs[-1]
    copies = []
    for i, (source, target) in enumerate(moves(here_ref, refs[:-1])):
        copy = pltpu.make_async_copy(source, target, sems.at[i])
        copy.start()
        copies.append(copy)
    for copy in copies:
        copy.wait()


def place(moves, count, here, sources, shapes):
    return pl.pallas_call(
        functools.partial(place_body, moves),
        out_shape=[jax.ShapeDtypeStruct(shape, BF) for shape in shapes],
        in_specs=[pl.BlockSpec(memory_space=pltpu.SMEM)]
        + [pl.BlockSpec(memory_space=pl.ANY)] * len(sources),
        out_specs=[pl.BlockSpec(memory_space=pltpu.VMEM)] * len(shapes),
        scratch_shapes=[pltpu.SemaphoreType.DMA((count,))],
        compiler_params=pltpu.CompilerParams(vmem_limit_bytes=48 * 1024 * 1024),
        cost_estimate=pl.CostEstimate(flops=0, bytes_accessed=2**20, transcendentals=0),
    )(here, *sources)


def back(at, by, size):
    return lax.rem(at + size - by, size)


def place_mix(pieces, here, ax, ay, az, columns, width):
    nx, ny, nz = ax.size, ay.size, az.size
    arrays = []
    for piece in pieces:
        if not any(piece[3] is array for array in arrays):
            arrays.append(piece[3])
    rows, half = arrays[0].shape[-2], width // 2
    where = [next(i for i, a in enumerate(arrays) if a is piece[3]) for piece in pieces]

    def moves(at, refs):
        wide, small, narrow = refs[-3:]
        for (dx, dy, backs, _, lead), i in zip(pieces, where, strict=True):
            x, y = back(at[0], dx, nx), back(at[1], dy, ny)
            for n, dz in enumerate(backs):
                z = back(at[2], dz, nz)
                block = refs[i].at[lead + (n,)]
                yield block.at[:, :, pl.ds(0, columns)], wide.at[x, :, z, y]
                yield block.at[:, :, pl.ds(columns, 128)], small.at[x, :, z, y]
                for k in range(2):
                    yield (
                        block.at[k, :, pl.ds(columns + 128, half)],
                        narrow.at[x, z, y, :, pl.ds(k * half, half)],
                    )

    lead = (nx, 2, nz, ny, rows)
    shapes = [lead + (columns,), lead + (128,), (nx, nz, ny, rows, width)]
    wide, small, narrow = place(moves, 4 * nx * ny * nz, here, arrays, shapes)
    return wide.reshape(-1, columns), small.reshape(-1, 128), narrow.reshape(-1, width)


def cost():
    return pl.CostEstimate(flops=0, bytes_accessed=2**16, transcendentals=0)


def params():
    return pltpu.CompilerParams(vmem_limit_bytes=40 * 1024 * 1024)


def whole(array):
    return pl.BlockSpec(
        array.shape, lambda i: (0,) * array.ndim, pipeline_mode=pl.Buffered(1)
    )


def tiles(rows, columns):
    return pl.BlockSpec((rows, columns), lambda i: (i, 0))


def chunks(columns):
    step = 384 if columns % 384 == 0 else 128 if columns % 128 == 0 else columns
    return [(a, step) for a in range(0, columns, step)]


def logistic(v):
    return 0.5 * jnp.tanh(0.5 * v) + 0.5


def forward_body(x_ref, w_ref, ev_ref, s_ref):
    hidden = s_ref.shape[1]
    x = x_ref[...]
    for a, n in chunks(hidden):
        gate = times(x, w_ref[:, a : a + n])
        rise = times(x, w_ref[:, hidden + a : hidden + a + n])
        ev_ref[:, a : a + n] = gate.astype(BF)
        ev_ref[:, hidden + a : hidden + a + n] = rise.astype(BF)
        s_ref[:, a : a + n] = (gate * logistic(gate) * rise).astype(BF)


def ffn_forward(x, w, tile):
    count, both = x.shape[0], w.shape[1]
    return pl.pallas_call(
        forward_body,
        grid=(count // tile,),
        in_specs=[tiles(tile, x.shape[1]), whole(w)],
        out_specs=[tiles(tile, both), tiles(tile, both // 2)],
        out_shape=[
            jax.ShapeDtypeStruct((count, both), BF),
            jax.ShapeDtypeStruct((count, both // 2), BF),
        ],
        compiler_params=params(),
        cost_estimate=cost(),
    )(x, w)


def back_body(half, dy_ref, ev_ref, down_ref, w_ref, dev_ref, keep_ref, send_ref):
    hidden = down_ref.shape[0]
    dy = dy_ref[...]
    for a, n in chunks(hidden):
        back = contract_cols(dy, down_ref[a : a + n, :])
        gate = ev_ref[:, a : a + n].astype(F32)
        rise = ev_ref[:, hidden + a : hidden + a + n].astype(F32)
        sigma = logistic(gate)
        back = back * sigma
        dev_ref[:, a : a + n] = (back * rise * (1.0 + gate * (1.0 - sigma))).astype(BF)
        dev_ref[:, hidden + a : hidden + a + n] = (back * gate).astype(BF)
    split_rows(half, contract_cols(dev_ref[...], w_ref[...]), keep_ref, send_ref)


def split_rows(half, value, keep_ref, send_ref):
    @pl.when(pl.program_id(0) < half)
    def _():
        keep_ref[...] = value

    @pl.when(pl.program_id(0) >= half)
    def _():
        send_ref[...] = value


def split_specs(tile, columns, half):
    return [
        pl.BlockSpec((tile, columns), lambda i: (jnp.minimum(i, half - 1), 0)),
        pl.BlockSpec((tile, columns), lambda i: (jnp.maximum(i - half, 0), 0)),
    ]


def ffn_back(dy, ev, down, w, tile):
    count, width = dy.shape
    both, half = w.shape[1], count // (2 * tile)
    return pl.pallas_call(
        functools.partial(back_body, half),
        grid=(count // tile,),
        in_specs=[tiles(tile, width), tiles(tile, both), whole(down), whole(w)],
        out_specs=[tiles(tile, both)] + split_specs(tile, width, half),
        out_shape=[jax.ShapeDtypeStruct((count, both), BF)]
        + [jax.ShapeDtypeStruct((count // 2, width), F32)] * 2,
        compiler_params=params(),
        cost_estimate=cost(),
    )(dy, ev, down, w)


def fed_body(half, s_ref, down_ref, keep_ref, send_ref):
    split_rows(half, times(s_ref[...], down_ref[...]), keep_ref, send_ref)


def ffn_out(s, down, tile):
    count, width = s.shape[0], down.shape[1]
    half = count // (2 * tile)
    return pl.pallas_call(
        functools.partial(fed_body, half),
        grid=(2 * half,),
        in_specs=[tiles(tile, s.shape[1]), whole(down)],
        out_specs=split_specs(tile, width, half),
        out_shape=[jax.ShapeDtypeStruct((count // 2, width), F32)] * 2,
        compiler_params=params(),
        cost_estimate=cost(),
    )(s, down)


def grad_body(count, *refs):
    total = contract_rows(refs[0][...], refs[count][...])
    for i in range(1, count):
        total = total + contract_rows(refs[i][...], refs[count + i][...])
    for ref in refs[2 * count : -1]:
        total = total + ref[...]
    refs[-1][...] = total.astype(refs[-1].dtype).reshape(refs[-1].shape)


def weight_grad(lefts, rights, tile, out_spec, shape, kind=BF, extra=()):
    count, rows = lefts[0].shape
    left = pl.BlockSpec((count, tile), lambda i: (0, i))
    return pl.pallas_call(
        functools.partial(grad_body, len(lefts)),
        grid=(rows // tile,),
        in_specs=[left] * len(lefts) + [whole(right) for right in rights] + [out_spec] * len(extra),
        out_specs=out_spec,
        out_shape=jax.ShapeDtypeStruct(shape, kind),
        compiler_params=params(),
        cost_estimate=cost(),
    )(*lefts, *rights, *extra)


def gate_up_grad(lefts, rights, nx, nz, rows):
    columns, width = rights[0].shape[1], lefts[0].shape[1]
    tile, lead = nz * 2 * rows, (nx, nz, 2, 2 * rows)
    if tile % 128 == 0:
        spec = pl.BlockSpec((1, nz, 1, 2 * rows, columns), lambda i: (i // 2, 0, i % 2, 0, 0))
        out = weight_grad(lefts, rights, tile, spec, lead + (columns,))
    else:
        out = weight_grad(lefts, rights, 256, tiles(256, columns), (width, columns))
        out = out.reshape(nx, 2, nz, 2 * rows, columns).transpose(0, 2, 1, 3, 4)
    return out.reshape(width, columns)


def per_device(
    block_input,
    in_weight,
    out_weight,
    gate_weight,
    up_weight,
    down_weight,
    norm_gain,
    ffn_gain,
    conv_weight,
    seq_starts,
    cotangent,
):
    ax, ac, az, ay = (Axis(name) for name in AXES)
    nx, nz = ax.size, az.size
    core, y_here = ac.here, ay.here
    here = jnp.stack([ax.here, ay.here, az.here]).astype(jnp.int32)
    tokens, width = block_input.shape
    rows = in_weight.shape[0]
    hidden = gate_weight.shape[1] // 4
    feats = width // 2
    wide_cols = 3 * feats
    lower = nz // 2
    z_back = (0,) + az.steps
    first_back, second_back = z_back[:lower], z_back[lower:]

    small = jnp.concatenate(
        [norm_gain[:, None], ffn_gain[:, None], conv_weight, jnp.zeros((rows, 123), F32)], 1
    ).astype(BF)
    in_sets = in_weight.astype(BF).reshape(rows, 3 * nx, 2, feats // nx)

    def in_part(which):
        return jnp.concatenate([pick(in_sets, which, 2).reshape(rows, wide_cols), small], 1)

    in_mine, in_got = in_part(core), ac.shift(in_part(1 - core))
    starts_core = ac.shift(seq_starts)

    def split_hidden(weight):
        cut = weight.astype(BF).reshape(rows, nx, 2, nz, 2, hidden // (nx * nz))
        return jnp.transpose(cut, (2, 4, 0, 1, 3, 5)).reshape(2, 2, rows, hidden)

    in_mine, in_got, gate_weight, up_weight = fence(in_mine, in_got, gate_weight, up_weight)
    out_low = out_weight.astype(BF).reshape(rows, 2, feats).transpose(1, 0, 2)
    mix = jnp.concatenate([ordered(in_mine, in_got, core, 0), out_low], 2)
    mix_z = {by: az.shift(mix, by) for by in first_back[1:]}
    gate_up = jnp.concatenate([split_hidden(gate_weight), split_hidden(up_weight)], 3)
    pair_mine = pick(gate_up, core, 0)
    pair_got = ac.shift(pick(gate_up, 1 - core, 0))

    pair_mine, pair_got, mix, mix_z, cotangent, down_low = fence(
        pair_mine, pair_got, mix, mix_z, cotangent, down_weight.astype(BF)
    )
    first = jnp.stack([mix] + [mix_z[by] for by in first_back[1:]])
    first_x = [ax.shift(first, by) for by in ax.steps]
    second = [az.shift(mix, by) for by in second_back]
    pair = ordered(pair_mine, pair_got, core, 0)
    quad_mine, quad_got = pick(pair, y_here, 1), ay.shift(pick(pair, 1 - y_here, 1))
    dy_low, dy_high = cotangent[: tokens // 2], cotangent[tokens // 2 :]
    quad = ordered(quad_mine, quad_got, y_here, 1)
    second, first, first_x, quad, down_low = fence(second, first, first_x, quad, down_low)
    gathered = lax.all_gather(quad.reshape(4 * rows, 2 * hidden), ("x", "z"), axis=0, tiled=True)
    second = jnp.stack(second)
    second_y = ay.shift(second)

    second_y, second, first, first_x, block_input, cotangent, down_low = fence(
        second_y, second, first, first_x, block_input, cotangent, down_low
    )
    ffn_down = lax.all_gather(down_low, ("x", "z"), axis=0, tiled=True)
    second_pair = jnp.stack([second, second_y])
    second_x = [ax.shift(second_pair, by) for by in ax.steps]
    first_y = ay.shift(jnp.stack([first] + first_x))
    x_core = ac.shift(block_input)
    dy_core = ac.shift(cotangent)
    inputs = jnp.concatenate([block_input, x_core], 0).astype(F32)
    scale_mix = lax.rsqrt(jnp.mean(inputs * inputs, axis=1, keepdims=True) + EPS)

    first_y, second_x, second_pair, first, first_x, scale_mix, dy_core, dy_low = fence(
        first_y, second_x, second_pair, first, first_x, scale_mix, dy_core, dy_low
    )
    dy_low_y = ay.shift(dy_low)
    pieces = [(0, 0, first_back, first, ())]
    pieces += [(0, dy, second_back, second_pair, (dy,)) for dy in range(2)]
    pieces += [(dx, 0, first_back, a, ()) for dx, a in zip(ax.steps, first_x, strict=True)]
    pieces += [(dx, 1, first_back, first_y, (n,)) for n, dx in enumerate((0,) + ax.steps)]
    for dx, a in zip(ax.steps, second_x, strict=True):
        pieces += [(dx, dy, second_back, a, (dy,)) for dy in range(2)]
    mix_in, tiny, mix_out = place_mix(pieces, here, ax, ay, az, wide_cols, width)
    tiny = tiny[:, :8].astype(F32)
    gain_mix, gain_ffn = tiny[:, 0], tiny[:, 1]
    taps = pick(tiny[:, 2:5].reshape(nx, 2, feats // nx, 3), core, 1).reshape(feats, 3)

    own_inputs = block_input.astype(F32)
    starts = jnp.concatenate([seq_starts, starts_core], 0)
    normed_mix = (inputs * scale_mix * gain_mix[None, :]).astype(BF)
    projected = times(normed_mix, mix_in)
    projected, dy_low_y = fence(projected, dy_low_y)
    dy_low_far = ac.shift(dy_low_y)

    b_branch = projected[:, :feats]
    c_branch = projected[:, feats : 2 * feats]
    x_branch = projected[:, 2 * feats :]
    product = (b_branch * x_branch).reshape(2, tokens, feats)
    earlier = passed_along(product[:, tokens - 2 :], 1)
    position = lax.axis_index(("z", "y")) * tokens + jnp.arange(tokens + 2, dtype=jnp.int32)

    def offsets(at):
        reached = starts[:, None, :] <= at[None, :, None]
        return at[None, :] - jnp.max(jnp.where(reached, starts[:, None, :], 0), axis=2)

    own_offset = offsets(position[:tokens])
    next_offset = offsets(position)
    padded = jnp.concatenate([earlier, product], 1)
    mixed = jnp.zeros((2, tokens, feats), F32)
    for lag in range(3):
        valid = (own_offset >= lag).astype(F32)[:, :, None]
        mixed = mixed + valid * taps[:, 2 - lag] * padded[:, 2 - lag : 2 - lag + tokens]
    mixed = mixed.reshape(2 * tokens, feats)
    gated = (c_branch * mixed).astype(BF)
    mixer_keep = times(gated[:tokens], mix_out)
    mixer_got = ac.shift(times(gated[tokens:], mix_out))

    mixer_got, mixer_keep = fence(mixer_got, mixer_keep)
    h = own_inputs + (mixer_keep + mixer_got)
    scale_ffn = lax.rsqrt(jnp.mean(h * h, axis=1, keepdims=True) + EPS)
    normed_own = (h * scale_ffn * gain_ffn[None, :]).astype(BF)
    normed_core = ac.shift(normed_own)
    gathered = gathered.reshape(nx, nz, 2, 2 * rows, 2 * hidden).transpose(0, 2, 1, 3, 4)
    gate_up = gathered.reshape(width, 2 * hidden)

    normed_core, normed_own, h, scale_ffn, gate_up = fence(
        normed_core, normed_own, h, scale_ffn, gate_up
    )
    normed_y = ay.shift(normed_own)
    near = jnp.concatenate([normed_own, normed_core], 0)
    dy_near = jnp.concatenate([cotangent, dy_core], 0)
    near_ev, near_s = ffn_forward(near, gate_up, tokens // 2)
    tile = 384 if hidden % 384 == 0 else hidden
    spec = pl.BlockSpec((tile, width), lambda i: (i, 0))
    near_down = weight_grad([near_s], [dy_near], tile, spec, (hidden, width), F32)

    normed_y, near_ev, near_s, dy_high, near_down = fence(
        normed_y, near_ev, near_s, dy_high, near_down
    )
    dy_high_y = ay.shift(dy_high)
    far = jnp.concatenate([normed_y, ac.shift(normed_y)], 0)
    far_ev, far_s = ffn_forward(far, gate_up, tokens // 2)

    far_s, far_ev, ffn_down, dy_high_y = fence(far_s, far_ev, ffn_down, dy_high_y)
    dy_far = jnp.concatenate([dy_low_y, dy_high_y, dy_low_far, ac.shift(dy_high_y)], 0)
    grad_down = weight_grad([far_s], [dy_far], tile, spec, (hidden, width), BF, [near_down])
    far_ev, far_s, grad_down = fence(far_ev, far_s, grad_down)
    part_down = lax.psum_scatter(grad_down, ("x", "z"), scatter_dimension=0, tiled=True)

    far_dev, far_keep, far_send = ffn_back(dy_far, far_ev, ffn_down, gate_up, tokens // 2)
    far_keep, far_send, far_s, near_ev, dy_near = fence(
        far_keep, far_send, far_s, near_ev, dy_near
    )
    far_got = ac.shift(far_send)
    far_got, far_keep, near_ev, far_s = fence(far_got, far_keep, near_ev, far_s)

    normed_y_got = ay.shift((far_keep + far_got).astype(BF))
    near_dev, near_keep, near_send = ffn_back(dy_near, near_ev, ffn_down, gate_up, tokens // 2)
    grad_gate_up = gate_up_grad([near, far], [near_dev, far_dev], nx, nz, rows)
    normed_y_got, near_keep, near_send, grad_gate_up = fence(
        normed_y_got, near_keep, near_send, grad_gate_up
    )

    near_got = ac.shift(near_send)
    quad = lax.psum_scatter(grad_gate_up, ("x", "z"), scatter_dimension=0, tiled=True)
    near_got, near_keep, far_s = fence(near_got, near_keep, far_s)
    far_fed, far_fed_send = ffn_out(far_s, ffn_down, tokens // 2)
    grad_normed = near_keep + near_got + normed_y_got.astype(F32)
    grad_gain_ffn = jnp.sum(grad_normed * h * scale_ffn, axis=0)
    weighted = grad_normed * gain_ffn[None, :]
    grad_hidden = (
        cotangent.astype(F32)
        + scale_ffn * weighted
        - h * scale_ffn**3 * jnp.mean(weighted * h, axis=1, keepdims=True)
    )
    hidden_own = grad_hidden.astype(BF)
    hidden_got = ac.shift(hidden_own)

    hidden_got, hidden_own, grad_hidden, far_fed, far_fed_send = fence(
        hidden_got, hidden_own, grad_hidden, far_fed, far_fed_send
    )
    far_fed_got = ac.shift(far_fed_send)
    hidden_low = jnp.concatenate([hidden_own, hidden_got], 0)
    grad_gated = contract_cols(hidden_low, mix_out)
    grad_c = grad_gated * mixed
    grad_mixed = (grad_gated * c_branch).reshape(2, tokens, feats)
    later = passed_along(grad_mixed[:, :2], -1)
    back_out = contract_rows(gated, hidden_low).astype(BF)

    trailing = jnp.concatenate([grad_mixed, later], 1)
    grad_product = jnp.zeros((2, tokens, feats), F32)
    tap_grads = []
    for lag in range(3):
        ahead = (next_offset[:, lag : lag + tokens] >= lag).astype(F32)[:, :, None]
        grad_product = grad_product + ahead * taps[:, 2 - lag] * trailing[:, lag : lag + tokens]
    for column in range(3):
        valid = (own_offset >= 2 - column).astype(F32)[:, :, None]
        tap_grads.append(
            jnp.sum(valid * grad_mixed * padded[:, column : column + tokens], axis=(0, 1))
        )
    grad_product = grad_product.reshape(2 * tokens, feats)
    grad_projected = jnp.concatenate(
        [grad_product * x_branch, grad_c, grad_product * b_branch], 1
    ).astype(BF)

    back_in = contract_rows(normed_mix, grad_projected).astype(BF)
    back_mix = jnp.concatenate(
        [
            back_in.reshape(nx, 2, nz, 2, rows, wide_cols),
            back_out.reshape(nx, nz, 2, rows, 2, feats).transpose(0, 4, 1, 2, 3, 5),
        ],
        5,
    )
    back_mix, grad_projected, near_s, far_fed_got = fence(
        back_mix, grad_projected, near_s, far_fed_got
    )
    first_own, first_got = sent(back_mix[:, :, :lower], ay, 3)
    second_own, second_got = sent(back_mix[:, :, lower:], ax, 0)
    mix_got = ac.shift(contract_cols(grad_projected[tokens:], mix_in))
    mix_keep = contract_cols(grad_projected[:tokens], mix_in)
    near_fed, near_fed_send = ffn_out(near_s, ffn_down, tokens // 2)
    near_fed_got = ac.shift(near_fed_send)
    grad_normed_mix = mix_keep + mix_got
    own_scale = scale_mix[:tokens]
    grad_gain_mix = jnp.sum(grad_normed_mix * own_inputs * own_scale, axis=0)
    weighted_mix = grad_normed_mix * gain_mix[None, :]
    grad_inputs = (
        grad_hidden
        + own_scale * weighted_mix
        - own_inputs * own_scale**3 * jnp.mean(weighted_mix * own_inputs, axis=1, keepdims=True)
    ).astype(BF)
    tap_rows = jnp.stack(tap_grads).reshape(3, nx, 1, feats // nx)
    on_core = (jnp.arange(2) == core).astype(F32)[None, None, :, None]
    tap_rows = (tap_rows * on_core).reshape(3, width)
    terms = jnp.concatenate([grad_gain_mix[None], grad_gain_ffn[None], tap_rows], 0)
    terms = terms + ac.shift(terms)

    first_got, first_own, second_got, second_own, grad_inputs, near_fed_got, terms = fence(
        first_got, first_own, second_got, second_own, grad_inputs, near_fed_got, terms
    )
    first_own, first_got = sent(summed(first_own, first_got).astype(BF), ax, 0)
    second_own, second_got = sent(summed(second_own, second_got).astype(BF), ay, 2)
    terms = summed(terms, [az.shift(terms, by) for by in az.steps])

    first_got, first_own, second_got, second_own, terms = fence(
        first_got, first_own, second_got, second_own, terms
    )
    own_z = jnp.concatenate(
        [summed(first_own, first_got).astype(BF), summed(second_own, second_got).astype(BF)], 1
    )
    mix_own, mix_parts = sent(own_z, az, 1)
    terms = summed(terms, [ax.shift(terms, by) for by in ax.steps])
    terms = terms + ay.shift(terms)
    fed_y = ay.shift((far_fed + far_fed_got).astype(BF))
    mix_parts, mix_own, terms, fed_y, quad = fence(mix_parts, mix_own, terms, fed_y, quad)

    quad = quad.reshape(2, 2, rows, 2 * hidden)
    quad_mine, quad_got = sent(quad, ay, 1)
    block_output = (h + (near_fed + near_fed_got + fed_y.astype(F32))).astype(BF)
    mix_sum = summed(mix_own, mix_parts)
    part_out = mix_sum[..., wide_cols:].transpose(1, 0, 2).reshape(rows, width)
    in_mine, in_got = sent(mix_sum[..., :wide_cols], ac, 0)
    cut = (rows, 3 * nx, feats // nx)
    part_in = ordered(in_mine.reshape(cut), in_got[0].reshape(cut), core, 2)
    pair = ordered(quad_mine, quad_got[0], y_here, 1)
    pair_mine, pair_got = sent(pair, ac, 0)
    quads = ordered(pair_mine, pair_got[0], core, 0).astype(F32)

    def join_hidden(sets):
        cut = sets.reshape(2, 2, rows, nx, nz, hidden // (nx * nz))
        return jnp.transpose(cut, (2, 3, 0, 4, 1, 5)).reshape(rows, 4 * hidden)

    part_gate, part_rise = join_hidden(quads[..., :hidden]), join_hidden(quads[..., hidden:])
    own_terms = lax.dynamic_slice_in_dim(terms, lax.axis_index(AXES) * rows, rows, 1)
    return (
        block_output,
        grad_inputs,
        part_in.reshape(rows, 3 * width),
        part_out,
        part_gate,
        part_rise,
        part_down.astype(F32),
        own_terms[0],
        own_terms[1],
        own_terms[2:].T,
    )


def solution(mesh):
    nd, nf = mesh.shape["dp"], mesh.shape["fsdp"]
    rows, line = P(AXES, None), P(AXES)
    return jax.shard_map(
        per_device,
        mesh=Mesh(mesh.devices.reshape(nd // 2, 2, nf // 2, 2), AXES),
        in_specs=(rows,) * 6 + (line, line, rows, P(("x", "core"), None), rows),
        out_specs=(rows,) * 7 + (line, line, rows),
        check_vma=False,
    )
```

```python
import functools
import itertools
import math

import jax
import jax.numpy as jnp
from jax import lax
from jax.experimental import pallas as pl
from jax.experimental.pallas import tpu as pltpu
from jax.sharding import Mesh
from jax.sharding import PartitionSpec as P

EPS = 1e-05
AXES = ("far", "x", "core", "z", "y")
SPREAD = ("far", "z", "y")
BF = jnp.bfloat16
F32 = jnp.float32


class Axis:
    def __init__(self, name):
        self.name, self.size = name, lax.axis_size(name)
        self.here = lax.axis_index(name)
        near = sorted(range(1, self.size), key=lambda by: (min(by, self.size - by), by))
        self.steps = tuple(near)

    def shift(self, value, by=1):
        return lax.ppermute(value, self.name, [(i, (i + by) % self.size) for i in range(self.size)])

    def at(self, by):
        return lax.rem(self.here + by, self.size)


def passed_along(shard, by):
    peers = lax.axis_size(("z", "y"))
    pairs = [(i, i + by) for i in range(peers) if 0 <= i + by < peers]
    return lax.ppermute(shard, ("z", "y"), pairs)


def fence(*values):
    return lax.optimization_barrier(values)


def contract_rows(left, right):
    return lax.dot_general(
        left, right, (((0,), (0,)), ((), ())), preferred_element_type=F32
    )


def contract_cols(left, right):
    return lax.dot_general(
        left, right, (((1,), (1,)), ((), ())), preferred_element_type=F32
    )


def times(left, right):
    return jnp.dot(left, right, preferred_element_type=F32)


def pick(value, at, dim):
    return lax.dynamic_index_in_dim(value, at, dim, keepdims=False)


def ordered(mine, other, here, dim):
    low = jnp.where(here == 0, mine, other)
    high = jnp.where(here == 0, other, mine)
    return jnp.stack([low, high], dim)


def cut(value, axis, dim):
    return pick(value, axis.here, dim), [pick(value, axis.at(by), dim) for by in axis.steps]


def shifted(parts, axis):
    return [axis.shift(part, by) for part, by in zip(parts, axis.steps, strict=True)]


def summed(own, others):
    total = own.astype(F32)
    for other in others:
        total = total + other.astype(F32)
    return total


def place_body(moves, here_ref, *refs):
    sems = refs[-1]
    copies = []
    for i, (source, target) in enumerate(moves(here_ref, refs[:-1])):
        copy = pltpu.make_async_copy(source, target, sems.at[i])
        copy.start()
        copies.append(copy)
    for copy in copies:
        copy.wait()


def out_array(shape, kind):
    return pltpu.HBM(shape, kind) if math.prod(shape) >= 2**18 else jax.ShapeDtypeStruct(shape, kind)


def pinned(*arrays):
    return [
        pltpu.with_memory_space_constraint(a, pltpu.HBM) if a.size >= 2**18 else a for a in arrays
    ]


def place(moves, count, here, sources, shapes):
    return pl.pallas_call(
        functools.partial(place_body, moves),
        out_shape=[out_array(shape, BF) for shape in shapes],
        in_specs=[pl.BlockSpec(memory_space=pltpu.SMEM)]
        + [pl.BlockSpec(memory_space=pl.ANY)] * len(sources),
        out_specs=[pl.BlockSpec(memory_space=pltpu.VMEM)] * len(shapes),
        scratch_shapes=[pltpu.SemaphoreType.DMA((count,))],
        compiler_params=params(20),
        cost_estimate=pl.CostEstimate(flops=0, bytes_accessed=2**20, transcendentals=0),
    )(here, *pinned(*sources))


def back(at, by, size):
    return lax.rem(at + size - by, size)


def place_mix(pieces, here, ax, ay, az, columns, width):
    nx, ny, nz = ax.size, ay.size, az.size
    rows, half = pieces[0][3].shape[-2], width // 2

    def moves(at, refs):
        wide, small, narrow = refs[-3:]
        for (dx, dy, backs, _), source in zip(pieces, refs[:-3], strict=True):
            x, y = back(at[0], dx, nx), back(at[1], dy, ny)
            for n, dz in enumerate(backs):
                z = back(at[2], dz, nz)
                block = source.at[n]
                yield block.at[:, :, pl.ds(0, columns)], wide.at[x, :, z, y]
                yield block.at[:, :, pl.ds(columns, 128)], small.at[x, :, z, y]
                for k in range(2):
                    yield (
                        block.at[k, :, pl.ds(columns + 128, half)],
                        narrow.at[x, z, y, :, pl.ds(k * half, half)],
                    )

    lead = (nx, 2, nz, ny, rows)
    shapes = [lead + (columns,), lead + (128,), (nx, nz, ny, rows, width)]
    arrays = [piece[3] for piece in pieces]
    wide, small, narrow = place(moves, 4 * nx * ny * nz, here, arrays, shapes)
    return wide.reshape(-1, columns), small.reshape(-1, 128), narrow.reshape(-1, width)


def cost():
    return pl.CostEstimate(flops=0, bytes_accessed=2**16, transcendentals=0)


def params(mib):
    return pltpu.CompilerParams(vmem_limit_bytes=mib * 1024 * 1024)


def whole(array):
    return pl.BlockSpec(
        array.shape, lambda i: (0,) * array.ndim, pipeline_mode=pl.Buffered(1)
    )


def tiles(rows, columns):
    return pl.BlockSpec((rows, columns), lambda i: (i, 0))


def chunks(columns):
    step = 384 if columns % 384 == 0 else 128 if columns % 128 == 0 else columns
    return [(a, step) for a in range(0, columns, step)]


def logistic(v):
    return 0.5 * jnp.tanh(0.5 * v) + 0.5


def piece_specs(pieces, tile):
    specs = []
    for p, piece in enumerate(pieces):
        first, last = p * piece.shape[0] // tile, (p + 1) * piece.shape[0] // tile - 1

        def at(i, first=first, last=last):
            return jnp.clip(i - first, 0, last - first), 0

        specs.append(pl.BlockSpec((tile, piece.shape[1]), at))
    return specs


def piece_tile(refs):
    steps = pl.num_programs(0) // len(refs)
    value = refs[0][...]
    for p, ref in enumerate(refs[1:], 1):
        value = jnp.where(pl.program_id(0) >= p * steps, ref[...], value)
    return value


def forward_body(count, *refs):
    w_ref, ev_ref, s_ref = refs[count:]
    hidden = s_ref.shape[1]
    x = piece_tile(refs[:count])
    for a, n in chunks(hidden):
        gate = times(x, w_ref[:, a : a + n])
        rise = times(x, w_ref[:, hidden + a : hidden + a + n])
        ev_ref[:, a : a + n] = gate.astype(BF)
        ev_ref[:, hidden + a : hidden + a + n] = rise.astype(BF)
        s_ref[:, a : a + n] = (gate * logistic(gate) * rise).astype(BF)


def ffn_forward(pieces, w, tile):
    count, both = sum(piece.shape[0] for piece in pieces), w.shape[1]
    return pl.pallas_call(
        functools.partial(forward_body, len(pieces)),
        grid=(count // tile,),
        in_specs=piece_specs(pieces, tile) + [whole(w)],
        out_specs=[tiles(tile, both), tiles(tile, both // 2)],
        out_shape=[out_array((count, both), BF), out_array((count, both // 2), BF)],
        compiler_params=params(24),
        cost_estimate=cost(),
    )(*pinned(*pieces, w))


def back_body(count, half, *refs):
    ev_ref, down_ref, w_ref, dev_ref, keep_ref, *sends = refs[count:]
    hidden = down_ref.shape[0]
    dy = piece_tile(refs[:count])
    for a, n in chunks(hidden):
        back = contract_cols(dy, down_ref[a : a + n, :])
        gate = ev_ref[:, a : a + n].astype(F32)
        rise = ev_ref[:, hidden + a : hidden + a + n].astype(F32)
        sigma = logistic(gate)
        back = back * sigma
        dev_ref[:, a : a + n] = (back * rise * (1.0 + gate * (1.0 - sigma))).astype(BF)
        dev_ref[:, hidden + a : hidden + a + n] = (back * gate).astype(BF)
    split_pieces(half, contract_cols(dev_ref[...], w_ref[...]), keep_ref, sends)


def split_rows(half, value, keep_ref, send_ref):
    @pl.when(pl.program_id(0) < half)
    def _():
        keep_ref[...] = value

    @pl.when(pl.program_id(0) >= half)
    def _():
        send_ref[...] = value


def split_specs(tile, columns, half):
    return [
        pl.BlockSpec((tile, columns), lambda i: (jnp.minimum(i, half - 1), 0)),
        pl.BlockSpec((tile, columns), lambda i: (jnp.maximum(i - half, 0), 0)),
    ]


def split_pieces(half, value, keep_ref, sends):
    cuts = len(sends) // half
    size = value.shape[0] // cuts

    @pl.when(pl.program_id(0) < half)
    def _():
        keep_ref[...] = value

    for n, ref in enumerate(sends):

        @pl.when(pl.program_id(0) == half + n // cuts)
        def _(n=n, ref=ref):
            at = n % cuts * size
            ref[...] = value[at : at + size].astype(ref.dtype)


def piece_outputs(count, width, tile, cuts):
    half, size = count // (2 * tile), tile // cuts
    specs = split_specs(tile, width, half)[:1]
    specs += [pl.BlockSpec((size, width), lambda i: (0, 0))] * (half * cuts)
    shapes = [out_array((count // 2, width), F32)]
    return specs, shapes + [out_array((size, width), BF)] * (half * cuts)


def ffn_back(pieces, ev, down, w, tile):
    count, both = ev.shape
    width, half = down.shape[1], count // (2 * tile)
    specs, shapes = piece_outputs(count, width, tile, 2)
    out = pl.pallas_call(
        functools.partial(back_body, len(pieces), half),
        grid=(2 * half,),
        in_specs=piece_specs(pieces, tile) + [tiles(tile, both), whole(down), whole(w)],
        out_specs=[tiles(tile, both)] + specs,
        out_shape=[out_array((count, both), BF)] + shapes,
        compiler_params=params(32),
        cost_estimate=cost(),
    )(*pinned(*pieces, ev, down, w))
    return out[0], out[1], out[2:]


def rows_body(function, half, left_ref, weight_ref, keep_ref, *sends):
    split_pieces(half, function(left_ref[...], weight_ref[...]), keep_ref, sends)


def row_halves(function, left, weight, width, tile):
    count = left.shape[0]
    half = count // (2 * tile)
    specs, shapes = piece_outputs(count, width, tile, 2)
    out = pl.pallas_call(
        functools.partial(rows_body, function, half),
        grid=(2 * half,),
        in_specs=[tiles(tile, left.shape[1]), whole(weight)],
        out_specs=specs,
        out_shape=shapes,
        compiler_params=params(20),
        cost_estimate=cost(),
    )(*pinned(left, weight))
    return out[0], out[1:]


def input_grad_body(half, dp_ref, win_ref, x_ref, keep_ref, *refs):
    sends, gain_ref = refs[:-1], refs[-1]
    value = contract_cols(dp_ref[...], win_ref[...])
    split_pieces(half, value, keep_ref, sends)
    x = x_ref[...].astype(F32)
    scale = lax.rsqrt(jnp.mean(x * x, axis=1, keepdims=True) + EPS)

    @pl.when(pl.program_id(0) == 0)
    def _():
        gain_ref[...] = jnp.zeros_like(gain_ref)

    gain_ref[...] += jnp.sum(value * (x * scale), axis=0, keepdims=True)


def input_grad(dp, win, x, tile):
    count, width = x.shape
    half = count // (2 * tile)
    specs, shapes = piece_outputs(count, width, tile, 2)
    out = pl.pallas_call(
        functools.partial(input_grad_body, half),
        grid=(2 * half,),
        in_specs=[tiles(tile, dp.shape[1]), whole(win), tiles(tile, width)],
        out_specs=specs + [pl.BlockSpec((1, width), lambda i: (0, 0))],
        out_shape=shapes + [jax.ShapeDtypeStruct((1, width), F32)],
        compiler_params=params(24),
        cost_estimate=cost(),
    )(*pinned(dp, win, x))
    return out[0], out[1:-1], out[-1][0]


def grad_body(lefts, rights, *refs):
    rest = refs[len(lefts) + len(rights) :]
    total = None
    for i, (first, end) in enumerate(lefts):
        for j, (start, stop) in enumerate(rights):
            low, high = max(first, start), min(end, stop)
            if low < high:
                left = refs[i][low - first : high - first, :]
                right = refs[len(lefts) + j][low - start : high - start, :]
                term = contract_rows(left, right)
                total = term if total is None else total + term
    for ref in rest[:-1]:
        total = total + ref[...]
    rest[-1][...] = total.astype(rest[-1].dtype).reshape(rest[-1].shape)


def token_spans(pieces):
    ends = list(itertools.accumulate(piece.shape[0] for piece in pieces))
    return list(zip([0] + ends[:-1], ends, strict=True))


def weight_grad(lefts, rights, tile, out_spec, shape, kind=BF, extra=()):
    rows = lefts[0].shape[1]
    return pl.pallas_call(
        functools.partial(grad_body, token_spans(lefts), token_spans(rights)),
        grid=(rows // tile,),
        in_specs=[pl.BlockSpec((left.shape[0], tile), lambda i: (0, i)) for left in lefts]
        + [whole(right) for right in rights]
        + [out_spec] * len(extra),
        out_specs=out_spec,
        out_shape=out_array(shape, kind),
        compiler_params=params(34),
        cost_estimate=cost(),
    )(*pinned(*lefts, *rights, *extra))


def gate_up_grad(lefts, rights, far, nz, rows):
    columns, width = rights[0].shape[1], lefts[0].shape[1]
    tile = 2 * nz * rows
    if tile % 128 == 0 and rows % 16 == 0:
        block = (1, 2 * nz, 1, rows, columns)
        spec = pl.BlockSpec(block, lambda i: (i // 4, 0, i % 4, 0, 0))
        out = weight_grad(lefts, rights, tile, spec, (far, 2 * nz, 4, rows, columns))
    else:
        out = weight_grad(lefts, rights, 256, tiles(256, columns), (width, columns))
        out = out.reshape(far, 4, 2 * nz, rows, columns).transpose(0, 2, 1, 3, 4)
    return out.reshape(width, columns)


def mix_grad_body(lower, here_ref, a_ref, dp_ref, g_ref, dh_ref, dh2_ref, *refs):
    group, wide, columns = dh_ref.shape[0], dp_ref.shape[1], refs[0].shape[-1]
    out = contract_rows(g_ref[:group, :], dh_ref[...])
    out = out + contract_rows(g_ref[group:, :], dh2_ref[...])
    parts = (
        (contract_rows(a_ref[...], dp_ref[...]), slice(0, wide)),
        (out, slice(wide, columns)),
    )
    own_y = here_ref[1] == 0
    for value, where in parts:
        value = value.astype(BF).reshape(-1, 2, refs[0].shape[2], value.shape[1])
        low, high = value[:, 0], value[:, 1]
        own, other = jnp.where(own_y, low, high), jnp.where(own_y, high, low)
        blocks = (own[:lower], other[:lower], own[lower:], other[lower:])
        for dx in range(2):

            @pl.when(lax.rem(pl.program_id(1) + here_ref[0], 2) == dx)
            def _(blocks=blocks, targets=refs[4 * dx : 4 * dx + 4], where=where):
                for block, target in zip(blocks, targets, strict=True):
                    target[0, :, :, where] = block


def mix_grad(normed, grad_projected, gated, hidden_low, here, nz, rows, lower):
    count, wide = grad_projected.shape
    half = hidden_low[0].shape[1] // 2
    columns, tile = wide + half, 2 * nz * rows
    shapes = [(2, n, rows, columns) for n in (lower, lower, nz - lower, nz - lower)] * 2
    out = pl.pallas_call(
        functools.partial(mix_grad_body, lower),
        grid=(2, 2),
        in_specs=[
            pl.BlockSpec(memory_space=pltpu.SMEM),
            pl.BlockSpec((count, tile), lambda k, x: (0, 2 * x + k)),
            pl.BlockSpec((count, wide), lambda k, x: (0, 0), pipeline_mode=pl.Buffered(1)),
            pl.BlockSpec((count, tile), lambda k, x: (0, x)),
            pl.BlockSpec((count // 2, half), lambda k, x: (0, k)),
            pl.BlockSpec((count // 2, half), lambda k, x: (0, k)),
        ],
        out_specs=[pl.BlockSpec((1,) + shape[1:], lambda k, x: (k, 0, 0, 0)) for shape in shapes],
        out_shape=[out_array(shape, BF) for shape in shapes],
        compiler_params=params(24),
        cost_estimate=cost(),
    )(here, *pinned(normed, grad_projected, gated, *hidden_low))
    return [out[:4], out[4:]]


def mixer_body(
    per_group, x_ref, gain_ref, win_ref, halo_ref, masks_ref, taps_ref, wout_ref, *refs
):
    normed_ref, projected_ref, mixed_ref, gated_ref, keep_ref, send_ref, rows, carry = refs
    count, feats = mixed_ref.shape
    x = x_ref[...].astype(F32)
    scale = lax.rsqrt(jnp.mean(x * x, axis=1, keepdims=True) + EPS)
    normed = (x * scale * gain_ref[...]).astype(BF)
    normed_ref[...] = normed
    projected = times(normed, win_ref[...])
    projected_ref[...] = projected
    product = projected[:, :feats] * projected[:, 2 * feats :]
    opens = lax.rem(pl.program_id(0), per_group) == 0
    rows[6:8, :] = jnp.where(opens, halo_ref[0], carry[...])
    rows[8 : 8 + count, :] = product
    mixed = taps_ref[2:3, :] * product
    mixed = mixed + masks_ref[:, 0:1] * (taps_ref[1:2, :] * rows[7 : 7 + count, :])
    mixed = mixed + masks_ref[:, 1:2] * (taps_ref[0:1, :] * rows[6 : 6 + count, :])
    carry[...] = product[count - 2 :]
    mixed_ref[...] = mixed
    gated = (projected[:, feats : 2 * feats] * mixed).astype(BF)
    gated_ref[...] = gated
    half = pl.num_programs(0) // 2
    split_rows(half, times(gated, wout_ref[...]), keep_ref, send_ref)


def mixer_forward(x, gain, win, halo, masks, taps, wout, tile):
    count, width = x.shape
    wide, feats = win.shape[1], wout.shape[0]
    per_group = count // (2 * tile)
    row = pl.BlockSpec((1, width), lambda i: (0, 0))
    return pl.pallas_call(
        functools.partial(mixer_body, per_group),
        grid=(2 * per_group,),
        in_specs=[
            tiles(tile, width),
            row,
            whole(win),
            pl.BlockSpec((1, 2, feats), lambda i: (i // per_group, 0, 0)),
            tiles(tile, masks.shape[1]),
            whole(taps),
            whole(wout),
        ],
        out_specs=[tiles(tile, width), tiles(tile, wide), tiles(tile, feats), tiles(tile, feats)]
        + split_specs(tile, width, per_group),
        out_shape=[
            out_array((count, width), BF),
            out_array((count, wide), F32),
            out_array((count, feats), F32),
            out_array((count, feats), BF),
        ]
        + [out_array((count // 2, width), F32)] * 2,
        scratch_shapes=[pltpu.VMEM((tile + 8, feats), F32), pltpu.VMEM((2, feats), F32)],
        compiler_params=params(28),
        cost_estimate=cost(),
    )(*pinned(x, gain[None], win, halo, masks, taps, wout))


def mixer_back_body(
    per_group, dh_ref, dh2_ref, wout_ref, projected_ref, mixed_ref, halo_ref, masks_ref, *refs
):
    taps_ref, *refs = refs
    out_ref, grad_ref, rows, carry = refs
    count, feats = mixed_ref.shape
    projected = projected_ref[...]
    dh = jnp.where(pl.program_id(0) < per_group, dh_ref[...], dh2_ref[...])
    back = contract_cols(dh, wout_ref[...])
    grad_c = back * mixed_ref[...]
    grad_mixed = back * projected[:, feats : 2 * feats]
    closes = lax.rem(pl.program_id(0), per_group) == 0
    rows[0:count, :] = grad_mixed
    rows[count : count + 2, :] = jnp.where(closes, halo_ref[0], carry[...])
    carry[...] = grad_mixed[:2]
    ahead = (
        grad_mixed,
        masks_ref[:, 2:3] * rows[1 : 1 + count, :],
        masks_ref[:, 3:4] * rows[2 : 2 + count, :],
    )
    grad_product = sum(taps_ref[2 - lag : 3 - lag, :] * ahead[lag] for lag in range(3))
    b_branch, x_branch = projected[:, :feats], projected[:, 2 * feats :]
    out_ref[:, :feats] = (grad_product * x_branch).astype(BF)
    out_ref[:, feats : 2 * feats] = grad_c.astype(BF)
    out_ref[:, 2 * feats :] = (grad_product * b_branch).astype(BF)

    @pl.when(pl.program_id(0) == 0)
    def _():
        grad_ref[...] = jnp.zeros_like(grad_ref)

    product = b_branch * x_branch
    for lag in range(3):
        grad_ref[2 - lag : 3 - lag, :] += jnp.sum(product * ahead[lag], axis=0, keepdims=True)


def mixer_back(dh, wout, projected, mixed, halo, masks, taps, tile):
    count, wide = projected.shape
    width, feats = dh[0].shape[1], wout.shape[0]
    per_group = count // (2 * tile)

    def at(i):
        return (i // per_group) * per_group + per_group - 1 - lax.rem(i, per_group)

    def turned(columns):
        return pl.BlockSpec((tile, columns), lambda i: (at(i), 0))

    return pl.pallas_call(
        functools.partial(mixer_back_body, per_group),
        grid=(2 * per_group,),
        in_specs=[
            pl.BlockSpec((tile, width), lambda i: (jnp.maximum(per_group - 1 - i, 0), 0)),
            pl.BlockSpec(
                (tile, width), lambda i: (jnp.minimum(2 * per_group - 1 - i, per_group - 1), 0)
            ),
            whole(wout),
            turned(wide),
            turned(feats),
            pl.BlockSpec((1, 2, feats), lambda i: (i // per_group, 0, 0)),
            turned(masks.shape[1]),
            whole(taps),
        ],
        out_specs=[turned(wide), pl.BlockSpec((8, feats), lambda i: (0, 0))],
        out_shape=[
            out_array((count, wide), BF),
            out_array((8, feats), F32),
        ],
        scratch_shapes=[pltpu.VMEM((tile + 8, feats), F32), pltpu.VMEM((2, feats), F32)],
        compiler_params=params(24),
        cost_estimate=cost(),
    )(*pinned(*dh, wout, projected, mixed, halo, masks, taps))


def norm_back_body(counts, *refs):
    grad, refs = 0.0, list(refs)
    for count in counts:
        grad = grad + piece_tile(refs[:count]).astype(F32)
        refs = refs[count:]
    x_ref, gain_ref, up_ref, *outs = refs
    x = x_ref[...].astype(F32)
    scale = lax.rsqrt(jnp.mean(x * x, axis=1, keepdims=True) + EPS)
    scaled = x * scale
    weighted = grad * gain_ref[...]
    mean = jnp.mean(weighted * scaled, axis=1, keepdims=True)
    out = up_ref[...].astype(F32) + scale * (weighted - scaled * mean)
    for ref in outs[:-1]:
        ref[...] = out.astype(ref.dtype)

    @pl.when(pl.program_id(0) == 0)
    def _():
        outs[-1][...] = jnp.zeros_like(outs[-1])

    outs[-1][...] += jnp.sum(grad * scaled, axis=0, keepdims=True)


def norm_back(grads, x, gain, upstream, kinds, tile):
    count, width = x.shape
    line = pl.BlockSpec((1, width), lambda i: (0, 0))
    specs = [spec for pieces in grads for spec in piece_specs(pieces, tile)]
    out = pl.pallas_call(
        functools.partial(norm_back_body, [len(pieces) for pieces in grads]),
        grid=(count // tile,),
        in_specs=specs + [tiles(tile, width), line, tiles(tile, width)],
        out_specs=[tiles(tile, width)] * len(kinds) + [line],
        out_shape=[out_array((count, width), kind) for kind in kinds]
        + [jax.ShapeDtypeStruct((1, width), F32)],
        compiler_params=params(16),
        cost_estimate=cost(),
    )(*pinned(*[piece for pieces in grads for piece in pieces], x, gain[None], upstream))
    return out[:-1], out[-1][0]


def per_device(
    block_input,
    in_weight,
    out_weight,
    gate_weight,
    up_weight,
    down_weight,
    norm_gain,
    ffn_gain,
    conv_weight,
    seq_starts,
    cotangent,
):
    ax, ac, az, ay = Axis(("far", "x")), Axis("core"), Axis("z"), Axis("y")
    ap = Axis("x")
    nx, nz, far = ax.size, az.size, lax.axis_size("far")
    core = ac.here
    here = jnp.stack([ax.here, ay.here, az.here]).astype(jnp.int32)
    tokens, width = block_input.shape
    rows = in_weight.shape[0]
    hidden = gate_weight.shape[1] // 4
    feats = width // 2
    wide_cols = 3 * feats
    lower = nz // 2
    few = max(1, nz // 4)
    z_back = (0,) + az.steps
    first_back, second_back = z_back[:lower], z_back[lower:]

    small = jnp.concatenate(
        [norm_gain[:, None], ffn_gain[:, None], conv_weight, jnp.zeros((rows, 123), F32)], 1
    ).astype(BF)
    in_sets = in_weight.astype(BF).reshape(rows, 3 * nx, 2, feats // nx)

    def in_part(which):
        return jnp.concatenate([pick(in_sets, which, 2).reshape(rows, wide_cols), small], 1)

    in_mine, in_got = in_part(core), ac.shift(in_part(1 - core))
    starts_core = ac.shift(seq_starts)

    def split_hidden(weight):
        cut = weight.astype(BF).reshape(rows, far, 2, 2, hidden // far)
        return jnp.transpose(cut, (2, 3, 0, 1, 4)).reshape(2, 2, rows, hidden)

    in_mine, in_got, gate_weight, up_weight = fence(in_mine, in_got, gate_weight, up_weight)
    out_low = out_weight.astype(BF).reshape(rows, 2, feats).transpose(1, 0, 2)
    mix = jnp.concatenate([ordered(in_mine, in_got, core, 0), out_low], 2)
    mix_z = {by: az.shift(mix, by) for by in first_back[1:]}
    gate_up = jnp.concatenate([split_hidden(gate_weight), split_hidden(up_weight)], 3)
    pair_mine = pick(gate_up, core, 1)
    pair_got = ac.shift(pick(gate_up, 1 - core, 1))

    pair_mine, pair_got, mix, mix_z, cotangent, down_low = fence(
        pair_mine, pair_got, mix, mix_z, cotangent, down_weight.astype(BF)
    )
    first = jnp.stack([mix] + [mix_z[by] for by in first_back[1:]])
    first_y = ay.shift(first)
    second = [az.shift(mix, by) for by in second_back]
    pair = ordered(pair_mine, pair_got, core, 1)
    quad_mine, quad_got = pick(pair, ap.here, 0), ap.shift(pick(pair, 1 - ap.here, 0))
    quad = ordered(quad_mine, quad_got, ap.here, 0)
    first_x = [ax.shift(first, by) for by in ax.steps]
    second, first, first_y, first_x, quad, down_low = fence(
        second, first, first_y, first_x, quad, down_low
    )

    gathered = lax.all_gather(quad.reshape(4 * rows, 2 * hidden), SPREAD, axis=0, tiled=True)
    second = jnp.stack(second)
    second_x = [ax.shift(second, by) for by in ax.steps]
    second_y = ay.shift(second)
    second_x, second_y, second, first_y, block_input, cotangent, down_low = fence(
        second_x, second_y, second, first_y, block_input, cotangent, down_low
    )

    ffn_down = lax.all_gather(down_low, SPREAD, axis=0, tiled=True)
    first_yx = [ax.shift(first_y, by) for by in ax.steps]
    second_xy = [ay.shift(part) for part in second_x]
    x_core = ac.shift(block_input)
    dy_core = ac.shift(cotangent)
    x_all = jnp.concatenate([block_input, x_core], 0)
    starts = jnp.concatenate([seq_starts, starts_core], 0)
    position = lax.axis_index(("z", "y")) * tokens + jnp.arange(tokens + 2, dtype=jnp.int32)
    reached = starts[:, None, :] <= position[None, :, None]
    offset = position[None, :] - jnp.max(jnp.where(reached, starts[:, None, :], 0), axis=2)
    masks = [offset[:, :tokens] >= 1, offset[:, :tokens] >= 2]
    masks += [offset[:, 1 : 1 + tokens] >= 1, offset[:, 2:] >= 2]
    masks = jnp.stack(masks, 2).astype(F32).reshape(2 * tokens, 4)
    first_yx, second_xy, first, second, x_all, dy_core, masks, cotangent = fence(
        first_yx, second_xy, first, second, x_all, dy_core, masks, cotangent
    )

    dy_low, dy_high = cotangent[: tokens // 2], cotangent[tokens // 2 :]
    dy_low_x = ap.shift(dy_low)
    pieces = [(0, 0, first_back, first), (0, 1, first_back, first_y)]
    pieces += [(0, 0, second_back, second), (0, 1, second_back, second_y)]
    for n, dx in enumerate(ax.steps):
        pieces += [(dx, 0, first_back, first_x[n]), (dx, 1, first_back, first_yx[n])]
        pieces += [(dx, 0, second_back, second_x[n]), (dx, 1, second_back, second_xy[n])]
    mix_in, tiny, mix_out = place_mix(pieces, here, ax, ay, az, wide_cols, width)
    tiny = tiny[:, :8].astype(F32)
    gain_mix, gain_ffn = tiny[:, 0], tiny[:, 1]
    taps = pick(tiny[:, 2:5].reshape(nx, 2, feats // nx, 3), core, 1).reshape(feats, 3)

    taps = jnp.concatenate([taps.T, jnp.zeros((5, feats), F32)], 0)

    last = x_all.reshape(2, tokens, width)[:, tokens - 2 :].reshape(4, width).astype(F32)
    scale = lax.rsqrt(jnp.mean(last * last, axis=1, keepdims=True) + EPS)
    last = times((last * scale * gain_mix[None, :]).astype(BF), mix_in)
    halo = passed_along((last[:, :feats] * last[:, 2 * feats :]).reshape(2, 2, feats), 1)
    normed_mix, projected, mixed, gated, mixer_keep, mixer_send = mixer_forward(
        x_all, gain_mix, mix_in, halo, masks, taps, mix_out, tokens // 2
    )
    mixer_send, mixer_keep, dy_low_x = fence(mixer_send, mixer_keep, dy_low_x)

    mixer_got = ac.shift(mixer_send)
    dy_low_far = ac.shift(dy_low_x)
    own_inputs = block_input.astype(F32)
    h = own_inputs + (mixer_keep + mixer_got)
    scale_ffn = lax.rsqrt(jnp.mean(h * h, axis=1, keepdims=True) + EPS)
    normed_own = (h * scale_ffn * gain_ffn[None, :]).astype(BF)
    normed_core = ac.shift(normed_own)

    normed_core, normed_own, h, scale_ffn = fence(normed_core, normed_own, h, scale_ffn)
    normed_x = ap.shift(normed_own)
    gathered = gathered.reshape(far, 2 * nz, 4, rows, 2 * hidden)
    gate_up = gathered.transpose(0, 2, 1, 3, 4).reshape(width, 2 * hidden)
    near = [normed_own, normed_core]
    dy_near = [cotangent, dy_core]
    near_ev, near_s = ffn_forward(near, gate_up, tokens // 2)
    tile = 384 if hidden % 384 == 0 else hidden
    spec = pl.BlockSpec((tile, width), lambda i: (i, 0))
    near_down = weight_grad([near_s], dy_near, tile, spec, (hidden, width), F32)
    normed_x, near_ev, near_s, dy_high, near_down = fence(
        normed_x, near_ev, near_s, dy_high, near_down
    )

    dy_high_x = ap.shift(dy_high)
    far_tokens = [normed_x, ac.shift(normed_x)]
    far_ev, far_s = ffn_forward(far_tokens, gate_up, tokens // 2)
    far_s, far_ev, dy_high_x = fence(far_s, far_ev, dy_high_x)

    dy_far = [dy_low_x, dy_high_x, dy_low_far, ac.shift(dy_high_x)]
    grad_down = weight_grad([far_s], dy_far, tile, spec, (hidden, width), BF, [near_down])
    far_ev, far_s, grad_down, ffn_down = fence(far_ev, far_s, grad_down, ffn_down)

    down_own, down_send = cut(grad_down.reshape(far, nz, 2, -1, width), ay, 2)
    down_got = shifted(down_send, ay)
    far_dev, far_keep, far_send = ffn_back(dy_far, far_ev, ffn_down, gate_up, tokens // 2)
    far_got = [ac.shift(part) for part in far_send]
    far_fed, far_fed_send = row_halves(times, far_s, ffn_down, width, tokens // 2)
    down_own, down_got, far_dev, far_keep, far_got, far_fed, far_fed_send, near_ev, dy_near = fence(
        down_own, down_got, far_dev, far_keep, far_got, far_fed, far_fed_send, near_ev, dy_near
    )

    down_own, down_send = cut(summed(down_own, down_got).astype(BF), az, 1)
    down_got = shifted(down_send, az)
    normed_x_got = ap.shift((far_keep + jnp.concatenate(far_got, 0)).astype(BF))
    near_dev, near_keep, near_send = ffn_back(dy_near, near_ev, ffn_down, gate_up, tokens // 2)
    grad_gate_up = gate_up_grad(near + far_tokens, [near_dev, far_dev], far, nz, rows)
    normed_x_got, near_keep, near_send, grad_gate_up, down_own, down_got = fence(
        normed_x_got, near_keep, near_send, grad_gate_up, down_own, down_got
    )

    quad = lax.psum_scatter(grad_gate_up, SPREAD, scatter_dimension=0, tiled=True)
    near_got = [ac.shift(part) for part in near_send]
    far_fed_got = [ac.shift(part) for part in far_fed_send]
    near_got, near_keep, far_fed_got, far_fed = fence(near_got, near_keep, far_fed_got, far_fed)
    (grad_hidden, hidden_own), grad_gain_ffn = norm_back(
        [[near_keep], near_got, [normed_x_got]], h, gain_ffn, cotangent, (F32, BF), tokens // 4
    )
    hidden_got = ac.shift(hidden_own)

    hidden_got, hidden_own, grad_hidden, far_fed, far_fed_got = fence(
        hidden_got, hidden_own, grad_hidden, far_fed, far_fed_got
    )
    fed_x = ap.shift((far_fed + jnp.concatenate(far_fed_got, 0)).astype(BF))
    hidden_low = [hidden_own, hidden_got]
    opening = jnp.concatenate([part[:2] for part in hidden_low], 0)
    branch = projected.reshape(2, tokens, wide_cols)[:, :2, feats : 2 * feats].reshape(4, feats)
    opening = contract_cols(opening, mix_out) * branch
    later = passed_along(opening.reshape(2, 2, feats), -1)
    grad_projected, tap_grads = mixer_back(
        hidden_low, mix_out, projected, mixed, later, masks, taps, tokens // 2
    )
    if nx == 2 and rows % 16 == 0 and 2 * nz * rows % 128 == 0:
        blocks = mix_grad(normed_mix, grad_projected, gated, hidden_low, here, nz, rows, few)
    else:
        back_in = contract_rows(normed_mix, grad_projected).astype(BF)
        back_out = contract_rows(gated, jnp.concatenate(hidden_low, 0)).astype(BF)
        back_out = back_out.reshape(nx, nz, 2, rows, 2, feats).transpose(0, 4, 1, 2, 3, 5)
        back_mix = jnp.concatenate(
            [back_in.reshape(nx, 2, nz, 2, rows, wide_cols), back_out], 5
        )
        blocks = []
        for dx in (0,) + ax.steps:
            ys = [pick(pick(back_mix, ax.at(dx), 0), ay.at(dy), 2) for dy in range(2)]
            blocks.append([y[:, part] for part in (slice(few), slice(few, None)) for y in ys])
    blocks, grad_projected, near_s, fed_x = fence(blocks, grad_projected, near_s, fed_x)

    first_hop = [ay.shift(block[1]) for block in blocks[1:]]
    first_got = [ay.shift(blocks[0][1])]
    second_hop = [ax.shift(block[3], by) for block, by in zip(blocks[1:], ax.steps, strict=True)]
    mix_keep, mix_send, grad_gain_mix = input_grad(grad_projected, mix_in, x_all, tokens // 2)
    near_fed, near_fed_send = row_halves(times, near_s, ffn_down, width, tokens // 2)
    tap_rows = tap_grads[:3].reshape(3, nx, 1, feats // nx)
    on_core = (jnp.arange(2) == core).astype(F32)[None, None, :, None]
    tap_rows = (tap_rows * on_core).reshape(3, width)
    own_gain = jnp.concatenate([grad_gain_mix[None], grad_gain_ffn[None]], 0)
    terms = jnp.concatenate([own_gain, tap_rows], 0)
    first_hop, first_got, second_hop, blocks, mix_keep, mix_send, near_fed_send, terms = fence(
        first_hop, first_got, second_hop, blocks, mix_keep, mix_send, near_fed_send, terms
    )

    second_got = [ay.shift(summed(blocks[0][3], second_hop).astype(BF))]
    for n, by in enumerate(ax.steps):
        block = blocks[n + 1]
        first_got.append(ax.shift(summed(block[0], [first_hop[n]]).astype(BF), by))
        second_got.append(ax.shift(block[2], by))
    mix_got = [ac.shift(part) for part in mix_send]
    near_fed_got = [ac.shift(part) for part in near_fed_send]
    (grad_inputs,), _ = norm_back(
        [[mix_keep], mix_got], block_input, gain_mix, grad_hidden, (BF,), tokens // 4
    )
    for axis in (ac, ax):
        terms = summed(terms, [axis.shift(terms, by) for by in axis.steps])
    terms = terms.reshape(5, 2 * nx, nz, 2 * rows).transpose(2, 0, 1, 3).reshape(nz, -1)
    high = lax.reduce_precision(terms, 8, 7)
    terms = jnp.concatenate([high, terms - high], 1).astype(BF)
    extra = -(-terms.shape[1] // (2 * rows * 128)) * 128
    terms = jnp.pad(terms, ((0, 0), (0, 2 * rows * extra - terms.shape[1])))
    terms = terms.reshape(nz, 2, rows, extra).transpose(1, 0, 2, 3)
    first_got, second_got, blocks, grad_inputs, terms, near_fed_got = fence(
        first_got, second_got, blocks, grad_inputs, terms, near_fed_got
    )

    own_z = jnp.concatenate(
        [summed(blocks[0][0], first_got).astype(BF), summed(blocks[0][2], second_got).astype(BF)], 1
    )
    own_z = jnp.concatenate([own_z, terms], 3)
    mix_own, mix_send = cut(own_z, az, 1)
    mix_parts = shifted(mix_send, az)
    quad = quad.reshape(2, 2, rows, 2 * hidden)
    quad_mine, quad_send = cut(quad, ap, 0)
    quad_got = jnp.concatenate([ap.shift(part) for part in jnp.split(quad_send[0], 2, 2)], 2)
    mix_parts, mix_own, quad_mine, quad_got = fence(mix_parts, mix_own, quad_mine, quad_got)
    mix_sum = summed(mix_own, mix_parts)
    terms = mix_sum[..., wide_cols + feats :].reshape(-1)
    count = 5 * 4 * nx * rows
    terms = (terms[:count] + terms[count : 2 * count]).reshape(5, 4 * nx * rows)

    pair = ordered(quad_mine, quad_got, ap.here, 0)
    pair_mine, pair_send = cut(pair, ac, 1)
    pair_got = shifted(pair_send, ac)[0]

    terms = terms + ay.shift(terms)
    at = ((ax.here * 2 + core) * 2 + ay.here) * rows

    part_down = summed(down_own, down_got)
    if far > 1:
        part_down = lax.psum_scatter(part_down, "far", scatter_dimension=0, tiled=True)
    part_down = part_down[0]
    block_output = (h + (near_fed + jnp.concatenate(near_fed_got, 0) + fed_x.astype(F32))).astype(BF)
    part_out = mix_sum[..., wide_cols : wide_cols + feats].transpose(1, 0, 2).reshape(rows, width)
    in_mine, in_send = cut(mix_sum[..., :wide_cols], ac, 0)
    in_got = shifted(in_send, ac)[0]
    blocks = (rows, 3 * nx, feats // nx)
    part_in = ordered(in_mine.reshape(blocks), in_got.reshape(blocks), core, 2)
    quads = ordered(pair_mine, pair_got, core, 1).astype(F32)

    def join_hidden(sets):
        sets = sets.reshape(2, 2, rows, far, hidden // far)
        return jnp.transpose(sets, (2, 3, 0, 1, 4)).reshape(rows, 4 * hidden)

    part_gate, part_rise = join_hidden(quads[..., :hidden]), join_hidden(quads[..., hidden:])
    own_terms = lax.dynamic_slice_in_dim(terms, at, rows, 1)
    return (
        block_output,
        grad_inputs,
        part_in.reshape(rows, 3 * width),
        part_out,
        part_gate,
        part_rise,
        part_down,
        own_terms[0],
        own_terms[1],
        own_terms[2:].T,
    )


def solution(mesh):
    nd, nf = mesh.shape["dp"], mesh.shape["fsdp"]
    rows, line = P(AXES, None), P(AXES)
    return jax.shard_map(
        per_device,
        mesh=Mesh(mesh.devices.reshape(nd // 4, 2, 2, nf // 2, 2), AXES),
        in_specs=(rows,) * 6 + (line, line, rows, P(AXES[:3], None), rows),
        out_specs=(rows,) * 7 + (line, line, rows),
        check_vma=False,
    )
```

```python
import functools
import itertools
import math

import jax
import jax.numpy as jnp
from jax import lax
from jax.experimental import pallas as pl
from jax.experimental.pallas import tpu as pltpu
from jax.sharding import Mesh
from jax.sharding import PartitionSpec as P

EPS = 1e-05
AXES = ("far", "x", "core", "z", "y")
SPREAD = ("far", "z", "y")
BF = jnp.bfloat16
F32 = jnp.float32


class Axis:
    def __init__(self, name):
        self.name, self.size = name, lax.axis_size(name)
        self.here = lax.axis_index(name)
        near = sorted(range(1, self.size), key=lambda by: (min(by, self.size - by), by))
        self.steps = tuple(near)

    def shift(self, value, by=1):
        return lax.ppermute(value, self.name, [(i, (i + by) % self.size) for i in range(self.size)])

    def at(self, by):
        return lax.rem(self.here + by, self.size)


def passed_along(shard, by):
    peers = lax.axis_size(("z", "y"))
    pairs = [(i, i + by) for i in range(peers) if 0 <= i + by < peers]
    return lax.ppermute(shard, ("z", "y"), pairs)


def fence(*values):
    return lax.optimization_barrier(values)


def contract_rows(left, right):
    return lax.dot_general(
        left, right, (((0,), (0,)), ((), ())), preferred_element_type=F32
    )


def contract_cols(left, right):
    return lax.dot_general(
        left, right, (((1,), (1,)), ((), ())), preferred_element_type=F32
    )


def times(left, right):
    return jnp.dot(left, right, preferred_element_type=F32)


def pick(value, at, dim):
    return lax.dynamic_index_in_dim(value, at, dim, keepdims=False)


def ordered(mine, other, here, dim):
    low = jnp.where(here == 0, mine, other)
    high = jnp.where(here == 0, other, mine)
    return jnp.stack([low, high], dim)


def cut(value, axis, dim):
    return pick(value, axis.here, dim), [pick(value, axis.at(by), dim) for by in axis.steps]


def shifted(parts, axis):
    return [axis.shift(part, by) for part, by in zip(parts, axis.steps, strict=True)]


def summed(own, others):
    total = own.astype(F32)
    for other in others:
        total = total + other.astype(F32)
    return total


def place_body(moves, here_ref, *refs):
    sems = refs[-1]
    copies = []
    for i, (source, target) in enumerate(moves(here_ref, refs[:-1])):
        copy = pltpu.make_async_copy(source, target, sems.at[i])
        copy.start()
        copies.append(copy)
    for copy in copies:
        copy.wait()


def out_array(shape, kind):
    return pltpu.HBM(shape, kind) if math.prod(shape) >= 2**18 else jax.ShapeDtypeStruct(shape, kind)


def pinned(*arrays):
    return [
        pltpu.with_memory_space_constraint(a, pltpu.HBM) if a.size >= 2**18 else a for a in arrays
    ]


def kept(array):
    return pltpu.with_memory_space_constraint(array, pltpu.VMEM)


def place(moves, count, here, sources, shapes):
    return pl.pallas_call(
        functools.partial(place_body, moves),
        out_shape=[pltpu.VMEM(shape, BF) for shape in shapes],
        in_specs=[pl.BlockSpec(memory_space=pltpu.SMEM)]
        + [pl.BlockSpec(memory_space=pl.ANY)] * len(sources),
        out_specs=[pl.BlockSpec(memory_space=pltpu.VMEM)] * len(shapes),
        scratch_shapes=[pltpu.SemaphoreType.DMA((count,))],
        compiler_params=params(20),
        cost_estimate=pl.CostEstimate(flops=0, bytes_accessed=2**20, transcendentals=0),
    )(here, *pinned(*sources))


def back(at, by, size):
    return lax.rem(at + size - by, size)


def place_mix(pieces, here, ax, ay, az, columns, width):
    nx, ny, nz = ax.size, ay.size, az.size
    rows, half = pieces[0][3].shape[-2], width // 2

    def moves(at, refs):
        wide, small, narrow = refs[-3:]
        for (dx, dy, backs, _), source in zip(pieces, refs[:-3], strict=True):
            x, y = back(at[0], dx, nx), back(at[1], dy, ny)
            for n, dz in enumerate(backs):
                z = back(at[2], dz, nz)
                block = source.at[n]
                yield block.at[:, :, pl.ds(0, columns)], wide.at[x, :, z, y]
                yield block.at[:, :, pl.ds(columns, 128)], small.at[x, :, z, y]
                for k in range(2):
                    yield (
                        block.at[k, :, pl.ds(columns + 128, half)],
                        narrow.at[x, z, y, :, pl.ds(k * half, half)],
                    )

    lead = (nx, 2, nz, ny, rows)
    shapes = [lead + (columns,), lead + (128,), (nx, nz, ny, rows, width)]
    arrays = [piece[3] for piece in pieces]
    wide, small, narrow = place(moves, 4 * nx * ny * nz, here, arrays, shapes)
    return wide.reshape(-1, columns), small.reshape(-1, 128), narrow.reshape(-1, width)


def cost():
    return pl.CostEstimate(flops=0, bytes_accessed=2**16, transcendentals=0)


def params(mib):
    return pltpu.CompilerParams(vmem_limit_bytes=mib * 1024 * 1024)


def whole(array):
    return pl.BlockSpec(
        array.shape, lambda i: (0,) * array.ndim, pipeline_mode=pl.Buffered(1)
    )


def tiles(rows, columns):
    return pl.BlockSpec((rows, columns), lambda i: (i, 0))


def chunks(columns):
    step = 384 if columns % 384 == 0 else 128 if columns % 128 == 0 else columns
    return [(a, step) for a in range(0, columns, step)]


def logistic(v):
    return 0.5 * jnp.tanh(0.5 * v) + 0.5


def piece_specs(pieces, tile):
    specs = []
    for p, piece in enumerate(pieces):
        first, last = p * piece.shape[0] // tile, (p + 1) * piece.shape[0] // tile - 1

        def at(i, first=first, last=last):
            return jnp.clip(i - first, 0, last - first), 0

        specs.append(pl.BlockSpec((tile, piece.shape[1]), at))
    return specs


def piece_tile(refs):
    steps = pl.num_programs(0) // len(refs)
    value = refs[0][...]
    for p, ref in enumerate(refs[1:], 1):
        value = jnp.where(pl.program_id(0) >= p * steps, ref[...], value)
    return value


def forward_body(count, *refs):
    w_ref, ev_ref, s_ref = refs[count:]
    hidden = s_ref.shape[1]
    x = piece_tile(refs[:count])
    for a, n in chunks(hidden):
        gate = times(x, w_ref[:, a : a + n])
        rise = times(x, w_ref[:, hidden + a : hidden + a + n])
        ev_ref[:, a : a + n] = gate.astype(BF)
        ev_ref[:, hidden + a : hidden + a + n] = rise.astype(BF)
        s_ref[:, a : a + n] = (gate * logistic(gate) * rise).astype(BF)


def ffn_forward(pieces, w, tile):
    count, both = sum(piece.shape[0] for piece in pieces), w.shape[1]
    return pl.pallas_call(
        functools.partial(forward_body, len(pieces)),
        grid=(count // tile,),
        in_specs=piece_specs(pieces, tile) + [whole(w)],
        out_specs=[tiles(tile, both), tiles(tile, both // 2)],
        out_shape=[out_array((count, both), BF), out_array((count, both // 2), BF)],
        compiler_params=params(24),
        cost_estimate=cost(),
    )(*pinned(*pieces, w))


def back_body(count, half, *refs):
    ev_ref, down_ref, w_ref, dev_ref, keep_ref, *sends = refs[count:]
    hidden = down_ref.shape[0]
    dy = piece_tile(refs[:count])
    for a, n in chunks(hidden):
        back = contract_cols(dy, down_ref[a : a + n, :])
        gate = ev_ref[:, a : a + n].astype(F32)
        rise = ev_ref[:, hidden + a : hidden + a + n].astype(F32)
        sigma = logistic(gate)
        back = back * sigma
        dev_ref[:, a : a + n] = (back * rise * (1.0 + gate * (1.0 - sigma))).astype(BF)
        dev_ref[:, hidden + a : hidden + a + n] = (back * gate).astype(BF)
    split_pieces(half, contract_cols(dev_ref[...], w_ref[...]), keep_ref, sends)


def split_rows(half, value, keep_ref, send_ref):
    @pl.when(pl.program_id(0) < half)
    def _():
        keep_ref[...] = value

    @pl.when(pl.program_id(0) >= half)
    def _():
        send_ref[...] = value.astype(send_ref.dtype)


def split_specs(tile, columns, half):
    return [
        pl.BlockSpec((tile, columns), lambda i: (jnp.minimum(i, half - 1), 0)),
        pl.BlockSpec((tile, columns), lambda i: (jnp.maximum(i - half, 0), 0)),
    ]


def split_pieces(half, value, keep_ref, sends):
    cuts = len(sends) // half
    size = value.shape[0] // cuts

    @pl.when(pl.program_id(0) < half)
    def _():
        keep_ref[...] = value

    for n, ref in enumerate(sends):

        @pl.when(pl.program_id(0) == half + n // cuts)
        def _(n=n, ref=ref):
            at = n % cuts * size
            ref[...] = value[at : at + size].astype(ref.dtype)


def piece_outputs(count, width, tile, cuts):
    half, size = count // (2 * tile), tile // cuts
    specs = split_specs(tile, width, half)[:1]
    specs += [pl.BlockSpec((size, width), lambda i: (0, 0))] * (half * cuts)
    shapes = [out_array((count // 2, width), F32)]
    return specs, shapes + [out_array((size, width), BF)] * (half * cuts)


def ffn_back(pieces, ev, down, w, tile):
    count, both = ev.shape
    width, half = down.shape[1], count // (2 * tile)
    specs, shapes = piece_outputs(count, width, tile, 2)
    out = pl.pallas_call(
        functools.partial(back_body, len(pieces), half),
        grid=(2 * half,),
        in_specs=piece_specs(pieces, tile) + [tiles(tile, both), whole(down), whole(w)],
        out_specs=[tiles(tile, both)] + specs,
        out_shape=[pltpu.VMEM((count, both), BF)] + shapes,
        compiler_params=params(32),
        cost_estimate=cost(),
    )(*pinned(*pieces, ev, down, w))
    return out[0], out[1], out[2:]


def rows_body(function, half, left_ref, weight_ref, keep_ref, *sends):
    split_pieces(half, function(left_ref[...], weight_ref[...]), keep_ref, sends)


def row_halves(function, left, weight, width, tile):
    count = left.shape[0]
    half = count // (2 * tile)
    specs, shapes = piece_outputs(count, width, tile, 2)
    out = pl.pallas_call(
        functools.partial(rows_body, function, half),
        grid=(2 * half,),
        in_specs=[tiles(tile, left.shape[1]), whole(weight)],
        out_specs=specs,
        out_shape=shapes,
        compiler_params=params(20),
        cost_estimate=cost(),
    )(*pinned(left, weight))
    return out[0], out[1:]


def input_grad_body(half, dp_ref, win_ref, x_ref, keep_ref, *refs):
    sends, gain_ref = refs[:-1], refs[-1]
    value = contract_cols(dp_ref[...], win_ref[...])
    split_pieces(half, value, keep_ref, sends)
    x = x_ref[...].astype(F32)
    scale = lax.rsqrt(jnp.mean(x * x, axis=1, keepdims=True) + EPS)

    @pl.when(pl.program_id(0) == 0)
    def _():
        gain_ref[...] = jnp.zeros_like(gain_ref)

    gain_ref[...] += jnp.sum(value * (x * scale), axis=0, keepdims=True)


def input_grad(dp, win, x, tile):
    count, width = x.shape
    half = count // (2 * tile)
    specs, shapes = piece_outputs(count, width, tile, 2)
    out = pl.pallas_call(
        functools.partial(input_grad_body, half),
        grid=(2 * half,),
        in_specs=[tiles(tile, dp.shape[1]), whole(win), tiles(tile, width)],
        out_specs=specs + [pl.BlockSpec((1, width), lambda i: (0, 0))],
        out_shape=shapes + [jax.ShapeDtypeStruct((1, width), F32)],
        compiler_params=params(24),
        cost_estimate=cost(),
    )(*pinned(dp, win, x))
    return out[0], out[1:-1], out[-1][0]


def grad_body(lefts, rights, *refs):
    rest = refs[len(lefts) + len(rights) :]
    total = None
    for i, (first, end) in enumerate(lefts):
        for j, (start, stop) in enumerate(rights):
            low, high = max(first, start), min(end, stop)
            if low < high:
                left = refs[i][low - first : high - first, :]
                right = refs[len(lefts) + j][low - start : high - start, :]
                term = contract_rows(left, right)
                total = term if total is None else total + term
    for ref in rest[:-1]:
        total = total + ref[...]
    rest[-1][...] = total.astype(rest[-1].dtype).reshape(rest[-1].shape)


def token_spans(pieces):
    ends = list(itertools.accumulate(piece.shape[0] for piece in pieces))
    return list(zip([0] + ends[:-1], ends, strict=True))


def weight_grad(lefts, rights, tile, out_spec, shape, kind=BF, extra=(), stay=False):
    rows = lefts[0].shape[1]
    return pl.pallas_call(
        functools.partial(grad_body, token_spans(lefts), token_spans(rights)),
        grid=(rows // tile,),
        in_specs=[pl.BlockSpec((left.shape[0], tile), lambda i: (0, i)) for left in lefts]
        + [whole(right) for right in rights]
        + [out_spec] * len(extra),
        out_specs=out_spec,
        out_shape=out_array(shape, kind),
        compiler_params=params(34),
        cost_estimate=cost(),
    )(*pinned(*lefts), *(kept(right) if stay else pinned(right)[0] for right in rights), *pinned(*extra))


def gate_up_grad(lefts, rights, far, nz, rows):
    columns, width = rights[0].shape[1], lefts[0].shape[1]
    tile = 2 * nz * rows
    if tile % 128 == 0 and rows % 16 == 0:
        block = (1, 2 * nz, 1, rows, columns)
        spec = pl.BlockSpec(block, lambda i: (i // 4, 0, i % 4, 0, 0))
        out = weight_grad(lefts, rights, tile, spec, (far, 2 * nz, 4, rows, columns), stay=True)
    else:
        out = weight_grad(lefts, rights, 256, tiles(256, columns), (width, columns), stay=True)
        out = out.reshape(far, 4, 2 * nz, rows, columns).transpose(0, 2, 1, 3, 4)
    return out.reshape(width, columns)


def mix_grad_body(lower, here_ref, a_ref, dp_ref, g_ref, dh_ref, dh2_ref, *refs):
    group, wide, columns = dh_ref.shape[0], dp_ref.shape[1], refs[0].shape[-1]
    out = contract_rows(g_ref[:group, :], dh_ref[...])
    out = out + contract_rows(g_ref[group:, :], dh2_ref[...])
    parts = (
        (contract_rows(a_ref[...], dp_ref[...]), slice(0, wide)),
        (out, slice(wide, columns)),
    )
    own_y = here_ref[1] == 0
    for value, where in parts:
        value = value.astype(BF).reshape(-1, 2, refs[0].shape[2], value.shape[1])
        low, high = value[:, 0], value[:, 1]
        own, other = jnp.where(own_y, low, high), jnp.where(own_y, high, low)
        blocks = (own[:lower], other[:lower], own[lower:], other[lower:])
        for dx in range(2):

            @pl.when(lax.rem(pl.program_id(1) + here_ref[0], 2) == dx)
            def _(blocks=blocks, targets=refs[4 * dx : 4 * dx + 4], where=where):
                for block, target in zip(blocks, targets, strict=True):
                    target[0, :, :, where] = block


def mix_grad(normed, grad_projected, gated, hidden_low, here, nz, rows, lower):
    count, wide = grad_projected.shape
    half = hidden_low[0].shape[1] // 2
    columns, tile = wide + half, 2 * nz * rows
    shapes = [(2, n, rows, columns) for n in (lower, lower, nz - lower, nz - lower)] * 2
    out = pl.pallas_call(
        functools.partial(mix_grad_body, lower),
        grid=(2, 2),
        in_specs=[
            pl.BlockSpec(memory_space=pltpu.SMEM),
            pl.BlockSpec((count, tile), lambda k, x: (0, 2 * x + k)),
            pl.BlockSpec((count, wide), lambda k, x: (0, 0), pipeline_mode=pl.Buffered(1)),
            pl.BlockSpec((count, tile), lambda k, x: (0, x)),
            pl.BlockSpec((count // 2, half), lambda k, x: (0, k)),
            pl.BlockSpec((count // 2, half), lambda k, x: (0, k)),
        ],
        out_specs=[pl.BlockSpec((1,) + shape[1:], lambda k, x: (k, 0, 0, 0)) for shape in shapes],
        out_shape=[out_array(shape, BF) for shape in shapes],
        compiler_params=params(24),
        cost_estimate=cost(),
    )(here, *pinned(normed, grad_projected, gated, *hidden_low))
    return [out[:4], out[4:]]


def mixer_body(
    per_group, x_ref, gain_ref, win_ref, halo_ref, masks_ref, taps_ref, wout_ref, *refs
):
    normed_ref, projected_ref, mixed_ref, gated_ref, keep_ref, send_ref, rows, carry = refs
    count, feats = mixed_ref.shape
    x = x_ref[...].astype(F32)
    scale = lax.rsqrt(jnp.mean(x * x, axis=1, keepdims=True) + EPS)
    normed = (x * scale * gain_ref[...]).astype(BF)
    normed_ref[...] = normed
    projected = times(normed, win_ref[...])
    projected_ref[...] = projected
    product = projected[:, :feats] * projected[:, 2 * feats :]
    opens = lax.rem(pl.program_id(0), per_group) == 0
    rows[6:8, :] = jnp.where(opens, halo_ref[0], carry[...])
    rows[8 : 8 + count, :] = product
    mixed = taps_ref[2:3, :] * product
    mixed = mixed + masks_ref[:, 0:1] * (taps_ref[1:2, :] * rows[7 : 7 + count, :])
    mixed = mixed + masks_ref[:, 1:2] * (taps_ref[0:1, :] * rows[6 : 6 + count, :])
    carry[...] = product[count - 2 :]
    mixed_ref[...] = mixed
    gated = (projected[:, feats : 2 * feats] * mixed).astype(BF)
    gated_ref[...] = gated
    half = pl.num_programs(0) // 2
    split_rows(half, times(gated, wout_ref[...]), keep_ref, send_ref)


def mixer_forward(x, gain, win, halo, masks, taps, wout, tile):
    count, width = x.shape
    wide, feats = win.shape[1], wout.shape[0]
    per_group = count // (2 * tile)
    row = pl.BlockSpec((1, width), lambda i: (0, 0))
    return pl.pallas_call(
        functools.partial(mixer_body, per_group),
        grid=(2 * per_group,),
        in_specs=[
            tiles(tile, width),
            row,
            whole(win),
            pl.BlockSpec((1, 2, feats), lambda i: (i // per_group, 0, 0)),
            tiles(tile, masks.shape[1]),
            whole(taps),
            whole(wout),
        ],
        out_specs=[tiles(tile, width), tiles(tile, wide), tiles(tile, feats), tiles(tile, feats)]
        + split_specs(tile, width, per_group),
        out_shape=[
            out_array((count, width), BF),
            out_array((count, wide), F32),
            out_array((count, feats), F32),
            out_array((count, feats), BF),
        ]
        + [out_array((count // 2, width), kind) for kind in (F32, BF)],
        scratch_shapes=[pltpu.VMEM((tile + 8, feats), F32), pltpu.VMEM((2, feats), F32)],
        compiler_params=params(28),
        cost_estimate=cost(),
    )(*pinned(x, gain[None]), kept(win), *pinned(halo, masks, taps), kept(wout))


def mixer_back_body(
    per_group, dh_ref, dh2_ref, wout_ref, projected_ref, mixed_ref, halo_ref, masks_ref, *refs
):
    taps_ref, *refs = refs
    out_ref, grad_ref, rows, carry = refs
    count, feats = mixed_ref.shape
    projected = projected_ref[...]
    dh = jnp.where(pl.program_id(0) < per_group, dh_ref[...], dh2_ref[...])
    back = contract_cols(dh, wout_ref[...])
    grad_c = back * mixed_ref[...]
    grad_mixed = back * projected[:, feats : 2 * feats]
    closes = lax.rem(pl.program_id(0), per_group) == 0
    rows[0:count, :] = grad_mixed
    rows[count : count + 2, :] = jnp.where(closes, halo_ref[0], carry[...])
    carry[...] = grad_mixed[:2]
    ahead = (
        grad_mixed,
        masks_ref[:, 2:3] * rows[1 : 1 + count, :],
        masks_ref[:, 3:4] * rows[2 : 2 + count, :],
    )
    grad_product = sum(taps_ref[2 - lag : 3 - lag, :] * ahead[lag] for lag in range(3))
    b_branch, x_branch = projected[:, :feats], projected[:, 2 * feats :]
    out_ref[:, :feats] = (grad_product * x_branch).astype(BF)
    out_ref[:, feats : 2 * feats] = grad_c.astype(BF)
    out_ref[:, 2 * feats :] = (grad_product * b_branch).astype(BF)

    @pl.when(pl.program_id(0) == 0)
    def _():
        grad_ref[...] = jnp.zeros_like(grad_ref)

    product = b_branch * x_branch
    for lag in range(3):
        grad_ref[2 - lag : 3 - lag, :] += jnp.sum(product * ahead[lag], axis=0, keepdims=True)


def mixer_back(dh, wout, projected, mixed, halo, masks, taps, tile):
    count, wide = projected.shape
    width, feats = dh[0].shape[1], wout.shape[0]
    per_group = count // (2 * tile)

    def at(i):
        return (i // per_group) * per_group + per_group - 1 - lax.rem(i, per_group)

    def turned(columns):
        return pl.BlockSpec((tile, columns), lambda i: (at(i), 0))

    return pl.pallas_call(
        functools.partial(mixer_back_body, per_group),
        grid=(2 * per_group,),
        in_specs=[
            pl.BlockSpec((tile, width), lambda i: (jnp.maximum(per_group - 1 - i, 0), 0)),
            pl.BlockSpec(
                (tile, width), lambda i: (jnp.minimum(2 * per_group - 1 - i, per_group - 1), 0)
            ),
            whole(wout),
            turned(wide),
            turned(feats),
            pl.BlockSpec((1, 2, feats), lambda i: (i // per_group, 0, 0)),
            turned(masks.shape[1]),
            whole(taps),
        ],
        out_specs=[turned(wide), pl.BlockSpec((8, feats), lambda i: (0, 0))],
        out_shape=[
            out_array((count, wide), BF),
            out_array((8, feats), F32),
        ],
        scratch_shapes=[pltpu.VMEM((tile + 8, feats), F32), pltpu.VMEM((2, feats), F32)],
        compiler_params=params(24),
        cost_estimate=cost(),
    )(*pinned(*dh, wout, projected, mixed, halo, masks, taps))


def norm_back_body(counts, *refs):
    grad, refs = 0.0, list(refs)
    for count in counts:
        grad = grad + piece_tile(refs[:count]).astype(F32)
        refs = refs[count:]
    x_ref, gain_ref, up_ref, *outs = refs
    x = x_ref[...].astype(F32)
    scale = lax.rsqrt(jnp.mean(x * x, axis=1, keepdims=True) + EPS)
    scaled = x * scale
    weighted = grad * gain_ref[...]
    mean = jnp.mean(weighted * scaled, axis=1, keepdims=True)
    out = up_ref[...].astype(F32) + scale * (weighted - scaled * mean)
    for ref in outs[:-1]:
        ref[...] = out.astype(ref.dtype)

    @pl.when(pl.program_id(0) == 0)
    def _():
        outs[-1][...] = jnp.zeros_like(outs[-1])

    outs[-1][...] += jnp.sum(grad * scaled, axis=0, keepdims=True)


def norm_back(grads, x, gain, upstream, kinds, tile):
    count, width = x.shape
    line = pl.BlockSpec((1, width), lambda i: (0, 0))
    specs = [spec for pieces in grads for spec in piece_specs(pieces, tile)]
    out = pl.pallas_call(
        functools.partial(norm_back_body, [len(pieces) for pieces in grads]),
        grid=(count // tile,),
        in_specs=specs + [tiles(tile, width), line, tiles(tile, width)],
        out_specs=[tiles(tile, width)] * len(kinds) + [line],
        out_shape=[out_array((count, width), kind) for kind in kinds]
        + [jax.ShapeDtypeStruct((1, width), F32)],
        compiler_params=params(16),
        cost_estimate=cost(),
    )(*pinned(*[piece for pieces in grads for piece in pieces], x, gain[None], upstream))
    return out[:-1], out[-1][0]


def per_device(
    block_input,
    in_weight,
    out_weight,
    gate_weight,
    up_weight,
    down_weight,
    norm_gain,
    ffn_gain,
    conv_weight,
    seq_starts,
    cotangent,
):
    ax, ac, az, ay = Axis(("far", "x")), Axis("core"), Axis("z"), Axis("y")
    ap = Axis("x")
    nx, nz, far = ax.size, az.size, lax.axis_size("far")
    core = ac.here
    here = jnp.stack([ax.here, ay.here, az.here]).astype(jnp.int32)
    tokens, width = block_input.shape
    rows = in_weight.shape[0]
    hidden = gate_weight.shape[1] // 4
    feats = width // 2
    wide_cols = 3 * feats
    lower = nz // 2
    few = max(1, nz // 4)
    z_back = (0,) + az.steps
    first_back, second_back = z_back[:lower], z_back[lower:]

    small = jnp.concatenate(
        [norm_gain[:, None], ffn_gain[:, None], conv_weight, jnp.zeros((rows, 123), F32)], 1
    ).astype(BF)
    in_sets = in_weight.astype(BF).reshape(rows, 3 * nx, 2, feats // nx)

    def in_part(which):
        return jnp.concatenate([pick(in_sets, which, 2).reshape(rows, wide_cols), small], 1)

    in_mine, in_got = in_part(core), ac.shift(in_part(1 - core))
    starts_core = ac.shift(seq_starts)

    def split_hidden(weight):
        cut = weight.astype(BF).reshape(rows, far, 2, 2, hidden // far)
        return jnp.transpose(cut, (2, 3, 0, 1, 4)).reshape(2, 2, rows, hidden)

    in_mine, in_got, gate_weight, up_weight = fence(in_mine, in_got, gate_weight, up_weight)
    out_low = out_weight.astype(BF).reshape(rows, 2, feats).transpose(1, 0, 2)
    mix = jnp.concatenate([ordered(in_mine, in_got, core, 0), out_low], 2)
    mix_z = {by: az.shift(mix, by) for by in first_back[1:]}
    gate_up = jnp.concatenate([split_hidden(gate_weight), split_hidden(up_weight)], 3)
    pair_mine = pick(gate_up, core, 1)
    pair_send = jnp.split(pick(gate_up, 1 - core, 1), 2, 2)
    pair_got = jnp.concatenate([ac.shift(part) for part in pair_send], 2)

    pair_mine, pair_got, mix, mix_z, cotangent, down_low = fence(
        pair_mine, pair_got, mix, mix_z, cotangent, down_weight.astype(BF)
    )
    first = jnp.stack([mix] + [mix_z[by] for by in first_back[1:]])
    first_y = ay.shift(first)
    second = [az.shift(mix, by) for by in second_back]
    pair = ordered(pair_mine, pair_got, core, 1)
    quad_mine, quad_got = pick(pair, ap.here, 0), ap.shift(pick(pair, 1 - ap.here, 0))
    quad = ordered(quad_mine, quad_got, ap.here, 0)
    first_x = [ax.shift(first, by) for by in ax.steps]
    second, first, first_y, first_x, quad, down_low = fence(
        second, first, first_y, first_x, quad, down_low
    )

    gathered = lax.all_gather(quad.reshape(4 * rows, 2 * hidden), SPREAD, axis=0, tiled=True)
    second = jnp.stack(second)
    second_x = [ax.shift(second, by) for by in ax.steps]
    second_y = ay.shift(second)
    second_x, second_y, second, first_y, block_input, cotangent, down_low = fence(
        second_x, second_y, second, first_y, block_input, cotangent, down_low
    )

    ffn_down = lax.all_gather(down_low, SPREAD, axis=0, tiled=True)
    first_yx = [ax.shift(first_y, by) for by in ax.steps]
    second_xy = [ay.shift(part) for part in second_x]
    x_core = ac.shift(block_input)
    dy_core = ac.shift(cotangent)
    x_all = jnp.concatenate([block_input, x_core], 0)
    starts = jnp.concatenate([seq_starts, starts_core], 0)
    position = lax.axis_index(("z", "y")) * tokens + jnp.arange(tokens + 2, dtype=jnp.int32)
    reached = starts[:, None, :] <= position[None, :, None]
    offset = position[None, :] - jnp.max(jnp.where(reached, starts[:, None, :], 0), axis=2)
    masks = [offset[:, :tokens] >= 1, offset[:, :tokens] >= 2]
    masks += [offset[:, 1 : 1 + tokens] >= 1, offset[:, 2:] >= 2]
    masks = jnp.stack(masks, 2).astype(F32).reshape(2 * tokens, 4)
    first_yx, second_xy, first, second, x_all, dy_core, masks, cotangent = fence(
        first_yx, second_xy, first, second, x_all, dy_core, masks, cotangent
    )

    dy_low, dy_high = cotangent[: tokens // 2], cotangent[tokens // 2 :]
    dy_low_x = ap.shift(dy_low)
    pieces = [(0, 0, first_back, first), (0, 1, first_back, first_y)]
    pieces += [(0, 0, second_back, second), (0, 1, second_back, second_y)]
    for n, dx in enumerate(ax.steps):
        pieces += [(dx, 0, first_back, first_x[n]), (dx, 1, first_back, first_yx[n])]
        pieces += [(dx, 0, second_back, second_x[n]), (dx, 1, second_back, second_xy[n])]
    mix_in, tiny, mix_out = place_mix(pieces, here, ax, ay, az, wide_cols, width)
    tiny = tiny[:, :8].astype(F32)
    gain_mix, gain_ffn = tiny[:, 0], tiny[:, 1]
    taps = pick(tiny[:, 2:5].reshape(nx, 2, feats // nx, 3), core, 1).reshape(feats, 3)

    taps = jnp.concatenate([taps.T, jnp.zeros((5, feats), F32)], 0)

    last = x_all.reshape(2, tokens, width)[:, tokens - 2 :].reshape(4, width).astype(F32)
    scale = lax.rsqrt(jnp.mean(last * last, axis=1, keepdims=True) + EPS)
    last = times((last * scale * gain_mix[None, :]).astype(BF), mix_in)
    halo = passed_along((last[:, :feats] * last[:, 2 * feats :]).reshape(2, 2, feats), 1)
    normed_mix, projected, mixed, gated, mixer_keep, mixer_send = mixer_forward(
        x_all, gain_mix, mix_in, halo, masks, taps, mix_out, tokens // 2
    )
    mixer_send, mixer_keep, dy_low_x = fence(mixer_send, mixer_keep, dy_low_x)

    mixer_got = ac.shift(mixer_send)
    dy_low_far = ac.shift(dy_low_x)
    own_inputs = block_input.astype(F32)
    h = own_inputs + (mixer_keep + mixer_got)
    scale_ffn = lax.rsqrt(jnp.mean(h * h, axis=1, keepdims=True) + EPS)
    normed_own = (h * scale_ffn * gain_ffn[None, :]).astype(BF)
    normed_core = ac.shift(normed_own)

    normed_core, normed_own, h, scale_ffn = fence(normed_core, normed_own, h, scale_ffn)
    normed_x = ap.shift(normed_own)
    gathered = gathered.reshape(far, 2 * nz, 4, rows, 2 * hidden)
    gate_up = gathered.transpose(0, 2, 1, 3, 4).reshape(width, 2 * hidden)
    near = [normed_own, normed_core]
    dy_near = [cotangent, dy_core]
    near_ev, near_s = ffn_forward(near, gate_up, tokens // 2)
    tile = 384 if hidden % 384 == 0 else hidden
    spec = pl.BlockSpec((tile, width), lambda i: (i, 0))
    near_down = weight_grad([near_s], dy_near, tile, spec, (hidden, width), F32)
    normed_x, near_ev, near_s, dy_high, near_down = fence(
        normed_x, near_ev, near_s, dy_high, near_down
    )

    dy_high_x = ap.shift(dy_high)
    far_tokens = [normed_x, ac.shift(normed_x)]
    far_ev, far_s = ffn_forward(far_tokens, gate_up, tokens // 2)
    far_s, far_ev, dy_high_x = fence(far_s, far_ev, dy_high_x)

    dy_far = [dy_low_x, dy_high_x, dy_low_far, ac.shift(dy_high_x)]
    grad_down = weight_grad([far_s], dy_far, tile, spec, (hidden, width), BF, [near_down])
    far_ev, far_s, grad_down = fence(far_ev, far_s, grad_down)

    down_own, down_send = cut(grad_down.reshape(far, nz, 2, -1, width), ay, 2)
    down_got = shifted(down_send, ay)
    far_dev, far_keep, far_send = ffn_back(dy_far, far_ev, ffn_down, gate_up, tokens // 2)
    far_got = [ac.shift(part) for part in far_send]
    far_fed, far_fed_send = row_halves(times, far_s, ffn_down, width, tokens // 2)
    down_own, down_got, far_dev, far_keep, far_got, far_fed, far_fed_send, near_ev, dy_near = fence(
        down_own, down_got, far_dev, far_keep, far_got, far_fed, far_fed_send, near_ev, dy_near
    )

    down_own, down_send = cut(summed(down_own, down_got).astype(BF), az, 1)
    down_got = shifted(down_send, az)
    normed_x_got = ap.shift((far_keep + jnp.concatenate(far_got, 0)).astype(BF))
    near_dev, near_keep, near_send = ffn_back(dy_near, near_ev, ffn_down, gate_up, tokens // 2)
    grad_gate_up = gate_up_grad(near + far_tokens, [near_dev, far_dev], far, nz, rows)
    normed_x_got, near_keep, near_send, grad_gate_up, down_own, down_got = fence(
        normed_x_got, near_keep, near_send, grad_gate_up, down_own, down_got
    )

    quad = lax.psum_scatter(grad_gate_up, SPREAD, scatter_dimension=0, tiled=True)
    near_got = [ac.shift(part) for part in near_send]
    far_fed_got = [ac.shift(part) for part in far_fed_send]
    near_got, near_keep, far_fed_got, far_fed = fence(near_got, near_keep, far_fed_got, far_fed)
    (grad_hidden, hidden_own), grad_gain_ffn = norm_back(
        [[near_keep], near_got, [normed_x_got]], h, gain_ffn, cotangent, (F32, BF), tokens // 4
    )
    hidden_got = ac.shift(hidden_own)

    hidden_got, hidden_own, grad_hidden, far_fed, far_fed_got = fence(
        hidden_got, hidden_own, grad_hidden, far_fed, far_fed_got
    )
    fed_x = ap.shift((far_fed + jnp.concatenate(far_fed_got, 0)).astype(BF))
    hidden_low = [hidden_own, hidden_got]
    opening = jnp.concatenate([part[:2] for part in hidden_low], 0)
    branch = projected.reshape(2, tokens, wide_cols)[:, :2, feats : 2 * feats].reshape(4, feats)
    opening = contract_cols(opening, mix_out) * branch
    later = passed_along(opening.reshape(2, 2, feats), -1)
    grad_projected, tap_grads = mixer_back(
        hidden_low, mix_out, projected, mixed, later, masks, taps, tokens // 2
    )
    if nx == 2 and rows % 16 == 0 and 2 * nz * rows % 128 == 0:
        blocks = mix_grad(normed_mix, grad_projected, gated, hidden_low, here, nz, rows, few)
    else:
        back_in = contract_rows(normed_mix, grad_projected).astype(BF)
        back_out = contract_rows(gated, jnp.concatenate(hidden_low, 0)).astype(BF)
        back_out = back_out.reshape(nx, nz, 2, rows, 2, feats).transpose(0, 4, 1, 2, 3, 5)
        back_mix = jnp.concatenate(
            [back_in.reshape(nx, 2, nz, 2, rows, wide_cols), back_out], 5
        )
        blocks = []
        for dx in (0,) + ax.steps:
            ys = [pick(pick(back_mix, ax.at(dx), 0), ay.at(dy), 2) for dy in range(2)]
            blocks.append([y[:, part] for part in (slice(few), slice(few, None)) for y in ys])
    blocks, grad_projected, near_s, fed_x = fence(blocks, grad_projected, near_s, fed_x)

    first_hop = [ay.shift(block[1]) for block in blocks[1:]]
    first_got = [ay.shift(blocks[0][1])]
    second_hop = [ax.shift(block[3], by) for block, by in zip(blocks[1:], ax.steps, strict=True)]
    mix_keep, mix_send, grad_gain_mix = input_grad(grad_projected, mix_in, x_all, tokens // 2)
    near_fed, near_fed_send = row_halves(times, near_s, ffn_down, width, tokens // 2)
    tap_rows = tap_grads[:3].reshape(3, nx, 1, feats // nx)
    on_core = (jnp.arange(2) == core).astype(F32)[None, None, :, None]
    tap_rows = (tap_rows * on_core).reshape(3, width)
    own_gain = jnp.concatenate([grad_gain_mix[None], grad_gain_ffn[None]], 0)
    terms = jnp.concatenate([own_gain, tap_rows], 0)
    first_hop, first_got, second_hop, blocks, mix_keep, mix_send, near_fed_send, terms = fence(
        first_hop, first_got, second_hop, blocks, mix_keep, mix_send, near_fed_send, terms
    )

    second_got = [ay.shift(summed(blocks[0][3], second_hop).astype(BF))]
    for n, by in enumerate(ax.steps):
        block = blocks[n + 1]
        first_got.append(ax.shift(summed(block[0], [first_hop[n]]).astype(BF), by))
        second_got.append(ax.shift(block[2], by))
    mix_got = [ac.shift(part) for part in mix_send]
    near_fed_got = [ac.shift(part) for part in near_fed_send]
    (grad_inputs,), _ = norm_back(
        [[mix_keep], mix_got], block_input, gain_mix, grad_hidden, (BF,), tokens // 4
    )
    for axis in (ac, ax):
        terms = summed(terms, [axis.shift(terms, by) for by in axis.steps])
    terms = terms.reshape(5, 2 * nx, nz, 2 * rows).transpose(2, 0, 1, 3).reshape(nz, -1)
    high = lax.reduce_precision(terms, 8, 7)
    terms = jnp.concatenate([high, terms - high], 1).astype(BF)
    extra = -(-terms.shape[1] // (2 * rows * 128)) * 128
    terms = jnp.pad(terms, ((0, 0), (0, 2 * rows * extra - terms.shape[1])))
    terms = terms.reshape(nz, 2, rows, extra).transpose(1, 0, 2, 3)
    first_got, second_got, blocks, grad_inputs, terms, near_fed_got = fence(
        first_got, second_got, blocks, grad_inputs, terms, near_fed_got
    )

    own_z = jnp.concatenate(
        [summed(blocks[0][0], first_got).astype(BF), summed(blocks[0][2], second_got).astype(BF)], 1
    )
    own_z = jnp.concatenate([own_z, terms], 3)
    mix_own, mix_send = cut(own_z, az, 1)
    mix_parts = shifted(mix_send, az)
    quad = quad.reshape(4, rows, 2 * hidden)
    quad = [pick(quad, (2 * ap.here + core) ^ step, 0) for step in range(4)]
    quad[1:] = [
        lax.ppermute(part, ("x", "core"), [(i, i ^ step) for i in range(4)])
        for step, part in enumerate(quad[1:], 1)
    ]
    mix_parts, mix_own, quad = fence(mix_parts, mix_own, quad)
    mix_sum = summed(mix_own, mix_parts)
    terms = mix_sum[..., wide_cols + feats :].reshape(-1)
    count = 5 * 4 * nx * rows
    terms = (terms[:count] + terms[count : 2 * count]).reshape(5, 4 * nx * rows)

    terms = terms + ay.shift(terms)
    at = ((ax.here * 2 + core) * 2 + ay.here) * rows
    sides = [ordered(quad[n], quad[n + 1], core, 0) for n in (0, 2)]
    part_down = summed(down_own, down_got)
    if far > 1:
        part_down = lax.psum_scatter(part_down, "far", scatter_dimension=0, tiled=True)
    part_down = part_down[0]
    block_output = (h + (near_fed + jnp.concatenate(near_fed_got, 0) + fed_x.astype(F32))).astype(BF)
    part_out = mix_sum[..., wide_cols : wide_cols + feats].transpose(1, 0, 2).reshape(rows, width)
    in_mine, in_send = cut(mix_sum[..., :wide_cols], ac, 0)
    in_got = shifted(in_send, ac)[0]
    blocks = (rows, 3 * nx, feats // nx)
    part_in = ordered(in_mine.reshape(blocks), in_got.reshape(blocks), core, 2)
    quads = ordered(*sides, ap.here, 0).astype(F32)

    def join_hidden(sets):
        sets = sets.reshape(2, 2, rows, far, hidden // far)
        return jnp.transpose(sets, (2, 3, 0, 1, 4)).reshape(rows, 4 * hidden)

    part_gate, part_rise = join_hidden(quads[..., :hidden]), join_hidden(quads[..., hidden:])
    own_terms = lax.dynamic_slice_in_dim(terms, at, rows, 1)
    return (
        block_output,
        grad_inputs,
        part_in.reshape(rows, 3 * width),
        part_out,
        part_gate,
        part_rise,
        part_down,
        own_terms[0],
        own_terms[1],
        own_terms[2:].T,
    )


def solution(mesh):
    nd, nf = mesh.shape["dp"], mesh.shape["fsdp"]
    rows, line = P(AXES, None), P(AXES)
    return jax.shard_map(
        per_device,
        mesh=Mesh(mesh.devices.reshape(nd // 4, 2, 2, nf // 2, 2), AXES),
        in_specs=(rows,) * 6 + (line, line, rows, P(AXES[:3], None), rows),
        out_specs=(rows,) * 7 + (line, line, rows),
        check_vma=False,
    )
```

```python
import functools
import itertools
import math

import jax
import jax.numpy as jnp
from jax import lax
from jax.experimental import pallas as pl
from jax.experimental.pallas import tpu as pltpu
from jax.sharding import Mesh
from jax.sharding import PartitionSpec as P

EPS = 1e-05
AXES = ("far", "x", "core", "z", "y")
SPREAD = ("far", "z", "y")
BF = jnp.bfloat16
F32 = jnp.float32


class Axis:
    def __init__(self, name):
        self.name, self.size = name, lax.axis_size(name)
        self.here = lax.axis_index(name)
        near = sorted(range(1, self.size), key=lambda by: (min(by, self.size - by), by))
        self.steps = tuple(near)

    def shift(self, value, by=1):
        return lax.ppermute(value, self.name, [(i, (i + by) % self.size) for i in range(self.size)])

    def at(self, by):
        return lax.rem(self.here + by, self.size)


def passed_along(shard, by):
    peers = lax.axis_size(("z", "y"))
    pairs = [(i, i + by) for i in range(peers) if 0 <= i + by < peers]
    return lax.ppermute(shard, ("z", "y"), pairs)


def fence(*values):
    return lax.optimization_barrier(values)


def contract_rows(left, right):
    return lax.dot_general(
        left, right, (((0,), (0,)), ((), ())), preferred_element_type=F32
    )


def contract_cols(left, right):
    return lax.dot_general(
        left, right, (((1,), (1,)), ((), ())), preferred_element_type=F32
    )


def times(left, right):
    return jnp.dot(left, right, preferred_element_type=F32)


def pick(value, at, dim):
    return lax.dynamic_index_in_dim(value, at, dim, keepdims=False)


def ordered(mine, other, here, dim):
    low = jnp.where(here == 0, mine, other)
    high = jnp.where(here == 0, other, mine)
    return jnp.stack([low, high], dim)


def cut(value, axis, dim):
    return pick(value, axis.here, dim), [pick(value, axis.at(by), dim) for by in axis.steps]


def shifted(parts, axis):
    return [axis.shift(part, by) for part, by in zip(parts, axis.steps, strict=True)]


def summed(own, others):
    total = own.astype(F32)
    for other in others:
        total = total + other.astype(F32)
    return total


def place_body(moves, here_ref, *refs):
    sems = refs[-1]
    copies = []
    for i, (source, target) in enumerate(moves(here_ref, refs[:-1])):
        copy = pltpu.make_async_copy(source, target, sems.at[i])
        copy.start()
        copies.append(copy)
    for copy in copies:
        copy.wait()


def out_array(shape, kind):
    return pltpu.HBM(shape, kind) if math.prod(shape) >= 2**18 else jax.ShapeDtypeStruct(shape, kind)


def pinned(*arrays):
    return [
        pltpu.with_memory_space_constraint(a, pltpu.HBM) if a.size >= 2**18 else a for a in arrays
    ]


def kept(array):
    return pltpu.with_memory_space_constraint(array, pltpu.VMEM)


def place(moves, count, here, sources, shapes):
    return pl.pallas_call(
        functools.partial(place_body, moves),
        out_shape=[pltpu.VMEM(shape, BF) for shape in shapes],
        in_specs=[pl.BlockSpec(memory_space=pltpu.SMEM)]
        + [pl.BlockSpec(memory_space=pl.ANY)] * len(sources),
        out_specs=[pl.BlockSpec(memory_space=pltpu.VMEM)] * len(shapes),
        scratch_shapes=[pltpu.SemaphoreType.DMA((count,))],
        compiler_params=params(20),
        cost_estimate=pl.CostEstimate(flops=0, bytes_accessed=2**20, transcendentals=0),
    )(here, *pinned(*sources))


def back(at, by, size):
    return lax.rem(at + size - by, size)


def place_mix(pieces, here, ax, ay, az, columns, width):
    nx, ny, nz = ax.size, ay.size, az.size
    rows, half = pieces[0][3].shape[-2], width // 2

    def moves(at, refs):
        wide, small, narrow = refs[-3:]
        for (dx, dy, backs, _), source in zip(pieces, refs[:-3], strict=True):
            x, y = back(at[0], dx, nx), back(at[1], dy, ny)
            for n, dz in enumerate(backs):
                z = back(at[2], dz, nz)
                block = source.at[n]
                yield block.at[:, :, pl.ds(0, columns)], wide.at[x, :, z, y]
                yield block.at[:, :, pl.ds(columns, 128)], small.at[x, :, z, y]
                for k in range(2):
                    yield (
                        block.at[k, :, pl.ds(columns + 128, half)],
                        narrow.at[x, z, y, :, pl.ds(k * half, half)],
                    )

    lead = (nx, 2, nz, ny, rows)
    shapes = [lead + (columns,), lead + (128,), (nx, nz, ny, rows, width)]
    arrays = [piece[3] for piece in pieces]
    wide, small, narrow = place(moves, 4 * nx * ny * nz, here, arrays, shapes)
    return wide.reshape(-1, columns), small.reshape(-1, 128), narrow.reshape(-1, width)


def cost():
    return pl.CostEstimate(flops=0, bytes_accessed=2**16, transcendentals=0)


def params(mib):
    return pltpu.CompilerParams(vmem_limit_bytes=mib * 1024 * 1024)


def whole(array):
    return pl.BlockSpec(
        array.shape, lambda i: (0,) * array.ndim, pipeline_mode=pl.Buffered(1)
    )


def tiles(rows, columns):
    return pl.BlockSpec((rows, columns), lambda i: (i, 0))


def chunks(columns):
    step = 384 if columns % 384 == 0 else 128 if columns % 128 == 0 else columns
    return [(a, step) for a in range(0, columns, step)]


def logistic(v):
    return 0.5 * jnp.tanh(0.5 * v) + 0.5


def piece_specs(pieces, tile):
    specs = []
    for p, piece in enumerate(pieces):
        first, last = p * piece.shape[0] // tile, (p + 1) * piece.shape[0] // tile - 1

        def at(i, first=first, last=last):
            return jnp.clip(i - first, 0, last - first), 0

        specs.append(pl.BlockSpec((tile, piece.shape[1]), at))
    return specs


def piece_tile(refs):
    steps = pl.num_programs(0) // len(refs)
    value = refs[0][...]
    for p, ref in enumerate(refs[1:], 1):
        value = jnp.where(pl.program_id(0) >= p * steps, ref[...], value)
    return value


def forward_body(count, *refs):
    w_ref, ev_ref, s_ref = refs[count:]
    hidden = s_ref.shape[1]
    x = piece_tile(refs[:count])
    for a, n in chunks(hidden):
        gate = times(x, w_ref[:, a : a + n])
        rise = times(x, w_ref[:, hidden + a : hidden + a + n])
        ev_ref[:, a : a + n] = gate.astype(BF)
        ev_ref[:, hidden + a : hidden + a + n] = rise.astype(BF)
        s_ref[:, a : a + n] = (gate * logistic(gate) * rise).astype(BF)


def ffn_forward(pieces, w, tile):
    count, both = sum(piece.shape[0] for piece in pieces), w.shape[1]
    return pl.pallas_call(
        functools.partial(forward_body, len(pieces)),
        grid=(count // tile,),
        in_specs=piece_specs(pieces, tile) + [whole(w)],
        out_specs=[tiles(tile, both), tiles(tile, both // 2)],
        out_shape=[out_array((count, both), BF), out_array((count, both // 2), BF)],
        compiler_params=params(24),
        cost_estimate=cost(),
    )(*pinned(*pieces, w))


def back_body(count, half, *refs):
    ev_ref, down_ref, w_ref, dev_ref, keep_ref, *sends = refs[count:]
    hidden = down_ref.shape[0]
    dy = piece_tile(refs[:count])
    for a, n in chunks(hidden):
        back = contract_cols(dy, down_ref[a : a + n, :])
        gate = ev_ref[:, a : a + n].astype(F32)
        rise = ev_ref[:, hidden + a : hidden + a + n].astype(F32)
        sigma = logistic(gate)
        back = back * sigma
        dev_ref[:, a : a + n] = (back * rise * (1.0 + gate * (1.0 - sigma))).astype(BF)
        dev_ref[:, hidden + a : hidden + a + n] = (back * gate).astype(BF)
    split_pieces(half, contract_cols(dev_ref[...], w_ref[...]), keep_ref, sends)


def split_rows(half, value, keep_ref, send_ref):
    @pl.when(pl.program_id(0) < half)
    def _():
        keep_ref[...] = value

    @pl.when(pl.program_id(0) >= half)
    def _():
        send_ref[...] = value.astype(send_ref.dtype)


def split_specs(tile, columns, half):
    return [
        pl.BlockSpec((tile, columns), lambda i: (jnp.minimum(i, half - 1), 0)),
        pl.BlockSpec((tile, columns), lambda i: (jnp.maximum(i - half, 0), 0)),
    ]


def split_pieces(half, value, keep_ref, sends):
    cuts = len(sends) // half
    size = value.shape[0] // cuts

    @pl.when(pl.program_id(0) < half)
    def _():
        keep_ref[...] = value

    for n, ref in enumerate(sends):

        @pl.when(pl.program_id(0) == half + n // cuts)
        def _(n=n, ref=ref):
            at = n % cuts * size
            ref[...] = value[at : at + size].astype(ref.dtype)


def piece_outputs(count, width, tile, cuts):
    half, size = count // (2 * tile), tile // cuts
    specs = split_specs(tile, width, half)[:1]
    specs += [pl.BlockSpec((size, width), lambda i: (0, 0))] * (half * cuts)
    shapes = [out_array((count // 2, width), F32)]
    return specs, shapes + [out_array((size, width), BF)] * (half * cuts)


def ffn_back(pieces, ev, down, w, tile):
    count, both = ev.shape
    width, half = down.shape[1], count // (2 * tile)
    specs, shapes = piece_outputs(count, width, tile, 1)
    out = pl.pallas_call(
        functools.partial(back_body, len(pieces), half),
        grid=(2 * half,),
        in_specs=piece_specs(pieces, tile) + [tiles(tile, both), whole(down), whole(w)],
        out_specs=[tiles(tile, both)] + specs,
        out_shape=[pltpu.VMEM((count, both), BF)] + shapes,
        compiler_params=params(32),
        cost_estimate=cost(),
    )(*pinned(*pieces, ev, down, w))
    return out[0], out[1], out[2:]


def rows_body(function, half, left_ref, weight_ref, keep_ref, *sends):
    split_pieces(half, function(left_ref[...], weight_ref[...]), keep_ref, sends)


def row_halves(function, left, weight, width, tile):
    count = left.shape[0]
    half = count // (2 * tile)
    specs, shapes = piece_outputs(count, width, tile, 2)
    out = pl.pallas_call(
        functools.partial(rows_body, function, half),
        grid=(2 * half,),
        in_specs=[tiles(tile, left.shape[1]), whole(weight)],
        out_specs=specs,
        out_shape=shapes,
        compiler_params=params(20),
        cost_estimate=cost(),
    )(*pinned(left, weight))
    return out[0], out[1:]


def input_grad_body(half, dp_ref, win_ref, x_ref, keep_ref, *refs):
    sends, gain_ref = refs[:-1], refs[-1]
    value = contract_cols(dp_ref[...], win_ref[...])
    split_pieces(half, value, keep_ref, sends)
    x = x_ref[...].astype(F32)
    scale = lax.rsqrt(jnp.mean(x * x, axis=1, keepdims=True) + EPS)

    @pl.when(pl.program_id(0) == 0)
    def _():
        gain_ref[...] = jnp.zeros_like(gain_ref)

    gain_ref[...] += jnp.sum(value * (x * scale), axis=0, keepdims=True)


def input_grad(dp, win, x, tile):
    count, width = x.shape
    half = count // (2 * tile)
    specs, shapes = piece_outputs(count, width, tile, 2)
    out = pl.pallas_call(
        functools.partial(input_grad_body, half),
        grid=(2 * half,),
        in_specs=[tiles(tile, dp.shape[1]), whole(win), tiles(tile, width)],
        out_specs=specs + [pl.BlockSpec((1, width), lambda i: (0, 0))],
        out_shape=shapes + [jax.ShapeDtypeStruct((1, width), F32)],
        compiler_params=params(24),
        cost_estimate=cost(),
    )(*pinned(dp, win, x))
    return out[0], out[1:-1], out[-1][0]


def grad_body(lefts, rights, *refs):
    rest = refs[len(lefts) + len(rights) :]
    total = None
    for i, (first, end) in enumerate(lefts):
        for j, (start, stop) in enumerate(rights):
            low, high = max(first, start), min(end, stop)
            if low < high:
                left = refs[i][low - first : high - first, :]
                right = refs[len(lefts) + j][low - start : high - start, :]
                term = contract_rows(left, right)
                total = term if total is None else total + term
    for ref in rest[:-1]:
        total = total + ref[...]
    rest[-1][...] = total.astype(rest[-1].dtype).reshape(rest[-1].shape)


def token_spans(pieces):
    ends = list(itertools.accumulate(piece.shape[0] for piece in pieces))
    return list(zip([0] + ends[:-1], ends, strict=True))


def weight_grad(lefts, rights, tile, out_spec, shape, kind=BF, extra=(), stay=False):
    rows = lefts[0].shape[1]
    return pl.pallas_call(
        functools.partial(grad_body, token_spans(lefts), token_spans(rights)),
        grid=(rows // tile,),
        in_specs=[pl.BlockSpec((left.shape[0], tile), lambda i: (0, i)) for left in lefts]
        + [whole(right) for right in rights]
        + [out_spec] * len(extra),
        out_specs=out_spec,
        out_shape=out_array(shape, kind),
        compiler_params=params(34),
        cost_estimate=cost(),
    )(*pinned(*lefts), *(kept(right) if stay else pinned(right)[0] for right in rights), *pinned(*extra))


def gate_up_grad(lefts, rights, far, nz, rows):
    columns, width = rights[0].shape[1], lefts[0].shape[1]
    tile = 2 * nz * rows
    if tile % 128 == 0 and rows % 16 == 0:
        block = (1, 2 * nz, 1, rows, columns)
        spec = pl.BlockSpec(block, lambda i: (i // 4, 0, i % 4, 0, 0))
        out = weight_grad(lefts, rights, tile, spec, (far, 2 * nz, 4, rows, columns), stay=True)
    else:
        out = weight_grad(lefts, rights, 256, tiles(256, columns), (width, columns), stay=True)
        out = out.reshape(far, 4, 2 * nz, rows, columns).transpose(0, 2, 1, 3, 4)
    return out.reshape(width, columns)


def mixer_body(
    per_group, x_ref, gain_ref, win_ref, halo_ref, masks_ref, taps_ref, wout_ref, *refs
):
    normed_ref, projected_ref, mixed_ref, gated_ref, keep_ref, send_ref, rows, carry = refs
    count, feats = mixed_ref.shape
    x = x_ref[...].astype(F32)
    scale = lax.rsqrt(jnp.mean(x * x, axis=1, keepdims=True) + EPS)
    normed = (x * scale * gain_ref[...]).astype(BF)
    normed_ref[...] = normed
    projected = times(normed, win_ref[...])
    projected_ref[...] = projected
    product = projected[:, :feats] * projected[:, 2 * feats :]
    opens = lax.rem(pl.program_id(0), per_group) == 0
    rows[6:8, :] = jnp.where(opens, halo_ref[0], carry[...])
    rows[8 : 8 + count, :] = product
    mixed = taps_ref[2:3, :] * product
    mixed = mixed + masks_ref[:, 0:1] * (taps_ref[1:2, :] * rows[7 : 7 + count, :])
    mixed = mixed + masks_ref[:, 1:2] * (taps_ref[0:1, :] * rows[6 : 6 + count, :])
    carry[...] = product[count - 2 :]
    mixed_ref[...] = mixed
    gated = (projected[:, feats : 2 * feats] * mixed).astype(BF)
    gated_ref[...] = gated
    half = pl.num_programs(0) // 2
    split_rows(half, times(gated, wout_ref[...]), keep_ref, send_ref)


def mixer_forward(x, gain, win, halo, masks, taps, wout, tile):
    count, width = x.shape
    wide, feats = win.shape[1], wout.shape[0]
    per_group = count // (2 * tile)
    row = pl.BlockSpec((1, width), lambda i: (0, 0))
    return pl.pallas_call(
        functools.partial(mixer_body, per_group),
        grid=(2 * per_group,),
        in_specs=[
            tiles(tile, width),
            row,
            whole(win),
            pl.BlockSpec((1, 2, feats), lambda i: (i // per_group, 0, 0)),
            tiles(tile, masks.shape[1]),
            whole(taps),
            whole(wout),
        ],
        out_specs=[tiles(tile, width), tiles(tile, wide), tiles(tile, feats), tiles(tile, feats)]
        + split_specs(tile, width, per_group),
        out_shape=[
            out_array((count, width), BF),
            out_array((count, wide), F32),
            out_array((count, feats), F32),
            out_array((count, feats), BF),
        ]
        + [out_array((count // 2, width), kind) for kind in (F32, BF)],
        scratch_shapes=[pltpu.VMEM((tile + 8, feats), F32), pltpu.VMEM((2, feats), F32)],
        compiler_params=params(28),
        cost_estimate=cost(),
    )(*pinned(x, gain[None]), kept(win), *pinned(halo, masks, taps), kept(wout))


def mixer_back_body(
    per_group, dh_ref, dh2_ref, wout_ref, projected_ref, mixed_ref, halo_ref, masks_ref, *refs
):
    taps_ref, *refs = refs
    out_ref, grad_ref, rows, carry = refs
    count, feats = mixed_ref.shape
    projected = projected_ref[...]
    dh = jnp.where(pl.program_id(0) < per_group, dh_ref[...], dh2_ref[...])
    back = contract_cols(dh, wout_ref[...])
    grad_c = back * mixed_ref[...]
    grad_mixed = back * projected[:, feats : 2 * feats]
    closes = lax.rem(pl.program_id(0), per_group) == 0
    rows[0:count, :] = grad_mixed
    rows[count : count + 2, :] = jnp.where(closes, halo_ref[0], carry[...])
    carry[...] = grad_mixed[:2]
    ahead = (
        grad_mixed,
        masks_ref[:, 2:3] * rows[1 : 1 + count, :],
        masks_ref[:, 3:4] * rows[2 : 2 + count, :],
    )
    grad_product = sum(taps_ref[2 - lag : 3 - lag, :] * ahead[lag] for lag in range(3))
    b_branch, x_branch = projected[:, :feats], projected[:, 2 * feats :]
    out_ref[:, :feats] = (grad_product * x_branch).astype(BF)
    out_ref[:, feats : 2 * feats] = grad_c.astype(BF)
    out_ref[:, 2 * feats :] = (grad_product * b_branch).astype(BF)

    @pl.when(pl.program_id(0) == 0)
    def _():
        grad_ref[...] = jnp.zeros_like(grad_ref)

    product = b_branch * x_branch
    for lag in range(3):
        grad_ref[2 - lag : 3 - lag, :] += jnp.sum(product * ahead[lag], axis=0, keepdims=True)


def mixer_back(dh, wout, projected, mixed, halo, masks, taps, tile):
    count, wide = projected.shape
    width, feats = dh[0].shape[1], wout.shape[0]
    per_group = count // (2 * tile)

    def at(i):
        return (i // per_group) * per_group + per_group - 1 - lax.rem(i, per_group)

    def turned(columns):
        return pl.BlockSpec((tile, columns), lambda i: (at(i), 0))

    return pl.pallas_call(
        functools.partial(mixer_back_body, per_group),
        grid=(2 * per_group,),
        in_specs=[
            pl.BlockSpec((tile, width), lambda i: (jnp.maximum(per_group - 1 - i, 0), 0)),
            pl.BlockSpec(
                (tile, width), lambda i: (jnp.minimum(2 * per_group - 1 - i, per_group - 1), 0)
            ),
            whole(wout),
            turned(wide),
            turned(feats),
            pl.BlockSpec((1, 2, feats), lambda i: (i // per_group, 0, 0)),
            turned(masks.shape[1]),
            whole(taps),
        ],
        out_specs=[turned(wide), pl.BlockSpec((8, feats), lambda i: (0, 0))],
        out_shape=[
            out_array((count, wide), BF),
            out_array((8, feats), F32),
        ],
        scratch_shapes=[pltpu.VMEM((tile + 8, feats), F32), pltpu.VMEM((2, feats), F32)],
        compiler_params=params(24),
        cost_estimate=cost(),
    )(*pinned(*dh, wout, projected, mixed, halo, masks, taps))


def mixer_grads_body(per_group, lower, here_ref, normed_ref, gated_ref, *refs):
    ins, out_ref, grad_ref = refs[:8], refs[8], refs[9]
    blocks, (rows, carry, in_sum, out_sum) = refs[10:18], refs[18:]
    mixer_back_body(per_group, *ins, out_ref, grad_ref, rows, carry)
    width, wide = in_sum.shape
    tile = width // 4

    @pl.when(pl.program_id(0) == 0)
    def _():
        in_sum[...] = jnp.zeros_like(in_sum)
        out_sum[...] = jnp.zeros_like(out_sum)

    grad = out_ref[...]
    dh = jnp.where(pl.program_id(0) < per_group, ins[0][...], ins[1][...])
    for q in range(4):
        part = slice(q * tile, (q + 1) * tile)
        in_sum[part, :] += contract_rows(normed_ref[:, part], grad)
    for x in range(2):
        part = slice(x * tile, (x + 1) * tile)
        out_sum[part, :] += contract_rows(gated_ref[:, part], dh)

    @pl.when(pl.program_id(0) == pl.num_programs(0) - 1)
    def _():
        own_y = here_ref[1] == 0
        half = width // 2
        for dx in range(2):
            x = lax.rem(here_ref[0] + dx, 2)
            for k in range(2):
                q = pl.multiple_of((2 * x + k) * tile, tile)
                parts = (
                    (in_sum[pl.ds(q, tile), :], slice(0, wide)),
                    (
                        out_sum[pl.ds(pl.multiple_of(x * tile, tile), tile), k * half : (k + 1) * half],
                        slice(wide, wide + half),
                    ),
                )
                for value, where in parts:
                    value = value.astype(BF).reshape(-1, 2, blocks[0].shape[2], value.shape[1])
                    low, high = value[:, 0], value[:, 1]
                    own, other = jnp.where(own_y, low, high), jnp.where(own_y, high, low)
                    cuts = (own[:lower], other[:lower], own[lower:], other[lower:])
                    for cut_, target in zip(cuts, blocks[4 * dx : 4 * dx + 4], strict=True):
                        target[k, :, :, where] = cut_


def mixer_grads(dh, wout, projected, mixed, halo, masks, taps, normed, gated, here, nz, rows, lower, tile):
    count, wide = projected.shape
    width, feats = dh[0].shape[1], wout.shape[0]
    per_group = count // (2 * tile)

    def at(i):
        return (i // per_group) * per_group + per_group - 1 - lax.rem(i, per_group)

    def turned(columns):
        return pl.BlockSpec((tile, columns), lambda i: (at(i), 0))

    def fixed(shape):
        return pl.BlockSpec(shape, lambda i: (0,) * len(shape))

    columns = wide + width // 2
    shapes = [(2, n, rows, columns) for n in (lower, lower, nz - lower, nz - lower)] * 2
    out = pl.pallas_call(
        functools.partial(mixer_grads_body, per_group, lower),
        grid=(2 * per_group,),
        in_specs=[
            pl.BlockSpec(memory_space=pltpu.SMEM),
            turned(width),
            turned(feats),
            pl.BlockSpec((tile, width), lambda i: (jnp.maximum(per_group - 1 - i, 0), 0)),
            pl.BlockSpec(
                (tile, width), lambda i: (jnp.minimum(2 * per_group - 1 - i, per_group - 1), 0)
            ),
            whole(wout),
            turned(wide),
            turned(feats),
            pl.BlockSpec((1, 2, feats), lambda i: (i // per_group, 0, 0)),
            turned(masks.shape[1]),
            whole(taps),
        ],
        out_specs=[turned(wide), fixed((8, feats))] + [fixed(shape) for shape in shapes],
        out_shape=[out_array((count, wide), BF), out_array((8, feats), F32)]
        + [out_array(shape, BF) for shape in shapes],
        scratch_shapes=[
            pltpu.VMEM((tile + 8, feats), F32),
            pltpu.VMEM((2, feats), F32),
            pltpu.VMEM((width, wide), F32),
            pltpu.VMEM((feats, width), F32),
        ],
        compiler_params=params(46),
        cost_estimate=cost(),
    )(here, *pinned(normed, gated, *dh, wout, projected, mixed, halo, masks, taps))
    return out[0], out[1], [out[2:6], out[6:]]


def norm_back_body(counts, *refs):
    grad, refs = 0.0, list(refs)
    for count in counts:
        grad = grad + piece_tile(refs[:count]).astype(F32)
        refs = refs[count:]
    x_ref, gain_ref, up_ref, *outs = refs
    x = x_ref[...].astype(F32)
    scale = lax.rsqrt(jnp.mean(x * x, axis=1, keepdims=True) + EPS)
    scaled = x * scale
    weighted = grad * gain_ref[...]
    mean = jnp.mean(weighted * scaled, axis=1, keepdims=True)
    out = up_ref[...].astype(F32) + scale * (weighted - scaled * mean)
    for ref in outs[:-1]:
        ref[...] = out.astype(ref.dtype)

    @pl.when(pl.program_id(0) == 0)
    def _():
        outs[-1][...] = jnp.zeros_like(outs[-1])

    outs[-1][...] += jnp.sum(grad * scaled, axis=0, keepdims=True)


def norm_back(grads, x, gain, upstream, kinds, tile):
    count, width = x.shape
    line = pl.BlockSpec((1, width), lambda i: (0, 0))
    specs = [spec for pieces in grads for spec in piece_specs(pieces, tile)]
    out = pl.pallas_call(
        functools.partial(norm_back_body, [len(pieces) for pieces in grads]),
        grid=(count // tile,),
        in_specs=specs + [tiles(tile, width), line, tiles(tile, width)],
        out_specs=[tiles(tile, width)] * len(kinds) + [line],
        out_shape=[out_array((count, width), kind) for kind in kinds]
        + [jax.ShapeDtypeStruct((1, width), F32)],
        compiler_params=params(16),
        cost_estimate=cost(),
    )(*pinned(*[piece for pieces in grads for piece in pieces], x, gain[None], upstream))
    return out[:-1], out[-1][0]


def per_device(
    block_input,
    in_weight,
    out_weight,
    gate_weight,
    up_weight,
    down_weight,
    norm_gain,
    ffn_gain,
    conv_weight,
    seq_starts,
    cotangent,
):
    ax, ac, az, ay = Axis(("far", "x")), Axis("core"), Axis("z"), Axis("y")
    ap = Axis("x")
    nx, nz, far = ax.size, az.size, lax.axis_size("far")
    core = ac.here
    here = jnp.stack([ax.here, ay.here, az.here]).astype(jnp.int32)
    tokens, width = block_input.shape
    rows = in_weight.shape[0]
    hidden = gate_weight.shape[1] // 4
    feats = width // 2
    wide_cols = 3 * feats
    lower = nz // 2
    few = max(1, nz // 4)
    z_back = (0,) + az.steps
    first_back, second_back = z_back[:lower], z_back[lower:]

    small = jnp.concatenate(
        [norm_gain[:, None], ffn_gain[:, None], conv_weight, jnp.zeros((rows, 123), F32)], 1
    ).astype(BF)
    in_sets = in_weight.astype(BF).reshape(rows, 3 * nx, 2, feats // nx)

    def in_part(which):
        return jnp.concatenate([pick(in_sets, which, 2).reshape(rows, wide_cols), small], 1)

    in_mine, in_got = in_part(core), ac.shift(in_part(1 - core))
    starts_core = ac.shift(seq_starts)

    def split_hidden(weight):
        cut = weight.astype(BF).reshape(rows, far, 2, 2, hidden // far)
        return jnp.transpose(cut, (2, 3, 0, 1, 4)).reshape(2, 2, rows, hidden)

    in_mine, in_got, gate_weight, up_weight = fence(in_mine, in_got, gate_weight, up_weight)
    out_low = out_weight.astype(BF).reshape(rows, 2, feats).transpose(1, 0, 2)
    mix = jnp.concatenate([ordered(in_mine, in_got, core, 0), out_low], 2)
    mix_z = {by: az.shift(mix, by) for by in first_back[1:]}
    gate_up = jnp.concatenate([split_hidden(gate_weight), split_hidden(up_weight)], 3)
    pair_mine = pick(gate_up, core, 1)
    pair_send = jnp.split(pick(gate_up, 1 - core, 1), 2, 2)
    pair_got = jnp.concatenate([ac.shift(part) for part in pair_send], 2)

    pair_mine, pair_got, mix, mix_z, cotangent, down_low = fence(
        pair_mine, pair_got, mix, mix_z, cotangent, down_weight.astype(BF)
    )
    first = jnp.stack([mix] + [mix_z[by] for by in first_back[1:]])
    first_y = ay.shift(first)
    second = [az.shift(mix, by) for by in second_back]
    pair = ordered(pair_mine, pair_got, core, 1)
    quad_mine, quad_got = pick(pair, ap.here, 0), ap.shift(pick(pair, 1 - ap.here, 0))
    quad = ordered(quad_mine, quad_got, ap.here, 0)
    first_x = [ax.shift(first, by) for by in ax.steps]
    second, first, first_y, first_x, quad, down_low = fence(
        second, first, first_y, first_x, quad, down_low
    )

    gathered = lax.all_gather(quad.reshape(4 * rows, 2 * hidden), SPREAD, axis=0, tiled=True)
    second = jnp.stack(second)
    second_x = [ax.shift(second, by) for by in ax.steps]
    second_y = ay.shift(second)
    second_x, second_y, second, first_y, block_input, cotangent, down_low = fence(
        second_x, second_y, second, first_y, block_input, cotangent, down_low
    )

    ffn_down = lax.all_gather(down_low, SPREAD, axis=0, tiled=True)
    first_yx = [ax.shift(first_y, by) for by in ax.steps]
    second_xy = [ay.shift(part) for part in second_x]
    x_core = ac.shift(block_input)
    dy_core = ac.shift(cotangent)
    x_all = jnp.concatenate([block_input, x_core], 0)
    starts = jnp.concatenate([seq_starts, starts_core], 0)
    position = lax.axis_index(("z", "y")) * tokens + jnp.arange(tokens + 2, dtype=jnp.int32)
    reached = starts[:, None, :] <= position[None, :, None]
    offset = position[None, :] - jnp.max(jnp.where(reached, starts[:, None, :], 0), axis=2)
    masks = [offset[:, :tokens] >= 1, offset[:, :tokens] >= 2]
    masks += [offset[:, 1 : 1 + tokens] >= 1, offset[:, 2:] >= 2]
    masks = jnp.stack(masks, 2).astype(F32).reshape(2 * tokens, 4)
    first_yx, second_xy, first, second, x_all, dy_core, masks, cotangent = fence(
        first_yx, second_xy, first, second, x_all, dy_core, masks, cotangent
    )

    dy_x = ap.shift(cotangent)
    pieces = [(0, 0, first_back, first), (0, 1, first_back, first_y)]
    pieces += [(0, 0, second_back, second), (0, 1, second_back, second_y)]
    for n, dx in enumerate(ax.steps):
        pieces += [(dx, 0, first_back, first_x[n]), (dx, 1, first_back, first_yx[n])]
        pieces += [(dx, 0, second_back, second_x[n]), (dx, 1, second_back, second_xy[n])]
    mix_in, tiny, mix_out = place_mix(pieces, here, ax, ay, az, wide_cols, width)
    tiny = tiny[:, :8].astype(F32)
    gain_mix, gain_ffn = tiny[:, 0], tiny[:, 1]
    taps = pick(tiny[:, 2:5].reshape(nx, 2, feats // nx, 3), core, 1).reshape(feats, 3)

    taps = jnp.concatenate([taps.T, jnp.zeros((5, feats), F32)], 0)

    last = x_all.reshape(2, tokens, width)[:, tokens - 2 :].reshape(4, width).astype(F32)
    scale = lax.rsqrt(jnp.mean(last * last, axis=1, keepdims=True) + EPS)
    last = times((last * scale * gain_mix[None, :]).astype(BF), mix_in)
    halo = passed_along((last[:, :feats] * last[:, 2 * feats :]).reshape(2, 2, feats), 1)
    normed_mix, projected, mixed, gated, mixer_keep, mixer_send = mixer_forward(
        x_all, gain_mix, mix_in, halo, masks, taps, mix_out, tokens // 2
    )
    mixer_send, mixer_keep, dy_x = fence(mixer_send, mixer_keep, dy_x)

    mixer_got = ac.shift(mixer_send)
    dy_far = [dy_x, ac.shift(dy_x)]
    own_inputs = block_input.astype(F32)
    h = own_inputs + (mixer_keep + mixer_got)
    scale_ffn = lax.rsqrt(jnp.mean(h * h, axis=1, keepdims=True) + EPS)
    normed_own = (h * scale_ffn * gain_ffn[None, :]).astype(BF)
    normed_core = ac.shift(normed_own)

    normed_core, normed_own, h, scale_ffn = fence(normed_core, normed_own, h, scale_ffn)
    normed_x = ap.shift(normed_own)
    gathered = gathered.reshape(far, 2 * nz, 4, rows, 2 * hidden)
    gate_up = gathered.transpose(0, 2, 1, 3, 4).reshape(width, 2 * hidden)
    near = [normed_own, normed_core]
    dy_near = [cotangent, dy_core]
    near_ev, near_s = ffn_forward(near, gate_up, tokens // 2)
    tile = 384 if hidden % 384 == 0 else hidden
    spec = pl.BlockSpec((tile, width), lambda i: (i, 0))
    near_down = weight_grad([near_s], dy_near, tile, spec, (hidden, width), F32)
    normed_x, near_ev, near_s, near_down = fence(normed_x, near_ev, near_s, near_down)

    far_tokens = [normed_x, ac.shift(normed_x)]
    far_ev, far_s = ffn_forward(far_tokens, gate_up, tokens // 2)

    grad_down = weight_grad([far_s], dy_far, tile, spec, (hidden, width), BF, [near_down])
    far_ev, far_s, grad_down = fence(far_ev, far_s, grad_down)

    down_own, down_send = cut(grad_down.reshape(far, nz, 2, -1, width), ay, 2)
    down_got = shifted(down_send, ay)
    far_dev, far_keep, far_send = ffn_back(dy_far, far_ev, ffn_down, gate_up, tokens // 2)
    far_got = [ac.shift(part) for part in far_send]
    far_fed, far_fed_send = row_halves(times, far_s, ffn_down, width, tokens // 2)
    down_own, down_got, far_dev, far_keep, far_got, far_fed, far_fed_send, near_ev, dy_near = fence(
        down_own, down_got, far_dev, far_keep, far_got, far_fed, far_fed_send, near_ev, dy_near
    )

    down_own, down_send = cut(summed(down_own, down_got).astype(BF), az, 1)
    down_got = shifted(down_send, az)
    normed_x_got = ap.shift((far_keep + jnp.concatenate(far_got, 0)).astype(BF))
    near_dev, near_keep, near_send = ffn_back(dy_near, near_ev, ffn_down, gate_up, tokens // 2)
    grad_gate_up = gate_up_grad(near + far_tokens, [near_dev, far_dev], far, nz, rows)
    normed_x_got, near_keep, near_send, grad_gate_up, down_own, down_got = fence(
        normed_x_got, near_keep, near_send, grad_gate_up, down_own, down_got
    )

    quad = lax.psum_scatter(grad_gate_up, SPREAD, scatter_dimension=0, tiled=True)
    near_got = [ac.shift(part) for part in near_send]
    near_got, near_keep, far_fed_send, far_fed = fence(near_got, near_keep, far_fed_send, far_fed)
    far_fed_got = [ac.shift(part) for part in far_fed_send]
    (grad_hidden, hidden_own), grad_gain_ffn = norm_back(
        [[near_keep], near_got, [normed_x_got]], h, gain_ffn, cotangent, (F32, BF), tokens // 2
    )
    hidden_got = ac.shift(hidden_own)

    hidden_got, hidden_own, grad_hidden, far_fed, far_fed_got = fence(
        hidden_got, hidden_own, grad_hidden, far_fed, far_fed_got
    )
    fed_x = ap.shift((far_fed + jnp.concatenate(far_fed_got, 0)).astype(BF))
    hidden_low = [hidden_own, hidden_got]
    opening = jnp.concatenate([part[:2] for part in hidden_low], 0)
    branch = projected.reshape(2, tokens, wide_cols)[:, :2, feats : 2 * feats].reshape(4, feats)
    opening = contract_cols(opening, mix_out) * branch
    later = passed_along(opening.reshape(2, 2, feats), -1)
    back_args = (hidden_low, mix_out, projected, mixed, later, masks, taps)
    if nx == 2 and rows % 16 == 0 and 2 * nz * rows % 128 == 0:
        grad_projected, tap_grads, blocks = mixer_grads(
            *back_args, normed_mix, gated, here, nz, rows, few, tokens // 2
        )
    else:
        grad_projected, tap_grads = mixer_back(*back_args, tokens // 2)
        back_in = contract_rows(normed_mix, grad_projected).astype(BF)
        back_out = contract_rows(gated, jnp.concatenate(hidden_low, 0)).astype(BF)
        back_out = back_out.reshape(nx, nz, 2, rows, 2, feats).transpose(0, 4, 1, 2, 3, 5)
        back_mix = jnp.concatenate(
            [back_in.reshape(nx, 2, nz, 2, rows, wide_cols), back_out], 5
        )
        blocks = []
        for dx in (0,) + ax.steps:
            ys = [pick(pick(back_mix, ax.at(dx), 0), ay.at(dy), 2) for dy in range(2)]
            blocks.append([y[:, part] for part in (slice(few), slice(few, None)) for y in ys])
    blocks, grad_projected, near_s, fed_x = fence(blocks, grad_projected, near_s, fed_x)

    first_hop = [ay.shift(block[1]) for block in blocks[1:]]
    first_got = [ay.shift(blocks[0][1])]
    second_hop = [ax.shift(block[3], by) for block, by in zip(blocks[1:], ax.steps, strict=True)]
    mix_keep, mix_send, grad_gain_mix = input_grad(grad_projected, mix_in, x_all, tokens // 2)
    near_fed, near_fed_send = row_halves(times, near_s, ffn_down, width, tokens // 2)
    tap_rows = tap_grads[:3].reshape(3, nx, 1, feats // nx)
    on_core = (jnp.arange(2) == core).astype(F32)[None, None, :, None]
    tap_rows = (tap_rows * on_core).reshape(3, width)
    own_gain = jnp.concatenate([grad_gain_mix[None], grad_gain_ffn[None]], 0)
    terms = jnp.concatenate([own_gain, tap_rows], 0)
    first_hop, first_got, second_hop, blocks, mix_keep, mix_send, near_fed_send, terms = fence(
        first_hop, first_got, second_hop, blocks, mix_keep, mix_send, near_fed_send, terms
    )

    second_got = [ay.shift(summed(blocks[0][3], second_hop).astype(BF))]
    for n, by in enumerate(ax.steps):
        block = blocks[n + 1]
        first_got.append(ax.shift(summed(block[0], [first_hop[n]]).astype(BF), by))
        second_got.append(ax.shift(block[2], by))
    mix_got = [ac.shift(part) for part in mix_send]
    near_fed_got = [ac.shift(part) for part in near_fed_send]
    (grad_inputs,), _ = norm_back(
        [[mix_keep], mix_got], block_input, gain_mix, grad_hidden, (BF,), tokens // 4
    )
    for axis in (ac, ax):
        terms = summed(terms, [axis.shift(terms, by) for by in axis.steps])
    terms = terms.reshape(5, 2 * nx, nz, 2 * rows).transpose(2, 0, 1, 3).reshape(nz, -1)
    high = lax.reduce_precision(terms, 8, 7)
    terms = jnp.concatenate([high, terms - high], 1).astype(BF)
    extra = -(-terms.shape[1] // (2 * rows * 128)) * 128
    terms = jnp.pad(terms, ((0, 0), (0, 2 * rows * extra - terms.shape[1])))
    terms = terms.reshape(nz, 2, rows, extra).transpose(1, 0, 2, 3)
    first_got, second_got, blocks, grad_inputs, terms, near_fed_got = fence(
        first_got, second_got, blocks, grad_inputs, terms, near_fed_got
    )

    own_z = jnp.concatenate(
        [summed(blocks[0][0], first_got).astype(BF), summed(blocks[0][2], second_got).astype(BF)], 1
    )
    own_z = jnp.concatenate([own_z, terms], 3)
    mix_own, mix_send = cut(own_z, az, 1)
    mix_parts = shifted(mix_send, az)
    quad = quad.reshape(4, rows, 2 * hidden)
    quad = [pick(quad, (2 * ap.here + core) ^ step, 0) for step in range(4)]
    quad[1:] = [
        lax.ppermute(part, ("x", "core"), [(i, i ^ step) for i in range(4)])
        for step, part in enumerate(quad[1:], 1)
    ]
    mix_parts, mix_own, quad = fence(mix_parts, mix_own, quad)
    mix_sum = summed(mix_own, mix_parts)
    terms = mix_sum[..., wide_cols + feats :].reshape(-1)
    count = 5 * 4 * nx * rows
    terms = (terms[:count] + terms[count : 2 * count]).reshape(5, 4 * nx * rows)

    terms = terms + ay.shift(terms)
    at = ((ax.here * 2 + core) * 2 + ay.here) * rows
    sides = [ordered(quad[n], quad[n + 1], core, 0) for n in (0, 2)]
    part_down = summed(down_own, down_got)
    if far > 1:
        part_down = lax.psum_scatter(part_down, "far", scatter_dimension=0, tiled=True)
    part_down = part_down[0]
    block_output = (h + (near_fed + jnp.concatenate(near_fed_got, 0) + fed_x.astype(F32))).astype(BF)
    part_out = mix_sum[..., wide_cols : wide_cols + feats].transpose(1, 0, 2).reshape(rows, width)
    in_mine, in_send = cut(mix_sum[..., :wide_cols], ac, 0)
    in_got = shifted(in_send, ac)[0]
    blocks = (rows, 3 * nx, feats // nx)
    part_in = ordered(in_mine.reshape(blocks), in_got.reshape(blocks), core, 2)
    quads = ordered(*sides, ap.here, 0).astype(F32)

    def join_hidden(sets):
        sets = sets.reshape(2, 2, rows, far, hidden // far)
        return jnp.transpose(sets, (2, 3, 0, 1, 4)).reshape(rows, 4 * hidden)

    part_gate, part_rise = join_hidden(quads[..., :hidden]), join_hidden(quads[..., hidden:])
    own_terms = lax.dynamic_slice_in_dim(terms, at, rows, 1)
    return (
        block_output,
        grad_inputs,
        part_in.reshape(rows, 3 * width),
        part_out,
        part_gate,
        part_rise,
        part_down,
        own_terms[0],
        own_terms[1],
        own_terms[2:].T,
    )


def solution(mesh):
    nd, nf = mesh.shape["dp"], mesh.shape["fsdp"]
    rows, line = P(AXES, None), P(AXES)
    return jax.shard_map(
        per_device,
        mesh=Mesh(mesh.devices.reshape(nd // 4, 2, 2, nf // 2, 2), AXES),
        in_specs=(rows,) * 6 + (line, line, rows, P(AXES[:3], None), rows),
        out_specs=(rows,) * 7 + (line, line, rows),
        check_vma=False,
    )
```

```python
import functools
import itertools
import math

import jax
import jax.numpy as jnp
from jax import lax
from jax.experimental import pallas as pl
from jax.experimental.pallas import tpu as pltpu
from jax.sharding import Mesh
from jax.sharding import PartitionSpec as P

EPS = 1e-05
AXES = ("far", "x", "core", "z", "y")
SPREAD = ("far", "z", "y")
BF = jnp.bfloat16
F32 = jnp.float32


class Axis:
    def __init__(self, name):
        self.name, self.size = name, lax.axis_size(name)
        self.here = lax.axis_index(name)
        near = sorted(range(1, self.size), key=lambda by: (min(by, self.size - by), by))
        self.steps = tuple(near)

    def shift(self, value, by=1):
        return lax.ppermute(value, self.name, [(i, (i + by) % self.size) for i in range(self.size)])

    def at(self, by):
        return lax.rem(self.here + by, self.size)


def passed_along(shard, by):
    peers = lax.axis_size(("z", "y"))
    pairs = [(i, i + by) for i in range(peers) if 0 <= i + by < peers]
    return lax.ppermute(shard, ("z", "y"), pairs)


def fence(*values):
    return lax.optimization_barrier(values)


def contract_rows(left, right):
    return lax.dot_general(
        left, right, (((0,), (0,)), ((), ())), preferred_element_type=F32
    )


def contract_cols(left, right):
    return lax.dot_general(
        left, right, (((1,), (1,)), ((), ())), preferred_element_type=F32
    )


def times(left, right):
    return jnp.dot(left, right, preferred_element_type=F32)


def pick(value, at, dim):
    return lax.dynamic_index_in_dim(value, at, dim, keepdims=False)


def ordered(mine, other, here, dim):
    low = jnp.where(here == 0, mine, other)
    high = jnp.where(here == 0, other, mine)
    return jnp.stack([low, high], dim)


def cut(value, axis, dim):
    return pick(value, axis.here, dim), [pick(value, axis.at(by), dim) for by in axis.steps]


def shifted(parts, axis):
    return [axis.shift(part, by) for part, by in zip(parts, axis.steps, strict=True)]


def summed(own, others):
    total = own.astype(F32)
    for other in others:
        total = total + other.astype(F32)
    return total


def place_body(moves, here_ref, *refs):
    sems = refs[-1]
    copies = []
    for i, (source, target) in enumerate(moves(here_ref, refs[:-1])):
        copy = pltpu.make_async_copy(source, target, sems.at[i])
        copy.start()
        copies.append(copy)
    for copy in copies:
        copy.wait()


def out_array(shape, kind):
    return pltpu.HBM(shape, kind) if math.prod(shape) >= 2**18 else jax.ShapeDtypeStruct(shape, kind)


def pinned(*arrays):
    return [
        pltpu.with_memory_space_constraint(a, pltpu.HBM) if a.size >= 2**18 else a for a in arrays
    ]


def kept(array):
    return pltpu.with_memory_space_constraint(array, pltpu.VMEM)


def place(moves, count, here, sources, shapes):
    return pl.pallas_call(
        functools.partial(place_body, moves),
        out_shape=[pltpu.VMEM(shape, BF) for shape in shapes],
        in_specs=[pl.BlockSpec(memory_space=pltpu.SMEM)]
        + [pl.BlockSpec(memory_space=pl.ANY)] * len(sources),
        out_specs=[pl.BlockSpec(memory_space=pltpu.VMEM)] * len(shapes),
        scratch_shapes=[pltpu.SemaphoreType.DMA((count,))],
        compiler_params=params(20),
        cost_estimate=pl.CostEstimate(flops=0, bytes_accessed=2**20, transcendentals=0),
    )(here, *pinned(*sources))


def back(at, by, size):
    return lax.rem(at + size - by, size)


def place_mix(pieces, here, ax, ay, az, columns, width):
    nx, ny, nz = ax.size, ay.size, az.size
    rows, half = pieces[0][3].shape[-2], width // 2

    def moves(at, refs):
        wide, small, narrow = refs[-3:]
        for (dx, dy, backs, _), source in zip(pieces, refs[:-3], strict=True):
            x, y = back(at[0], dx, nx), back(at[1], dy, ny)
            for n, dz in enumerate(backs):
                z = back(at[2], dz, nz)
                block = source.at[n]
                yield block.at[:, :, pl.ds(0, columns)], wide.at[x, :, z, y]
                yield block.at[:, :, pl.ds(columns, 128)], small.at[x, :, z, y]
                for k in range(2):
                    yield (
                        block.at[k, :, pl.ds(columns + 128, half)],
                        narrow.at[x, z, y, :, pl.ds(k * half, half)],
                    )

    lead = (nx, 2, nz, ny, rows)
    shapes = [lead + (columns,), lead + (128,), (nx, nz, ny, rows, width)]
    arrays = [piece[3] for piece in pieces]
    wide, small, narrow = place(moves, 4 * nx * ny * nz, here, arrays, shapes)
    return wide.reshape(-1, columns), small.reshape(-1, 128), narrow.reshape(-1, width)


def cost():
    return pl.CostEstimate(flops=0, bytes_accessed=2**16, transcendentals=0)


def params(mib):
    return pltpu.CompilerParams(vmem_limit_bytes=mib * 1024 * 1024)


def whole(array):
    return pl.BlockSpec(
        array.shape, lambda i: (0,) * array.ndim, pipeline_mode=pl.Buffered(1)
    )


def tiles(rows, columns):
    return pl.BlockSpec((rows, columns), lambda i: (i, 0))


def chunks(columns):
    step = 384 if columns % 384 == 0 else 128 if columns % 128 == 0 else columns
    return [(a, step) for a in range(0, columns, step)]


def logistic(v):
    return 0.5 * jnp.tanh(0.5 * v) + 0.5


def piece_specs(pieces, tile):
    specs = []
    for p, piece in enumerate(pieces):
        first, last = p * piece.shape[0] // tile, (p + 1) * piece.shape[0] // tile - 1

        def at(i, first=first, last=last):
            return jnp.clip(i - first, 0, last - first), 0

        specs.append(pl.BlockSpec((tile, piece.shape[1]), at))
    return specs


def piece_tile(refs):
    steps = pl.num_programs(0) // len(refs)
    value = refs[0][...]
    for p, ref in enumerate(refs[1:], 1):
        value = jnp.where(pl.program_id(0) >= p * steps, ref[...], value)
    return value


def forward_body(count, *refs):
    w_ref, ev_ref, s_ref = refs[count:]
    hidden = s_ref.shape[1]
    x = piece_tile(refs[:count])
    for a, n in chunks(hidden):
        gate = times(x, w_ref[:, a : a + n])
        rise = times(x, w_ref[:, hidden + a : hidden + a + n])
        ev_ref[:, a : a + n] = gate.astype(BF)
        ev_ref[:, hidden + a : hidden + a + n] = rise.astype(BF)
        s_ref[:, a : a + n] = (gate * logistic(gate) * rise).astype(BF)


def ffn_forward(pieces, w, tile):
    count, both = sum(piece.shape[0] for piece in pieces), w.shape[1]
    return pl.pallas_call(
        functools.partial(forward_body, len(pieces)),
        grid=(count // tile,),
        in_specs=piece_specs(pieces, tile) + [whole(w)],
        out_specs=[tiles(tile, both), tiles(tile, both // 2)],
        out_shape=[out_array((count, both), BF), out_array((count, both // 2), BF)],
        compiler_params=params(24),
        cost_estimate=cost(),
    )(*pinned(*pieces, w))


def back_body(count, half, *refs):
    ev_ref, down_ref, w_ref, dev_ref, keep_ref, *sends = refs[count:]
    hidden = down_ref.shape[0]
    dy = piece_tile(refs[:count])
    for a, n in chunks(hidden):
        back = contract_cols(dy, down_ref[a : a + n, :])
        gate = ev_ref[:, a : a + n].astype(F32)
        rise = ev_ref[:, hidden + a : hidden + a + n].astype(F32)
        sigma = logistic(gate)
        back = back * sigma
        dev_ref[:, a : a + n] = (back * rise * (1.0 + gate * (1.0 - sigma))).astype(BF)
        dev_ref[:, hidden + a : hidden + a + n] = (back * gate).astype(BF)
    split_pieces(half, contract_cols(dev_ref[...], w_ref[...]), keep_ref, sends)


def split_rows(half, value, keep_ref, send_ref):
    @pl.when(pl.program_id(0) < half)
    def _():
        keep_ref[...] = value

    @pl.when(pl.program_id(0) >= half)
    def _():
        send_ref[...] = value.astype(send_ref.dtype)


def split_specs(tile, columns, half):
    return [
        pl.BlockSpec((tile, columns), lambda i: (jnp.minimum(i, half - 1), 0)),
        pl.BlockSpec((tile, columns), lambda i: (jnp.maximum(i - half, 0), 0)),
    ]


def split_pieces(half, value, keep_ref, sends):
    cuts = len(sends) // half
    size = value.shape[0] // cuts

    @pl.when(pl.program_id(0) < half)
    def _():
        keep_ref[...] = value

    for n, ref in enumerate(sends):

        @pl.when(pl.program_id(0) == half + n // cuts)
        def _(n=n, ref=ref):
            at = n % cuts * size
            ref[...] = value[at : at + size].astype(ref.dtype)


def piece_outputs(count, width, tile, cuts):
    half, size = count // (2 * tile), tile // cuts
    specs = split_specs(tile, width, half)[:1]
    specs += [pl.BlockSpec((size, width), lambda i: (0, 0))] * (half * cuts)
    shapes = [out_array((count // 2, width), F32)]
    return specs, shapes + [out_array((size, width), BF)] * (half * cuts)


def ffn_back(pieces, ev, down, w, tile):
    count, both = ev.shape
    width, half = down.shape[1], count // (2 * tile)
    specs, shapes = piece_outputs(count, width, tile, 1)
    out = pl.pallas_call(
        functools.partial(back_body, len(pieces), half),
        grid=(2 * half,),
        in_specs=piece_specs(pieces, tile) + [tiles(tile, both), whole(down), whole(w)],
        out_specs=[tiles(tile, both)] + specs,
        out_shape=[pltpu.VMEM((count, both), BF)] + shapes,
        compiler_params=params(32),
        cost_estimate=cost(),
    )(*pinned(*pieces, ev, down, w))
    return out[0], out[1], out[2:]


def rows_body(function, half, left_ref, weight_ref, keep_ref, *sends):
    split_pieces(half, function(left_ref[...], weight_ref[...]), keep_ref, sends)


def row_halves(function, left, weight, width, tile):
    count = left.shape[0]
    half = count // (2 * tile)
    specs, shapes = piece_outputs(count, width, tile, 2)
    out = pl.pallas_call(
        functools.partial(rows_body, function, half),
        grid=(2 * half,),
        in_specs=[tiles(tile, left.shape[1]), whole(weight)],
        out_specs=specs,
        out_shape=shapes,
        compiler_params=params(20),
        cost_estimate=cost(),
    )(*pinned(left, weight))
    return out[0], out[1:]


def input_grad_body(half, dp_ref, win_ref, x_ref, keep_ref, *refs):
    sends, gain_ref = refs[:-1], refs[-1]
    value = contract_cols(dp_ref[...], win_ref[...])
    split_pieces(half, value, keep_ref, sends)
    x = x_ref[...].astype(F32)
    scale = lax.rsqrt(jnp.mean(x * x, axis=1, keepdims=True) + EPS)

    @pl.when(pl.program_id(0) == 0)
    def _():
        gain_ref[...] = jnp.zeros_like(gain_ref)

    gain_ref[...] += jnp.sum(value * (x * scale), axis=0, keepdims=True)


def input_grad(dp, win, x, tile):
    count, width = x.shape
    half = count // (2 * tile)
    specs, shapes = piece_outputs(count, width, tile, 2)
    out = pl.pallas_call(
        functools.partial(input_grad_body, half),
        grid=(2 * half,),
        in_specs=[tiles(tile, dp.shape[1]), whole(win), tiles(tile, width)],
        out_specs=specs + [pl.BlockSpec((1, width), lambda i: (0, 0))],
        out_shape=shapes + [jax.ShapeDtypeStruct((1, width), F32)],
        compiler_params=params(24),
        cost_estimate=cost(),
    )(*pinned(dp, win, x))
    return out[0], out[1:-1], out[-1][0]


def grad_body(lefts, rights, *refs):
    rest = refs[len(lefts) + len(rights) :]
    total = None
    for i, (first, end) in enumerate(lefts):
        for j, (start, stop) in enumerate(rights):
            low, high = max(first, start), min(end, stop)
            if low < high:
                left = refs[i][low - first : high - first, :]
                right = refs[len(lefts) + j][low - start : high - start, :]
                term = contract_rows(left, right)
                total = term if total is None else total + term
    for ref in rest[:-1]:
        total = total + ref[...]
    rest[-1][...] = total.astype(rest[-1].dtype).reshape(rest[-1].shape)


def token_spans(pieces):
    ends = list(itertools.accumulate(piece.shape[0] for piece in pieces))
    return list(zip([0] + ends[:-1], ends, strict=True))


def weight_grad(lefts, rights, tile, out_spec, shape, kind=BF, extra=(), stay=False):
    rows = lefts[0].shape[1]
    return pl.pallas_call(
        functools.partial(grad_body, token_spans(lefts), token_spans(rights)),
        grid=(rows // tile,),
        in_specs=[pl.BlockSpec((left.shape[0], tile), lambda i: (0, i)) for left in lefts]
        + [whole(right) for right in rights]
        + [out_spec] * len(extra),
        out_specs=out_spec,
        out_shape=out_array(shape, kind),
        compiler_params=params(34),
        cost_estimate=cost(),
    )(*pinned(*lefts), *(kept(right) if stay else pinned(right)[0] for right in rights), *pinned(*extra))


def gate_up_grad(lefts, rights, far, nz, rows):
    columns, width = rights[0].shape[1], lefts[0].shape[1]
    tile = 2 * nz * rows
    if tile % 128 == 0 and rows % 16 == 0:
        block = (1, 2 * nz, 1, rows, columns)
        spec = pl.BlockSpec(block, lambda i: (i // 4, 0, i % 4, 0, 0))
        out = weight_grad(lefts, rights, tile, spec, (far, 2 * nz, 4, rows, columns), stay=True)
    else:
        out = weight_grad(lefts, rights, 256, tiles(256, columns), (width, columns), stay=True)
        out = out.reshape(far, 4, 2 * nz, rows, columns).transpose(0, 2, 1, 3, 4)
    return out.reshape(width, columns)


def mixer_body(
    per_group, x_ref, gain_ref, win_ref, halo_ref, masks_ref, taps_ref, wout_ref, *refs
):
    normed_ref, projected_ref, mixed_ref, gated_ref, keep_ref, send_ref, rows, carry = refs
    count, feats = mixed_ref.shape
    x = x_ref[...].astype(F32)
    scale = lax.rsqrt(jnp.mean(x * x, axis=1, keepdims=True) + EPS)
    normed = (x * scale * gain_ref[...]).astype(BF)
    normed_ref[...] = normed
    projected = times(normed, win_ref[...])
    projected_ref[...] = projected
    product = projected[:, :feats] * projected[:, 2 * feats :]
    opens = lax.rem(pl.program_id(0), per_group) == 0
    rows[6:8, :] = jnp.where(opens, halo_ref[0], carry[...])
    rows[8 : 8 + count, :] = product
    mixed = taps_ref[2:3, :] * product
    mixed = mixed + masks_ref[:, 0:1] * (taps_ref[1:2, :] * rows[7 : 7 + count, :])
    mixed = mixed + masks_ref[:, 1:2] * (taps_ref[0:1, :] * rows[6 : 6 + count, :])
    carry[...] = product[count - 2 :]
    mixed_ref[...] = mixed
    gated = (projected[:, feats : 2 * feats] * mixed).astype(BF)
    gated_ref[...] = gated
    half = pl.num_programs(0) // 2
    split_rows(half, times(gated, wout_ref[...]), keep_ref, send_ref)


def mixer_forward(x, gain, win, halo, masks, taps, wout, tile):
    count, width = x.shape
    wide, feats = win.shape[1], wout.shape[0]
    per_group = count // (2 * tile)
    row = pl.BlockSpec((1, width), lambda i: (0, 0))
    return pl.pallas_call(
        functools.partial(mixer_body, per_group),
        grid=(2 * per_group,),
        in_specs=[
            tiles(tile, width),
            row,
            whole(win),
            pl.BlockSpec((1, 2, feats), lambda i: (i // per_group, 0, 0)),
            tiles(tile, masks.shape[1]),
            whole(taps),
            whole(wout),
        ],
        out_specs=[tiles(tile, width), tiles(tile, wide), tiles(tile, feats), tiles(tile, feats)]
        + split_specs(tile, width, per_group),
        out_shape=[
            out_array((count, width), BF),
            out_array((count, wide), F32),
            out_array((count, feats), F32),
            out_array((count, feats), BF),
        ]
        + [out_array((count // 2, width), kind) for kind in (F32, BF)],
        scratch_shapes=[pltpu.VMEM((tile + 8, feats), F32), pltpu.VMEM((2, feats), F32)],
        compiler_params=params(28),
        cost_estimate=cost(),
    )(*pinned(x, gain[None]), kept(win), *pinned(halo, masks, taps), kept(wout))


def mixer_back_body(
    per_group, dh_ref, dh2_ref, wout_ref, projected_ref, mixed_ref, halo_ref, masks_ref, *refs
):
    taps_ref, *refs = refs
    out_ref, grad_ref, rows, carry = refs
    count, feats = mixed_ref.shape
    projected = projected_ref[...]
    dh = jnp.where(pl.program_id(0) < per_group, dh_ref[...], dh2_ref[...])
    back = contract_cols(dh, wout_ref[...])
    grad_c = back * mixed_ref[...]
    grad_mixed = back * projected[:, feats : 2 * feats]
    closes = lax.rem(pl.program_id(0), per_group) == 0
    rows[0:count, :] = grad_mixed
    rows[count : count + 2, :] = jnp.where(closes, halo_ref[0], carry[...])
    carry[...] = grad_mixed[:2]
    ahead = (
        grad_mixed,
        masks_ref[:, 2:3] * rows[1 : 1 + count, :],
        masks_ref[:, 3:4] * rows[2 : 2 + count, :],
    )
    grad_product = sum(taps_ref[2 - lag : 3 - lag, :] * ahead[lag] for lag in range(3))
    b_branch, x_branch = projected[:, :feats], projected[:, 2 * feats :]
    out_ref[:, :feats] = (grad_product * x_branch).astype(BF)
    out_ref[:, feats : 2 * feats] = grad_c.astype(BF)
    out_ref[:, 2 * feats :] = (grad_product * b_branch).astype(BF)

    @pl.when(pl.program_id(0) == 0)
    def _():
        grad_ref[...] = jnp.zeros_like(grad_ref)

    product = b_branch * x_branch
    for lag in range(3):
        grad_ref[2 - lag : 3 - lag, :] += jnp.sum(product * ahead[lag], axis=0, keepdims=True)


def mixer_back(dh, wout, projected, mixed, halo, masks, taps, tile):
    count, wide = projected.shape
    width, feats = dh[0].shape[1], wout.shape[0]
    per_group = count // (2 * tile)

    def at(i):
        return (i // per_group) * per_group + per_group - 1 - lax.rem(i, per_group)

    def turned(columns):
        return pl.BlockSpec((tile, columns), lambda i: (at(i), 0))

    return pl.pallas_call(
        functools.partial(mixer_back_body, per_group),
        grid=(2 * per_group,),
        in_specs=[
            pl.BlockSpec((tile, width), lambda i: (jnp.maximum(per_group - 1 - i, 0), 0)),
            pl.BlockSpec(
                (tile, width), lambda i: (jnp.minimum(2 * per_group - 1 - i, per_group - 1), 0)
            ),
            whole(wout),
            turned(wide),
            turned(feats),
            pl.BlockSpec((1, 2, feats), lambda i: (i // per_group, 0, 0)),
            turned(masks.shape[1]),
            whole(taps),
        ],
        out_specs=[turned(wide), pl.BlockSpec((8, feats), lambda i: (0, 0))],
        out_shape=[
            out_array((count, wide), BF),
            out_array((8, feats), F32),
        ],
        scratch_shapes=[pltpu.VMEM((tile + 8, feats), F32), pltpu.VMEM((2, feats), F32)],
        compiler_params=params(24),
        cost_estimate=cost(),
    )(*pinned(*dh, wout, projected, mixed, halo, masks, taps))


def mixer_grads_body(per_group, lower, here_ref, normed_ref, gated_ref, *refs):
    ins, out_ref, grad_ref = refs[:8], refs[8], refs[9]
    blocks, (rows, carry, in_sum, out_sum) = refs[10:18], refs[18:]
    mixer_back_body(per_group, *ins, out_ref, grad_ref, rows, carry)
    width, wide = in_sum.shape
    tile = width // 4

    @pl.when(pl.program_id(0) == 0)
    def _():
        in_sum[...] = jnp.zeros_like(in_sum)
        out_sum[...] = jnp.zeros_like(out_sum)

    grad = out_ref[...]
    dh = jnp.where(pl.program_id(0) < per_group, ins[0][...], ins[1][...])
    for q in range(4):
        part = slice(q * tile, (q + 1) * tile)
        in_sum[part, :] += contract_rows(normed_ref[:, part], grad)
    for x in range(2):
        part = slice(x * tile, (x + 1) * tile)
        out_sum[part, :] += contract_rows(gated_ref[:, part], dh)

    @pl.when(pl.program_id(0) == pl.num_programs(0) - 1)
    def _():
        own_y = here_ref[1] == 0
        half = width // 2
        for dx in range(2):
            x = lax.rem(here_ref[0] + dx, 2)
            for k in range(2):
                q = pl.multiple_of((2 * x + k) * tile, tile)
                parts = (
                    (in_sum[pl.ds(q, tile), :], slice(0, wide)),
                    (
                        out_sum[pl.ds(pl.multiple_of(x * tile, tile), tile), k * half : (k + 1) * half],
                        slice(wide, wide + half),
                    ),
                )
                for value, where in parts:
                    value = value.astype(BF).reshape(-1, 2, blocks[0].shape[2], value.shape[1])
                    low, high = value[:, 0], value[:, 1]
                    own, other = jnp.where(own_y, low, high), jnp.where(own_y, high, low)
                    cuts = (own[:lower], other[:lower], own[lower:], other[lower:])
                    for cut_, target in zip(cuts, blocks[4 * dx : 4 * dx + 4], strict=True):
                        target[k, :, :, where] = cut_


def mixer_grads(dh, wout, projected, mixed, halo, masks, taps, normed, gated, here, nz, rows, lower, tile):
    count, wide = projected.shape
    width, feats = dh[0].shape[1], wout.shape[0]
    per_group = count // (2 * tile)

    def at(i):
        return (i // per_group) * per_group + per_group - 1 - lax.rem(i, per_group)

    def turned(columns):
        return pl.BlockSpec((tile, columns), lambda i: (at(i), 0))

    def fixed(shape):
        return pl.BlockSpec(shape, lambda i: (0,) * len(shape))

    columns = wide + width // 2
    shapes = [(2, n, rows, columns) for n in (lower, lower, nz - lower, nz - lower)] * 2
    out = pl.pallas_call(
        functools.partial(mixer_grads_body, per_group, lower),
        grid=(2 * per_group,),
        in_specs=[
            pl.BlockSpec(memory_space=pltpu.SMEM),
            turned(width),
            turned(feats),
            pl.BlockSpec((tile, width), lambda i: (jnp.maximum(per_group - 1 - i, 0), 0)),
            pl.BlockSpec(
                (tile, width), lambda i: (jnp.minimum(2 * per_group - 1 - i, per_group - 1), 0)
            ),
            whole(wout),
            turned(wide),
            turned(feats),
            pl.BlockSpec((1, 2, feats), lambda i: (i // per_group, 0, 0)),
            turned(masks.shape[1]),
            whole(taps),
        ],
        out_specs=[turned(wide), fixed((8, feats))] + [fixed(shape) for shape in shapes],
        out_shape=[out_array((count, wide), BF), out_array((8, feats), F32)]
        + [out_array(shape, BF) for shape in shapes],
        scratch_shapes=[
            pltpu.VMEM((tile + 8, feats), F32),
            pltpu.VMEM((2, feats), F32),
            pltpu.VMEM((width, wide), F32),
            pltpu.VMEM((feats, width), F32),
        ],
        compiler_params=params(46),
        cost_estimate=cost(),
    )(here, *pinned(normed, gated, *dh, wout, projected, mixed, halo, masks, taps))
    return out[0], out[1], [out[2:6], out[6:]]


def norm_back_body(counts, *refs):
    grad, refs = 0.0, list(refs)
    for count in counts:
        grad = grad + piece_tile(refs[:count]).astype(F32)
        refs = refs[count:]
    x_ref, gain_ref, up_ref, *outs = refs
    x = x_ref[...].astype(F32)
    scale = lax.rsqrt(jnp.mean(x * x, axis=1, keepdims=True) + EPS)
    scaled = x * scale
    weighted = grad * gain_ref[...]
    mean = jnp.mean(weighted * scaled, axis=1, keepdims=True)
    out = up_ref[...].astype(F32) + scale * (weighted - scaled * mean)
    for ref in outs[:-1]:
        ref[...] = out.astype(ref.dtype)

    @pl.when(pl.program_id(0) == 0)
    def _():
        outs[-1][...] = jnp.zeros_like(outs[-1])

    outs[-1][...] += jnp.sum(grad * scaled, axis=0, keepdims=True)


def norm_back(grads, x, gain, upstream, kinds, tile):
    count, width = x.shape
    line = pl.BlockSpec((1, width), lambda i: (0, 0))
    specs = [spec for pieces in grads for spec in piece_specs(pieces, tile)]
    out = pl.pallas_call(
        functools.partial(norm_back_body, [len(pieces) for pieces in grads]),
        grid=(count // tile,),
        in_specs=specs + [tiles(tile, width), line, tiles(tile, width)],
        out_specs=[tiles(tile, width)] * len(kinds) + [line],
        out_shape=[out_array((count, width), kind) for kind in kinds]
        + [jax.ShapeDtypeStruct((1, width), F32)],
        compiler_params=params(16),
        cost_estimate=cost(),
    )(*pinned(*[piece for pieces in grads for piece in pieces], x, gain[None], upstream))
    return out[:-1], out[-1][0]


def join_body(here_ref, *refs):
    sets, outs = refs[:4], refs[4:]
    own, hidden = here_ref[3], outs[0].shape[1] // 4
    for half, out_ref in enumerate(outs):
        for block in range(4):
            value = sets[block][:, half * hidden : (half + 1) * hidden]
            for at in range(1, 4):
                other = sets[block ^ at][:, half * hidden : (half + 1) * hidden]
                value = jnp.where(own == at, other, value)
            out_ref[:, block * hidden : (block + 1) * hidden] = value.astype(F32)


def join_columns(sets, here):
    rows, both = sets[0].shape
    return pl.pallas_call(
        join_body,
        in_specs=[pl.BlockSpec(memory_space=pltpu.SMEM)]
        + [pl.BlockSpec(memory_space=pltpu.VMEM)] * 4,
        out_specs=[pl.BlockSpec(memory_space=pltpu.VMEM)] * 2,
        out_shape=[jax.ShapeDtypeStruct((rows, 2 * both), F32)] * 2,
        compiler_params=params(12),
        cost_estimate=cost(),
    )(here, *sets)


def per_device(
    block_input,
    in_weight,
    out_weight,
    gate_weight,
    up_weight,
    down_weight,
    norm_gain,
    ffn_gain,
    conv_weight,
    seq_starts,
    cotangent,
):
    ax, ac, az, ay = Axis(("far", "x")), Axis("core"), Axis("z"), Axis("y")
    ap = Axis("x")
    nx, nz, far = ax.size, az.size, lax.axis_size("far")
    core = ac.here
    here = jnp.stack([ax.here, ay.here, az.here, 2 * ap.here + core]).astype(jnp.int32)
    tokens, width = block_input.shape
    rows = in_weight.shape[0]
    hidden = gate_weight.shape[1] // 4
    feats = width // 2
    wide_cols = 3 * feats
    lower = nz // 2
    few = max(1, nz // 4)
    z_back = (0,) + az.steps
    first_back, second_back = z_back[:lower], z_back[lower:]

    small = jnp.concatenate(
        [norm_gain[:, None], ffn_gain[:, None], conv_weight, jnp.zeros((rows, 123), F32)], 1
    ).astype(BF)
    in_sets = in_weight.astype(BF).reshape(rows, 3 * nx, 2, feats // nx)

    def in_part(which):
        return jnp.concatenate([pick(in_sets, which, 2).reshape(rows, wide_cols), small], 1)

    in_mine, in_got = in_part(core), ac.shift(in_part(1 - core))
    starts_core = ac.shift(seq_starts)

    def split_hidden(weight):
        cut = weight.astype(BF).reshape(rows, far, 2, 2, hidden // far)
        return jnp.transpose(cut, (2, 3, 0, 1, 4)).reshape(2, 2, rows, hidden)

    in_mine, in_got, gate_weight, up_weight = fence(in_mine, in_got, gate_weight, up_weight)
    out_low = out_weight.astype(BF).reshape(rows, 2, feats).transpose(1, 0, 2)
    mix = jnp.concatenate([ordered(in_mine, in_got, core, 0), out_low], 2)
    mix_z = {by: az.shift(mix, by) for by in first_back[1:]}
    gate_up = jnp.concatenate([split_hidden(gate_weight), split_hidden(up_weight)], 3)
    pair_mine = pick(gate_up, core, 1)
    pair_send = jnp.split(pick(gate_up, 1 - core, 1), 2, 2)
    pair_got = jnp.concatenate([ac.shift(part) for part in pair_send], 2)

    pair_mine, pair_got, mix, mix_z, cotangent, down_low = fence(
        pair_mine, pair_got, mix, mix_z, cotangent, down_weight.astype(BF)
    )
    first = jnp.stack([mix] + [mix_z[by] for by in first_back[1:]])
    first_y = ay.shift(first)
    second = [az.shift(mix, by) for by in second_back]
    pair = ordered(pair_mine, pair_got, core, 1)
    quad_mine, quad_got = pick(pair, ap.here, 0), ap.shift(pick(pair, 1 - ap.here, 0))
    quad = ordered(quad_mine, quad_got, ap.here, 0)
    first_x = [ax.shift(first, by) for by in ax.steps]
    second, first, first_y, first_x, quad, down_low = fence(
        second, first, first_y, first_x, quad, down_low
    )

    gathered = lax.all_gather(quad.reshape(4 * rows, 2 * hidden), SPREAD, axis=0, tiled=True)
    second = jnp.stack(second)
    second_x = [ax.shift(second, by) for by in ax.steps]
    second_y = ay.shift(second)
    second_x, second_y, second, first_y, block_input, cotangent, down_low = fence(
        second_x, second_y, second, first_y, block_input, cotangent, down_low
    )

    ffn_down = lax.all_gather(down_low, SPREAD, axis=0, tiled=True)
    first_yx = [ax.shift(first_y, by) for by in ax.steps]
    second_xy = [ay.shift(part) for part in second_x]
    x_core = ac.shift(block_input)
    dy_core = ac.shift(cotangent)
    x_all = jnp.concatenate([block_input, x_core], 0)
    starts = jnp.concatenate([seq_starts, starts_core], 0)
    position = lax.axis_index(("z", "y")) * tokens + jnp.arange(tokens + 2, dtype=jnp.int32)
    reached = starts[:, None, :] <= position[None, :, None]
    offset = position[None, :] - jnp.max(jnp.where(reached, starts[:, None, :], 0), axis=2)
    masks = [offset[:, :tokens] >= 1, offset[:, :tokens] >= 2]
    masks += [offset[:, 1 : 1 + tokens] >= 1, offset[:, 2:] >= 2]
    masks = jnp.stack(masks, 2).astype(F32).reshape(2 * tokens, 4)
    first_yx, second_xy, first, second, x_all, dy_core, masks, cotangent = fence(
        first_yx, second_xy, first, second, x_all, dy_core, masks, cotangent
    )

    dy_x = ap.shift(cotangent)
    pieces = [(0, 0, first_back, first), (0, 1, first_back, first_y)]
    pieces += [(0, 0, second_back, second), (0, 1, second_back, second_y)]
    for n, dx in enumerate(ax.steps):
        pieces += [(dx, 0, first_back, first_x[n]), (dx, 1, first_back, first_yx[n])]
        pieces += [(dx, 0, second_back, second_x[n]), (dx, 1, second_back, second_xy[n])]
    mix_in, tiny, mix_out = place_mix(pieces, here, ax, ay, az, wide_cols, width)
    tiny = tiny[:, :8].astype(F32)
    gain_mix, gain_ffn = tiny[:, 0], tiny[:, 1]
    taps = pick(tiny[:, 2:5].reshape(nx, 2, feats // nx, 3), core, 1).reshape(feats, 3)

    taps = jnp.concatenate([taps.T, jnp.zeros((5, feats), F32)], 0)

    last = x_all.reshape(2, tokens, width)[:, tokens - 2 :].reshape(4, width).astype(F32)
    scale = lax.rsqrt(jnp.mean(last * last, axis=1, keepdims=True) + EPS)
    last = times((last * scale * gain_mix[None, :]).astype(BF), mix_in)
    halo = passed_along((last[:, :feats] * last[:, 2 * feats :]).reshape(2, 2, feats), 1)
    normed_mix, projected, mixed, gated, mixer_keep, mixer_send = mixer_forward(
        x_all, gain_mix, mix_in, halo, masks, taps, mix_out, tokens // 2
    )
    mixer_send, mixer_keep, dy_x = fence(mixer_send, mixer_keep, dy_x)

    mixer_got = ac.shift(mixer_send)
    dy_far = [dy_x, ac.shift(dy_x)]
    own_inputs = block_input.astype(F32)
    h = own_inputs + (mixer_keep + mixer_got)
    scale_ffn = lax.rsqrt(jnp.mean(h * h, axis=1, keepdims=True) + EPS)
    normed_own = (h * scale_ffn * gain_ffn[None, :]).astype(BF)
    normed_core = ac.shift(normed_own)

    normed_core, normed_own, h, scale_ffn = fence(normed_core, normed_own, h, scale_ffn)
    normed_x = ap.shift(normed_own)
    gathered = gathered.reshape(far, 2 * nz, 4, rows, 2 * hidden)
    gate_up = gathered.transpose(0, 2, 1, 3, 4).reshape(width, 2 * hidden)
    near = [normed_own, normed_core]
    dy_near = [cotangent, dy_core]
    near_ev, near_s = ffn_forward(near, gate_up, tokens // 2)
    tile = 384 if hidden % 384 == 0 else hidden
    spec = pl.BlockSpec((tile, width), lambda i: (i, 0))
    near_down = weight_grad([near_s], dy_near, tile, spec, (hidden, width), F32)
    normed_x, near_ev, near_s, near_down = fence(normed_x, near_ev, near_s, near_down)

    far_tokens = [normed_x, ac.shift(normed_x)]
    far_ev, far_s = ffn_forward(far_tokens, gate_up, tokens // 2)

    grad_down = weight_grad([far_s], dy_far, tile, spec, (hidden, width), BF, [near_down])
    far_ev, far_s, grad_down = fence(far_ev, far_s, grad_down)

    down_own, down_send = cut(grad_down.reshape(far, nz, 2, -1, width), ay, 2)
    down_got = shifted(down_send, ay)
    far_dev, far_keep, far_send = ffn_back(dy_far, far_ev, ffn_down, gate_up, tokens // 2)
    far_got = [ac.shift(part) for part in far_send]
    far_fed, far_fed_send = row_halves(times, far_s, ffn_down, width, tokens // 2)
    down_own, down_got, far_dev, far_keep, far_got, far_fed, far_fed_send, near_ev, dy_near = fence(
        down_own, down_got, far_dev, far_keep, far_got, far_fed, far_fed_send, near_ev, dy_near
    )

    down_own, down_send = cut(summed(down_own, down_got).astype(BF), az, 1)
    down_got = shifted(down_send, az)
    normed_x_got = ap.shift((far_keep + jnp.concatenate(far_got, 0)).astype(BF))
    near_dev, near_keep, near_send = ffn_back(dy_near, near_ev, ffn_down, gate_up, tokens // 2)
    grad_gate_up = gate_up_grad(near + far_tokens, [near_dev, far_dev], far, nz, rows)
    normed_x_got, near_keep, near_send, grad_gate_up, down_own, down_got = fence(
        normed_x_got, near_keep, near_send, grad_gate_up, down_own, down_got
    )

    quad = lax.psum_scatter(grad_gate_up, SPREAD, scatter_dimension=0, tiled=True)
    near_got = [ac.shift(part) for part in near_send]
    near_got, near_keep, far_fed_send, far_fed = fence(near_got, near_keep, far_fed_send, far_fed)
    far_fed_got = [ac.shift(part) for part in far_fed_send]
    (grad_hidden, hidden_own), grad_gain_ffn = norm_back(
        [[near_keep], near_got, [normed_x_got]], h, gain_ffn, cotangent, (F32, BF), tokens // 2
    )
    hidden_got = ac.shift(hidden_own)

    hidden_got, hidden_own, grad_hidden, far_fed, far_fed_got = fence(
        hidden_got, hidden_own, grad_hidden, far_fed, far_fed_got
    )
    fed_x = ap.shift((far_fed + jnp.concatenate(far_fed_got, 0)).astype(BF))
    hidden_low = [hidden_own, hidden_got]
    opening = jnp.concatenate([part[:2] for part in hidden_low], 0)
    branch = projected.reshape(2, tokens, wide_cols)[:, :2, feats : 2 * feats].reshape(4, feats)
    opening = contract_cols(opening, mix_out) * branch
    later = passed_along(opening.reshape(2, 2, feats), -1)
    back_args = (hidden_low, mix_out, projected, mixed, later, masks, taps)
    if nx == 2 and rows % 16 == 0 and 2 * nz * rows % 128 == 0:
        grad_projected, tap_grads, blocks = mixer_grads(
            *back_args, normed_mix, gated, here, nz, rows, few, tokens // 2
        )
    else:
        grad_projected, tap_grads = mixer_back(*back_args, tokens // 2)
        back_in = contract_rows(normed_mix, grad_projected).astype(BF)
        back_out = contract_rows(gated, jnp.concatenate(hidden_low, 0)).astype(BF)
        back_out = back_out.reshape(nx, nz, 2, rows, 2, feats).transpose(0, 4, 1, 2, 3, 5)
        back_mix = jnp.concatenate(
            [back_in.reshape(nx, 2, nz, 2, rows, wide_cols), back_out], 5
        )
        blocks = []
        for dx in (0,) + ax.steps:
            ys = [pick(pick(back_mix, ax.at(dx), 0), ay.at(dy), 2) for dy in range(2)]
            blocks.append([y[:, part] for part in (slice(few), slice(few, None)) for y in ys])
    blocks, grad_projected, near_s, fed_x = fence(blocks, grad_projected, near_s, fed_x)

    first_hop = [ay.shift(block[1]) for block in blocks[1:]]
    first_got = [ay.shift(blocks[0][1])]
    second_hop = [ax.shift(block[3], by) for block, by in zip(blocks[1:], ax.steps, strict=True)]
    mix_keep, mix_send, grad_gain_mix = input_grad(grad_projected, mix_in, x_all, tokens // 2)
    near_fed, near_fed_send = row_halves(times, near_s, ffn_down, width, tokens // 2)
    tap_rows = tap_grads[:3].reshape(3, nx, 1, feats // nx)
    on_core = (jnp.arange(2) == core).astype(F32)[None, None, :, None]
    tap_rows = (tap_rows * on_core).reshape(3, width)
    own_gain = jnp.concatenate([grad_gain_mix[None], grad_gain_ffn[None]], 0)
    terms = jnp.concatenate([own_gain, tap_rows], 0)
    first_hop, first_got, second_hop, blocks, mix_keep, mix_send, near_fed_send, terms = fence(
        first_hop, first_got, second_hop, blocks, mix_keep, mix_send, near_fed_send, terms
    )

    second_got = [ay.shift(summed(blocks[0][3], second_hop).astype(BF))]
    for n, by in enumerate(ax.steps):
        block = blocks[n + 1]
        first_got.append(ax.shift(summed(block[0], [first_hop[n]]).astype(BF), by))
        second_got.append(ax.shift(block[2], by))
    mix_got = [ac.shift(part) for part in mix_send]
    near_fed_got = [ac.shift(part) for part in near_fed_send]
    (grad_inputs,), _ = norm_back(
        [[mix_keep], mix_got], block_input, gain_mix, grad_hidden, (BF,), tokens // 4
    )
    for axis in (ac, ax):
        terms = summed(terms, [axis.shift(terms, by) for by in axis.steps])
    terms = terms.reshape(5, 2 * nx, nz, 2 * rows).transpose(2, 0, 1, 3).reshape(nz, -1)
    high = lax.reduce_precision(terms, 8, 7)
    terms = jnp.concatenate([high, terms - high], 1).astype(BF)
    extra = -(-terms.shape[1] // (2 * rows * 128)) * 128
    terms = jnp.pad(terms, ((0, 0), (0, 2 * rows * extra - terms.shape[1])))
    terms = terms.reshape(nz, 2, rows, extra).transpose(1, 0, 2, 3)
    first_got, second_got, blocks, grad_inputs, terms, near_fed_got = fence(
        first_got, second_got, blocks, grad_inputs, terms, near_fed_got
    )

    own_z = jnp.concatenate(
        [summed(blocks[0][0], first_got).astype(BF), summed(blocks[0][2], second_got).astype(BF)], 1
    )
    own_z = jnp.concatenate([own_z, terms], 3)
    mix_own, mix_send = cut(own_z, az, 1)
    mix_parts = shifted(mix_send, az)
    quad = quad.reshape(4, rows, 2 * hidden)
    quad = [pick(quad, (2 * ap.here + core) ^ step, 0) for step in range(4)]
    quad[1:] = [
        lax.ppermute(part, ("x", "core"), [(i, i ^ step) for i in range(4)])
        for step, part in enumerate(quad[1:], 1)
    ]
    mix_parts, mix_own, quad = fence(mix_parts, mix_own, quad)
    if far == 1 and hidden % 128 == 0 and rows % 16 == 0:
        joined = join_columns(quad, here)
    else:
        sides = [ordered(quad[n], quad[n + 1], core, 0) for n in (0, 2)]
        quads = ordered(*sides, ap.here, 0).astype(F32)
        joined = []
        for part in (quads[..., :hidden], quads[..., hidden:]):
            part = part.reshape(2, 2, rows, far, hidden // far)
            joined.append(jnp.transpose(part, (2, 3, 0, 1, 4)).reshape(rows, 4 * hidden))
    part_gate, part_rise = joined
    mix_sum = summed(mix_own, mix_parts)
    terms = mix_sum[..., wide_cols + feats :].reshape(-1)
    count = 5 * 4 * nx * rows
    terms = (terms[:count] + terms[count : 2 * count]).reshape(5, 4 * nx * rows)

    terms = terms + ay.shift(terms)
    at = ((ax.here * 2 + core) * 2 + ay.here) * rows
    part_down = summed(down_own, down_got)
    if far > 1:
        part_down = lax.psum_scatter(part_down, "far", scatter_dimension=0, tiled=True)
    part_down = part_down[0]
    block_output = (h + (near_fed + jnp.concatenate(near_fed_got, 0) + fed_x.astype(F32))).astype(BF)
    part_out = mix_sum[..., wide_cols : wide_cols + feats].transpose(1, 0, 2).reshape(rows, width)
    in_mine, in_send = cut(mix_sum[..., :wide_cols], ac, 0)
    in_got = shifted(in_send, ac)[0]
    blocks = (rows, 3 * nx, feats // nx)
    part_in = ordered(in_mine.reshape(blocks), in_got.reshape(blocks), core, 2)
    own_terms = lax.dynamic_slice_in_dim(terms, at, rows, 1)
    return (
        block_output,
        grad_inputs,
        part_in.reshape(rows, 3 * width),
        part_out,
        part_gate,
        part_rise,
        part_down,
        own_terms[0],
        own_terms[1],
        own_terms[2:].T,
    )


def solution(mesh):
    nd, nf = mesh.shape["dp"], mesh.shape["fsdp"]
    rows, line = P(AXES, None), P(AXES)
    return jax.shard_map(
        per_device,
        mesh=Mesh(mesh.devices.reshape(nd // 4, 2, 2, nf // 2, 2), AXES),
        in_specs=(rows,) * 6 + (line, line, rows, P(AXES[:3], None), rows),
        out_specs=(rows,) * 7 + (line, line, rows),
        check_vma=False,
    )
```

```python
import functools
import itertools
import math

import jax
import jax.numpy as jnp
from jax import lax
from jax.experimental import pallas as pl
from jax.experimental.pallas import tpu as pltpu
from jax.sharding import Mesh
from jax.sharding import PartitionSpec as P

EPS = 1e-05
AXES = ("far", "x", "core", "z", "y")
SPREAD = ("far", "z", "y")
BF = jnp.bfloat16
F32 = jnp.float32


class Axis:
    def __init__(self, name):
        self.name, self.size = name, lax.axis_size(name)
        self.here = lax.axis_index(name)
        near = sorted(range(1, self.size), key=lambda by: (min(by, self.size - by), by))
        self.steps = tuple(near)

    def shift(self, value, by=1):
        return lax.ppermute(value, self.name, [(i, (i + by) % self.size) for i in range(self.size)])

    def at(self, by):
        return lax.rem(self.here + by, self.size)


def passed_along(shard, by):
    peers = lax.axis_size(("z", "y"))
    pairs = [(i, i + by) for i in range(peers) if 0 <= i + by < peers]
    return lax.ppermute(shard, ("z", "y"), pairs)


def fence(*values):
    return lax.optimization_barrier(values)


def contract_rows(left, right):
    return lax.dot_general(
        left, right, (((0,), (0,)), ((), ())), preferred_element_type=F32
    )


def contract_cols(left, right):
    return lax.dot_general(
        left, right, (((1,), (1,)), ((), ())), preferred_element_type=F32
    )


def times(left, right):
    return jnp.dot(left, right, preferred_element_type=F32)


def pick(value, at, dim):
    return lax.dynamic_index_in_dim(value, at, dim, keepdims=False)


def ordered(mine, other, here, dim):
    low = jnp.where(here == 0, mine, other)
    high = jnp.where(here == 0, other, mine)
    return jnp.stack([low, high], dim)


def cut(value, axis, dim):
    return pick(value, axis.here, dim), [pick(value, axis.at(by), dim) for by in axis.steps]


def shifted(parts, axis):
    return [axis.shift(part, by) for part, by in zip(parts, axis.steps, strict=True)]


def summed(own, others):
    total = own.astype(F32)
    for other in others:
        total = total + other.astype(F32)
    return total


def place_body(moves, here_ref, *refs):
    sems = refs[-1]
    copies = []
    for i, (source, target) in enumerate(moves(here_ref, refs[:-1])):
        copy = pltpu.make_async_copy(source, target, sems.at[i])
        copy.start()
        copies.append(copy)
    for copy in copies:
        copy.wait()


def out_array(shape, kind):
    return pltpu.HBM(shape, kind) if math.prod(shape) >= 2**18 else jax.ShapeDtypeStruct(shape, kind)


def pinned(*arrays):
    return [
        pltpu.with_memory_space_constraint(a, pltpu.HBM) if a.size >= 2**18 else a for a in arrays
    ]


def kept(array):
    return pltpu.with_memory_space_constraint(array, pltpu.VMEM)


def place(moves, count, here, sources, shapes):
    return pl.pallas_call(
        functools.partial(place_body, moves),
        out_shape=[pltpu.VMEM(shape, BF) for shape in shapes],
        in_specs=[pl.BlockSpec(memory_space=pltpu.SMEM)]
        + [pl.BlockSpec(memory_space=pl.ANY)] * len(sources),
        out_specs=[pl.BlockSpec(memory_space=pltpu.VMEM)] * len(shapes),
        scratch_shapes=[pltpu.SemaphoreType.DMA((count,))],
        compiler_params=params(20),
        cost_estimate=pl.CostEstimate(flops=0, bytes_accessed=2**20, transcendentals=0),
    )(here, *pinned(*sources))


def back(at, by, size):
    return lax.rem(at + size - by, size)


def place_mix(pieces, here, ax, ay, az, columns, width):
    nx, ny, nz = ax.size, ay.size, az.size
    rows, half = pieces[0][3].shape[-2], width // 2

    def moves(at, refs):
        wide, small, narrow = refs[-3:]
        for (dx, dy, backs, _), source in zip(pieces, refs[:-3], strict=True):
            x, y = back(at[0], dx, nx), back(at[1], dy, ny)
            for n, dz in enumerate(backs):
                z = back(at[2], dz, nz)
                block = source.at[n]
                yield block.at[:, :, pl.ds(0, columns)], wide.at[x, :, z, y]
                yield block.at[:, :, pl.ds(columns, 128)], small.at[x, :, z, y]
                for k in range(2):
                    yield (
                        block.at[k, :, pl.ds(columns + 128, half)],
                        narrow.at[x, z, y, :, pl.ds(k * half, half)],
                    )

    lead = (nx, 2, nz, ny, rows)
    shapes = [lead + (columns,), lead + (128,), (nx, nz, ny, rows, width)]
    arrays = [piece[3] for piece in pieces]
    wide, small, narrow = place(moves, 4 * nx * ny * nz, here, arrays, shapes)
    return wide.reshape(-1, columns), small.reshape(-1, 128), narrow.reshape(-1, width)


def cost():
    return pl.CostEstimate(flops=0, bytes_accessed=2**16, transcendentals=0)


def params(mib):
    return pltpu.CompilerParams(vmem_limit_bytes=mib * 1024 * 1024)


def whole(array):
    return pl.BlockSpec(
        array.shape, lambda i: (0,) * array.ndim, pipeline_mode=pl.Buffered(1)
    )


def tiles(rows, columns):
    return pl.BlockSpec((rows, columns), lambda i: (i, 0))


def chunks(columns):
    step = 384 if columns % 384 == 0 else 128 if columns % 128 == 0 else columns
    return [(a, step) for a in range(0, columns, step)]


def logistic(v):
    return 0.5 * jnp.tanh(0.5 * v) + 0.5


def piece_specs(pieces, tile):
    specs = []
    for p, piece in enumerate(pieces):
        first, last = p * piece.shape[0] // tile, (p + 1) * piece.shape[0] // tile - 1

        def at(i, first=first, last=last):
            return jnp.clip(i - first, 0, last - first), 0

        specs.append(pl.BlockSpec((tile, piece.shape[1]), at))
    return specs


def piece_tile(refs):
    steps = pl.num_programs(0) // len(refs)
    value = refs[0][...]
    for p, ref in enumerate(refs[1:], 1):
        value = jnp.where(pl.program_id(0) >= p * steps, ref[...], value)
    return value


def forward_body(count, *refs):
    w_ref, ev_ref, s_ref = refs[count:]
    hidden = s_ref.shape[1]
    x = piece_tile(refs[:count])
    for a, n in chunks(hidden):
        gate = times(x, w_ref[:, a : a + n])
        rise = times(x, w_ref[:, hidden + a : hidden + a + n])
        ev_ref[:, a : a + n] = gate.astype(BF)
        ev_ref[:, hidden + a : hidden + a + n] = rise.astype(BF)
        s_ref[:, a : a + n] = (gate * logistic(gate) * rise).astype(BF)


def ffn_forward(pieces, w, tile):
    count, both = sum(piece.shape[0] for piece in pieces), w.shape[1]
    return pl.pallas_call(
        functools.partial(forward_body, len(pieces)),
        grid=(count // tile,),
        in_specs=piece_specs(pieces, tile) + [whole(w)],
        out_specs=[tiles(tile, both), tiles(tile, both // 2)],
        out_shape=[out_array((count, both), BF), out_array((count, both // 2), BF)],
        compiler_params=params(24),
        cost_estimate=cost(),
    )(*pinned(*pieces, w))


def back_body(count, half, *refs):
    ev_ref, down_ref, w_ref, dev_ref, keep_ref, *sends = refs[count:]
    hidden = down_ref.shape[0]
    dy = piece_tile(refs[:count])
    for a, n in chunks(hidden):
        back = contract_cols(dy, down_ref[a : a + n, :])
        gate = ev_ref[:, a : a + n].astype(F32)
        rise = ev_ref[:, hidden + a : hidden + a + n].astype(F32)
        sigma = logistic(gate)
        back = back * sigma
        dev_ref[:, a : a + n] = (back * rise * (1.0 + gate * (1.0 - sigma))).astype(BF)
        dev_ref[:, hidden + a : hidden + a + n] = (back * gate).astype(BF)
    split_pieces(half, contract_cols(dev_ref[...], w_ref[...]), keep_ref, sends)


def split_rows(half, value, keep_ref, send_ref):
    @pl.when(pl.program_id(0) < half)
    def _():
        keep_ref[...] = value

    @pl.when(pl.program_id(0) >= half)
    def _():
        send_ref[...] = value.astype(send_ref.dtype)


def split_specs(tile, columns, half):
    return [
        pl.BlockSpec((tile, columns), lambda i: (jnp.minimum(i, half - 1), 0)),
        pl.BlockSpec((tile, columns), lambda i: (jnp.maximum(i - half, 0), 0)),
    ]


def split_pieces(half, value, keep_ref, sends):
    cuts = len(sends) // half
    size = value.shape[0] // cuts

    @pl.when(pl.program_id(0) < half)
    def _():
        keep_ref[...] = value

    for n, ref in enumerate(sends):

        @pl.when(pl.program_id(0) == half + n // cuts)
        def _(n=n, ref=ref):
            at = n % cuts * size
            ref[...] = value[at : at + size].astype(ref.dtype)


def piece_outputs(count, width, tile, cuts):
    half, size = count // (2 * tile), tile // cuts
    specs = split_specs(tile, width, half)[:1]
    specs += [pl.BlockSpec((size, width), lambda i: (0, 0))] * (half * cuts)
    shapes = [out_array((count // 2, width), F32)]
    return specs, shapes + [out_array((size, width), BF)] * (half * cuts)


def ffn_back(pieces, ev, down, w, tile):
    count, both = ev.shape
    width, half = down.shape[1], count // (2 * tile)
    specs, shapes = piece_outputs(count, width, tile, 1)
    out = pl.pallas_call(
        functools.partial(back_body, len(pieces), half),
        grid=(2 * half,),
        in_specs=piece_specs(pieces, tile) + [tiles(tile, both), whole(down), whole(w)],
        out_specs=[tiles(tile, both)] + specs,
        out_shape=[pltpu.VMEM((count, both), BF)] + shapes,
        compiler_params=params(32),
        cost_estimate=cost(),
    )(*pinned(*pieces, ev, down, w))
    return out[0], out[1], out[2:]


def rows_body(function, half, left_ref, weight_ref, keep_ref, *sends):
    split_pieces(half, function(left_ref[...], weight_ref[...]), keep_ref, sends)


def row_halves(function, left, weight, width, tile):
    count = left.shape[0]
    half = count // (2 * tile)
    specs, shapes = piece_outputs(count, width, tile, 2)
    out = pl.pallas_call(
        functools.partial(rows_body, function, half),
        grid=(2 * half,),
        in_specs=[tiles(tile, left.shape[1]), whole(weight)],
        out_specs=specs,
        out_shape=shapes,
        compiler_params=params(20),
        cost_estimate=cost(),
    )(*pinned(left, weight))
    return out[0], out[1:]


def input_grad_body(half, dp_ref, win_ref, x_ref, keep_ref, *refs):
    sends, gain_ref = refs[:-1], refs[-1]
    value = contract_cols(dp_ref[...], win_ref[...])
    split_pieces(half, value, keep_ref, sends)
    x = x_ref[...].astype(F32)
    scale = lax.rsqrt(jnp.mean(x * x, axis=1, keepdims=True) + EPS)

    @pl.when(pl.program_id(0) == 0)
    def _():
        gain_ref[...] = jnp.zeros_like(gain_ref)

    gain_ref[...] += jnp.sum(value * (x * scale), axis=0, keepdims=True)


def input_grad(dp, win, x, tile):
    count, width = x.shape
    half = count // (2 * tile)
    specs, shapes = piece_outputs(count, width, tile, 2)
    out = pl.pallas_call(
        functools.partial(input_grad_body, half),
        grid=(2 * half,),
        in_specs=[tiles(tile, dp.shape[1]), whole(win), tiles(tile, width)],
        out_specs=specs + [pl.BlockSpec((1, width), lambda i: (0, 0))],
        out_shape=shapes + [jax.ShapeDtypeStruct((1, width), F32)],
        compiler_params=params(24),
        cost_estimate=cost(),
    )(*pinned(dp, win, x))
    return out[0], out[1:-1], out[-1][0]


def grad_body(lefts, rights, *refs):
    rest = refs[len(lefts) + len(rights) :]
    total = None
    for i, (first, end) in enumerate(lefts):
        for j, (start, stop) in enumerate(rights):
            low, high = max(first, start), min(end, stop)
            if low < high:
                left = refs[i][low - first : high - first, :]
                right = refs[len(lefts) + j][low - start : high - start, :]
                term = contract_rows(left, right)
                total = term if total is None else total + term
    for ref in rest[:-1]:
        total = total + ref[...]
    rest[-1][...] = total.astype(rest[-1].dtype).reshape(rest[-1].shape)


def token_spans(pieces):
    ends = list(itertools.accumulate(piece.shape[0] for piece in pieces))
    return list(zip([0] + ends[:-1], ends, strict=True))


def weight_grad(lefts, rights, tile, out_spec, shape, kind=BF, extra=(), stay=False):
    rows = lefts[0].shape[1]
    return pl.pallas_call(
        functools.partial(grad_body, token_spans(lefts), token_spans(rights)),
        grid=(rows // tile,),
        in_specs=[pl.BlockSpec((left.shape[0], tile), lambda i: (0, i)) for left in lefts]
        + [whole(right) for right in rights]
        + [out_spec] * len(extra),
        out_specs=out_spec,
        out_shape=out_array(shape, kind),
        compiler_params=params(34),
        cost_estimate=cost(),
    )(*pinned(*lefts), *(kept(right) if stay else pinned(right)[0] for right in rights), *pinned(*extra))


def gate_up_grad(lefts, rights, far, nz, rows):
    columns, width = rights[0].shape[1], lefts[0].shape[1]
    tile = 2 * nz * rows
    if tile % 128 == 0 and rows % 16 == 0:
        block = (1, 2 * nz, 1, rows, columns)
        spec = pl.BlockSpec(block, lambda i: (i // 4, 0, i % 4, 0, 0))
        out = weight_grad(lefts, rights, tile, spec, (far, 2 * nz, 4, rows, columns), stay=True)
    else:
        out = weight_grad(lefts, rights, 256, tiles(256, columns), (width, columns), stay=True)
        out = out.reshape(far, 4, 2 * nz, rows, columns).transpose(0, 2, 1, 3, 4)
    return out.reshape(width, columns)


def mixer_body(
    per_group, x_ref, gain_ref, win_ref, halo_ref, masks_ref, taps_ref, wout_ref, *refs
):
    normed_ref, projected_ref, mixed_ref, gated_ref, keep_ref, send_ref, rows, carry = refs
    count, feats = mixed_ref.shape
    x = x_ref[...].astype(F32)
    scale = lax.rsqrt(jnp.mean(x * x, axis=1, keepdims=True) + EPS)
    normed = (x * scale * gain_ref[...]).astype(BF)
    normed_ref[...] = normed
    projected = times(normed, win_ref[...])
    projected_ref[...] = projected
    product = projected[:, :feats] * projected[:, 2 * feats :]
    opens = lax.rem(pl.program_id(0), per_group) == 0
    rows[6:8, :] = jnp.where(opens, halo_ref[0], carry[...])
    rows[8 : 8 + count, :] = product
    mixed = taps_ref[2:3, :] * product
    mixed = mixed + masks_ref[:, 0:1] * (taps_ref[1:2, :] * rows[7 : 7 + count, :])
    mixed = mixed + masks_ref[:, 1:2] * (taps_ref[0:1, :] * rows[6 : 6 + count, :])
    carry[...] = product[count - 2 :]
    mixed_ref[...] = mixed
    gated = (projected[:, feats : 2 * feats] * mixed).astype(BF)
    gated_ref[...] = gated
    half = pl.num_programs(0) // 2
    split_rows(half, times(gated, wout_ref[...]), keep_ref, send_ref)


def mixer_forward(x, gain, win, halo, masks, taps, wout, tile):
    count, width = x.shape
    wide, feats = win.shape[1], wout.shape[0]
    per_group = count // (2 * tile)
    row = pl.BlockSpec((1, width), lambda i: (0, 0))
    return pl.pallas_call(
        functools.partial(mixer_body, per_group),
        grid=(2 * per_group,),
        in_specs=[
            tiles(tile, width),
            row,
            whole(win),
            pl.BlockSpec((1, 2, feats), lambda i: (i // per_group, 0, 0)),
            tiles(tile, masks.shape[1]),
            whole(taps),
            whole(wout),
        ],
        out_specs=[tiles(tile, width), tiles(tile, wide), tiles(tile, feats), tiles(tile, feats)]
        + split_specs(tile, width, per_group),
        out_shape=[
            out_array((count, width), BF),
            out_array((count, wide), F32),
            out_array((count, feats), F32),
            out_array((count, feats), BF),
        ]
        + [out_array((count // 2, width), kind) for kind in (F32, BF)],
        scratch_shapes=[pltpu.VMEM((tile + 8, feats), F32), pltpu.VMEM((2, feats), F32)],
        compiler_params=params(28),
        cost_estimate=cost(),
    )(*pinned(x, gain[None]), kept(win), *pinned(halo, masks, taps), kept(wout))


def mixer_back_body(
    per_group, dh_ref, dh2_ref, wout_ref, projected_ref, mixed_ref, halo_ref, masks_ref, *refs
):
    taps_ref, *refs = refs
    out_ref, grad_ref, rows, carry = refs
    count, feats = mixed_ref.shape
    projected = projected_ref[...]
    dh = jnp.where(pl.program_id(0) < per_group, dh_ref[...], dh2_ref[...])
    back = contract_cols(dh, wout_ref[...])
    grad_c = back * mixed_ref[...]
    grad_mixed = back * projected[:, feats : 2 * feats]
    closes = lax.rem(pl.program_id(0), per_group) == 0
    rows[0:count, :] = grad_mixed
    rows[count : count + 2, :] = jnp.where(closes, halo_ref[0], carry[...])
    carry[...] = grad_mixed[:2]
    ahead = (
        grad_mixed,
        masks_ref[:, 2:3] * rows[1 : 1 + count, :],
        masks_ref[:, 3:4] * rows[2 : 2 + count, :],
    )
    grad_product = sum(taps_ref[2 - lag : 3 - lag, :] * ahead[lag] for lag in range(3))
    b_branch, x_branch = projected[:, :feats], projected[:, 2 * feats :]
    out_ref[:, :feats] = (grad_product * x_branch).astype(BF)
    out_ref[:, feats : 2 * feats] = grad_c.astype(BF)
    out_ref[:, 2 * feats :] = (grad_product * b_branch).astype(BF)

    @pl.when(pl.program_id(0) == 0)
    def _():
        grad_ref[...] = jnp.zeros_like(grad_ref)

    product = b_branch * x_branch
    for lag in range(3):
        grad_ref[2 - lag : 3 - lag, :] += jnp.sum(product * ahead[lag], axis=0, keepdims=True)


def mixer_back(dh, wout, projected, mixed, halo, masks, taps, tile):
    count, wide = projected.shape
    width, feats = dh[0].shape[1], wout.shape[0]
    per_group = count // (2 * tile)

    def at(i):
        return (i // per_group) * per_group + per_group - 1 - lax.rem(i, per_group)

    def turned(columns):
        return pl.BlockSpec((tile, columns), lambda i: (at(i), 0))

    return pl.pallas_call(
        functools.partial(mixer_back_body, per_group),
        grid=(2 * per_group,),
        in_specs=[
            pl.BlockSpec((tile, width), lambda i: (jnp.maximum(per_group - 1 - i, 0), 0)),
            pl.BlockSpec(
                (tile, width), lambda i: (jnp.minimum(2 * per_group - 1 - i, per_group - 1), 0)
            ),
            whole(wout),
            turned(wide),
            turned(feats),
            pl.BlockSpec((1, 2, feats), lambda i: (i // per_group, 0, 0)),
            turned(masks.shape[1]),
            whole(taps),
        ],
        out_specs=[turned(wide), pl.BlockSpec((8, feats), lambda i: (0, 0))],
        out_shape=[
            out_array((count, wide), BF),
            out_array((8, feats), F32),
        ],
        scratch_shapes=[pltpu.VMEM((tile + 8, feats), F32), pltpu.VMEM((2, feats), F32)],
        compiler_params=params(24),
        cost_estimate=cost(),
    )(*pinned(*dh, wout, projected, mixed, halo, masks, taps))


def mixer_grads_body(per_group, lower, here_ref, normed_ref, gated_ref, *refs):
    ins, out_ref, grad_ref = refs[:8], refs[8], refs[9]
    blocks, (rows, carry, in_sum, out_sum) = refs[10:18], refs[18:]
    mixer_back_body(per_group, *ins, out_ref, grad_ref, rows, carry)
    width, wide = in_sum.shape
    tile = width // 4

    @pl.when(pl.program_id(0) == 0)
    def _():
        in_sum[...] = jnp.zeros_like(in_sum)
        out_sum[...] = jnp.zeros_like(out_sum)

    grad = out_ref[...]
    dh = jnp.where(pl.program_id(0) < per_group, ins[0][...], ins[1][...])
    for q in range(4):
        part = slice(q * tile, (q + 1) * tile)
        in_sum[part, :] += contract_rows(normed_ref[:, part], grad)
    for x in range(2):
        part = slice(x * tile, (x + 1) * tile)
        out_sum[part, :] += contract_rows(gated_ref[:, part], dh)

    @pl.when(pl.program_id(0) == pl.num_programs(0) - 1)
    def _():
        own_y = here_ref[1] == 0
        half = width // 2
        for dx in range(2):
            x = lax.rem(here_ref[0] + dx, 2)
            for k in range(2):
                q = pl.multiple_of((2 * x + k) * tile, tile)
                parts = (
                    (in_sum[pl.ds(q, tile), :], slice(0, wide)),
                    (
                        out_sum[pl.ds(pl.multiple_of(x * tile, tile), tile), k * half : (k + 1) * half],
                        slice(wide, wide + half),
                    ),
                )
                for value, where in parts:
                    value = value.astype(BF).reshape(-1, 2, blocks[0].shape[2], value.shape[1])
                    low, high = value[:, 0], value[:, 1]
                    own, other = jnp.where(own_y, low, high), jnp.where(own_y, high, low)
                    cuts = (own[:lower], other[:lower], own[lower:], other[lower:])
                    for cut_, target in zip(cuts, blocks[4 * dx : 4 * dx + 4], strict=True):
                        target[k, :, :, where] = cut_


def mixer_grads(dh, wout, projected, mixed, halo, masks, taps, normed, gated, here, nz, rows, lower, tile):
    count, wide = projected.shape
    width, feats = dh[0].shape[1], wout.shape[0]
    per_group = count // (2 * tile)

    def at(i):
        return (i // per_group) * per_group + per_group - 1 - lax.rem(i, per_group)

    def turned(columns):
        return pl.BlockSpec((tile, columns), lambda i: (at(i), 0))

    def fixed(shape):
        return pl.BlockSpec(shape, lambda i: (0,) * len(shape))

    columns = wide + width // 2
    shapes = [(2, n, rows, columns) for n in (lower, lower, nz - lower, nz - lower)] * 2
    out = pl.pallas_call(
        functools.partial(mixer_grads_body, per_group, lower),
        grid=(2 * per_group,),
        in_specs=[
            pl.BlockSpec(memory_space=pltpu.SMEM),
            turned(width),
            turned(feats),
            pl.BlockSpec((tile, width), lambda i: (jnp.maximum(per_group - 1 - i, 0), 0)),
            pl.BlockSpec(
                (tile, width), lambda i: (jnp.minimum(2 * per_group - 1 - i, per_group - 1), 0)
            ),
            whole(wout),
            turned(wide),
            turned(feats),
            pl.BlockSpec((1, 2, feats), lambda i: (i // per_group, 0, 0)),
            turned(masks.shape[1]),
            whole(taps),
        ],
        out_specs=[turned(wide), fixed((8, feats))] + [fixed(shape) for shape in shapes],
        out_shape=[out_array((count, wide), BF), out_array((8, feats), F32)]
        + [out_array(shape, BF) for shape in shapes],
        scratch_shapes=[
            pltpu.VMEM((tile + 8, feats), F32),
            pltpu.VMEM((2, feats), F32),
            pltpu.VMEM((width, wide), F32),
            pltpu.VMEM((feats, width), F32),
        ],
        compiler_params=params(46),
        cost_estimate=cost(),
    )(here, *pinned(normed, gated, *dh, wout, projected, mixed, halo, masks, taps))
    return out[0], out[1], [out[2:6], out[6:]]


def norm_back_body(counts, *refs):
    grad, refs = 0.0, list(refs)
    for count in counts:
        grad = grad + piece_tile(refs[:count]).astype(F32)
        refs = refs[count:]
    x_ref, gain_ref, up_ref, *outs = refs
    x = x_ref[...].astype(F32)
    scale = lax.rsqrt(jnp.mean(x * x, axis=1, keepdims=True) + EPS)
    scaled = x * scale
    weighted = grad * gain_ref[...]
    mean = jnp.mean(weighted * scaled, axis=1, keepdims=True)
    out = up_ref[...].astype(F32) + scale * (weighted - scaled * mean)
    for ref in outs[:-1]:
        ref[...] = out.astype(ref.dtype)

    @pl.when(pl.program_id(0) == 0)
    def _():
        outs[-1][...] = jnp.zeros_like(outs[-1])

    outs[-1][...] += jnp.sum(grad * scaled, axis=0, keepdims=True)


def norm_back(grads, x, gain, upstream, kinds, tile):
    count, width = x.shape
    line = pl.BlockSpec((1, width), lambda i: (0, 0))
    specs = [spec for pieces in grads for spec in piece_specs(pieces, tile)]
    out = pl.pallas_call(
        functools.partial(norm_back_body, [len(pieces) for pieces in grads]),
        grid=(count // tile,),
        in_specs=specs + [tiles(tile, width), line, tiles(tile, width)],
        out_specs=[tiles(tile, width)] * len(kinds) + [line],
        out_shape=[out_array((count, width), kind) for kind in kinds]
        + [jax.ShapeDtypeStruct((1, width), F32)],
        compiler_params=params(16),
        cost_estimate=cost(),
    )(*pinned(*[piece for pieces in grads for piece in pieces], x, gain[None], upstream))
    return out[:-1], out[-1][0]


def join_body(here_ref, *refs):
    sets, outs = refs[:4], refs[4:]
    own, hidden = here_ref[3], outs[0].shape[1] // 4
    for half, out_ref in enumerate(outs):
        for block in range(4):
            value = sets[block][:, half * hidden : (half + 1) * hidden]
            for at in range(1, 4):
                other = sets[block ^ at][:, half * hidden : (half + 1) * hidden]
                value = jnp.where(own == at, other, value)
            out_ref[:, block * hidden : (block + 1) * hidden] = value.astype(F32)


def join_columns(sets, here):
    rows, both = sets[0].shape
    return pl.pallas_call(
        join_body,
        in_specs=[pl.BlockSpec(memory_space=pltpu.SMEM)]
        + [pl.BlockSpec(memory_space=pltpu.VMEM)] * 4,
        out_specs=[pl.BlockSpec(memory_space=pltpu.VMEM)] * 2,
        out_shape=[jax.ShapeDtypeStruct((rows, 2 * both), F32)] * 2,
        compiler_params=params(12),
        cost_estimate=cost(),
    )(here, *sets)


def per_device(
    block_input,
    in_weight,
    out_weight,
    gate_weight,
    up_weight,
    down_weight,
    norm_gain,
    ffn_gain,
    conv_weight,
    seq_starts,
    cotangent,
):
    ax, ac, az, ay = Axis(("far", "x")), Axis("core"), Axis("z"), Axis("y")
    ap = Axis("x")
    nx, nz, far = ax.size, az.size, lax.axis_size("far")
    core = ac.here
    here = jnp.stack([ax.here, ay.here, az.here, 2 * ap.here + core]).astype(jnp.int32)
    tokens, width = block_input.shape
    rows = in_weight.shape[0]
    hidden = gate_weight.shape[1] // 4
    feats = width // 2
    wide_cols = 3 * feats
    lower = nz // 2
    few = max(1, nz // 4)
    z_back = (0,) + az.steps
    first_back, second_back = z_back[:lower], z_back[lower:]

    small = jnp.concatenate(
        [norm_gain[:, None], ffn_gain[:, None], conv_weight, jnp.zeros((rows, 123), F32)], 1
    ).astype(BF)
    in_sets = in_weight.astype(BF).reshape(rows, 3 * nx, 2, feats // nx)

    def in_part(which):
        return jnp.concatenate([pick(in_sets, which, 2).reshape(rows, wide_cols), small], 1)

    in_mine, in_got = in_part(core), ac.shift(in_part(1 - core))
    starts_core = ac.shift(seq_starts)

    def split_hidden(weight):
        cut = weight.astype(BF).reshape(rows, far, 2, 2, hidden // far)
        return jnp.transpose(cut, (2, 3, 0, 1, 4)).reshape(2, 2, rows, hidden)

    in_mine, in_got, gate_weight, up_weight = fence(in_mine, in_got, gate_weight, up_weight)
    out_low = out_weight.astype(BF).reshape(rows, 2, feats).transpose(1, 0, 2)
    mix = jnp.concatenate([ordered(in_mine, in_got, core, 0), out_low], 2)
    mix_z = {by: az.shift(mix, by) for by in first_back[1:]}
    gate_up = jnp.concatenate([split_hidden(gate_weight), split_hidden(up_weight)], 3)
    pair_mine = pick(gate_up, core, 1)
    pair_send = jnp.split(pick(gate_up, 1 - core, 1), 2, 2)
    pair_got = jnp.concatenate([ac.shift(part) for part in pair_send], 2)

    pair_mine, pair_got, mix, mix_z, cotangent, down_low = fence(
        pair_mine, pair_got, mix, mix_z, cotangent, down_weight.astype(BF)
    )
    first = jnp.stack([mix] + [mix_z[by] for by in first_back[1:]])
    first_y = ay.shift(first)
    second = [az.shift(mix, by) for by in second_back]
    pair = ordered(pair_mine, pair_got, core, 1)
    quad_mine, quad_got = pick(pair, ap.here, 0), ap.shift(pick(pair, 1 - ap.here, 0))
    quad = ordered(quad_mine, quad_got, ap.here, 0)
    first_x = [ax.shift(first, by) for by in ax.steps]
    second, first, first_y, first_x, quad, down_low = fence(
        second, first, first_y, first_x, quad, down_low
    )

    gathered = lax.all_gather(quad.reshape(4 * rows, 2 * hidden), SPREAD, axis=0, tiled=True)
    second = jnp.stack(second)
    second_x = [ax.shift(second, by) for by in ax.steps]
    second_y = ay.shift(second)
    second_x, second_y, second, first_y, block_input, cotangent, down_low = fence(
        second_x, second_y, second, first_y, block_input, cotangent, down_low
    )

    ffn_down = lax.all_gather(down_low, SPREAD, axis=0, tiled=True)
    first_yx = [ax.shift(first_y, by) for by in ax.steps]
    second_xy = [ay.shift(part) for part in second_x]
    x_core = ac.shift(block_input)
    dy_core = ac.shift(cotangent)
    x_all = jnp.concatenate([block_input, x_core], 0)
    starts = jnp.concatenate([seq_starts, starts_core], 0)
    position = lax.axis_index(("z", "y")) * tokens + jnp.arange(tokens + 2, dtype=jnp.int32)
    reached = starts[:, None, :] <= position[None, :, None]
    offset = position[None, :] - jnp.max(jnp.where(reached, starts[:, None, :], 0), axis=2)
    masks = [offset[:, :tokens] >= 1, offset[:, :tokens] >= 2]
    masks += [offset[:, 1 : 1 + tokens] >= 1, offset[:, 2:] >= 2]
    masks = jnp.stack(masks, 2).astype(F32).reshape(2 * tokens, 4)
    first_yx, second_xy, first, second, x_all, dy_core, masks, cotangent = fence(
        first_yx, second_xy, first, second, x_all, dy_core, masks, cotangent
    )

    dy_x = ap.shift(cotangent)
    pieces = [(0, 0, first_back, first), (0, 1, first_back, first_y)]
    pieces += [(0, 0, second_back, second), (0, 1, second_back, second_y)]
    for n, dx in enumerate(ax.steps):
        pieces += [(dx, 0, first_back, first_x[n]), (dx, 1, first_back, first_yx[n])]
        pieces += [(dx, 0, second_back, second_x[n]), (dx, 1, second_back, second_xy[n])]
    mix_in, tiny, mix_out = place_mix(pieces, here, ax, ay, az, wide_cols, width)
    tiny = tiny[:, :8].astype(F32)
    gain_mix, gain_ffn = tiny[:, 0], tiny[:, 1]
    taps = pick(tiny[:, 2:5].reshape(nx, 2, feats // nx, 3), core, 1).reshape(feats, 3)

    taps = jnp.concatenate([taps.T, jnp.zeros((5, feats), F32)], 0)

    last = x_all.reshape(2, tokens, width)[:, tokens - 2 :].reshape(4, width).astype(F32)
    scale = lax.rsqrt(jnp.mean(last * last, axis=1, keepdims=True) + EPS)
    last = times((last * scale * gain_mix[None, :]).astype(BF), mix_in)
    halo = passed_along((last[:, :feats] * last[:, 2 * feats :]).reshape(2, 2, feats), 1)
    normed_mix, projected, mixed, gated, mixer_keep, mixer_send = mixer_forward(
        x_all, gain_mix, mix_in, halo, masks, taps, mix_out, tokens // 2
    )
    mixer_send, mixer_keep, dy_x = fence(mixer_send, mixer_keep, dy_x)

    mixer_got = ac.shift(mixer_send)
    dy_far = [dy_x, ac.shift(dy_x)]
    own_inputs = block_input.astype(F32)
    h = own_inputs + (mixer_keep + mixer_got)
    scale_ffn = lax.rsqrt(jnp.mean(h * h, axis=1, keepdims=True) + EPS)
    normed_own = (h * scale_ffn * gain_ffn[None, :]).astype(BF)
    normed_core = ac.shift(normed_own)

    normed_core, normed_own, h, scale_ffn = fence(normed_core, normed_own, h, scale_ffn)
    normed_x = ap.shift(normed_own)
    gathered = gathered.reshape(far, 2 * nz, 4, rows, 2 * hidden)
    gate_up = gathered.transpose(0, 2, 1, 3, 4).reshape(width, 2 * hidden)
    near = [normed_own, normed_core]
    dy_near = [cotangent, dy_core]
    near_ev, near_s = ffn_forward(near, gate_up, tokens // 2)
    tile = 384 if hidden % 384 == 0 else hidden
    spec = pl.BlockSpec((tile, width), lambda i: (i, 0))
    near_down = weight_grad([near_s], dy_near, tile, spec, (hidden, width), F32)
    normed_x, near_ev, near_s, near_down = fence(normed_x, near_ev, near_s, near_down)

    far_tokens = [normed_x, ac.shift(normed_x)]
    far_ev, far_s = ffn_forward(far_tokens, gate_up, tokens // 2)

    grad_down = weight_grad([far_s], dy_far, tile, spec, (hidden, width), BF, [near_down])
    far_ev, far_s, grad_down = fence(far_ev, far_s, grad_down)

    down_own, down_send = cut(grad_down.reshape(far, nz, 2, -1, width), ay, 2)
    down_got = shifted(down_send, ay)
    far_dev, far_keep, far_send = ffn_back(dy_far, far_ev, ffn_down, gate_up, tokens // 2)
    far_got = [ac.shift(part) for part in far_send]
    far_fed, far_fed_send = row_halves(times, far_s, ffn_down, width, tokens // 2)
    down_own, down_got, far_dev, far_keep, far_got, far_fed, far_fed_send, near_ev, dy_near = fence(
        down_own, down_got, far_dev, far_keep, far_got, far_fed, far_fed_send, near_ev, dy_near
    )

    down_own, down_send = cut(summed(down_own, down_got).astype(BF), az, 1)
    down_got = shifted(down_send, az)
    normed_x_got = ap.shift((far_keep + jnp.concatenate(far_got, 0)).astype(BF))
    near_dev, near_keep, near_send = ffn_back(dy_near, near_ev, ffn_down, gate_up, tokens // 2)
    grad_gate_up = gate_up_grad(near + far_tokens, [near_dev, far_dev], far, nz, rows)
    normed_x_got, near_keep, near_send, grad_gate_up, down_own, down_got = fence(
        normed_x_got, near_keep, near_send, grad_gate_up, down_own, down_got
    )

    quad = lax.psum_scatter(grad_gate_up, SPREAD, scatter_dimension=0, tiled=True)
    near_got = [ac.shift(part) for part in near_send]
    far_fed_got = [ac.shift(part) for part in far_fed_send]
    near_got, near_keep, far_fed_got, far_fed = fence(near_got, near_keep, far_fed_got, far_fed)
    (grad_hidden, hidden_own), grad_gain_ffn = norm_back(
        [[near_keep], near_got, [normed_x_got]], h, gain_ffn, cotangent, (F32, BF), tokens // 2
    )
    fed_x = ap.shift((far_fed + jnp.concatenate(far_fed_got, 0)).astype(BF))

    head = hidden_own[:2]
    head_got = ac.shift(head)
    hidden_got = ac.shift(hidden_own)
    head_got, head, grad_hidden = fence(head_got, head, grad_hidden)
    hidden_low = [hidden_own, hidden_got]
    opening = jnp.concatenate([head, head_got], 0)
    branch = projected.reshape(2, tokens, wide_cols)[:, :2, feats : 2 * feats].reshape(4, feats)
    opening = contract_cols(opening, mix_out) * branch
    later = passed_along(opening.reshape(2, 2, feats), -1)
    back_args = (hidden_low, mix_out, projected, mixed, later, masks, taps)
    if nx == 2 and rows % 16 == 0 and 2 * nz * rows % 128 == 0:
        grad_projected, tap_grads, blocks = mixer_grads(
            *back_args, normed_mix, gated, here, nz, rows, few, tokens // 2
        )
    else:
        grad_projected, tap_grads = mixer_back(*back_args, tokens // 2)
        back_in = contract_rows(normed_mix, grad_projected).astype(BF)
        back_out = contract_rows(gated, jnp.concatenate(hidden_low, 0)).astype(BF)
        back_out = back_out.reshape(nx, nz, 2, rows, 2, feats).transpose(0, 4, 1, 2, 3, 5)
        back_mix = jnp.concatenate(
            [back_in.reshape(nx, 2, nz, 2, rows, wide_cols), back_out], 5
        )
        blocks = []
        for dx in (0,) + ax.steps:
            ys = [pick(pick(back_mix, ax.at(dx), 0), ay.at(dy), 2) for dy in range(2)]
            blocks.append([y[:, part] for part in (slice(few), slice(few, None)) for y in ys])
    blocks, grad_projected, near_s, fed_x = fence(blocks, grad_projected, near_s, fed_x)

    first_hop = [ay.shift(block[1]) for block in blocks[1:]]
    first_got = [ay.shift(blocks[0][1])]
    second_hop = [ax.shift(block[3], by) for block, by in zip(blocks[1:], ax.steps, strict=True)]
    mix_keep, mix_send, grad_gain_mix = input_grad(grad_projected, mix_in, x_all, tokens // 2)
    near_fed, near_fed_send = row_halves(times, near_s, ffn_down, width, tokens // 2)
    tap_rows = tap_grads[:3].reshape(3, nx, 1, feats // nx)
    on_core = (jnp.arange(2) == core).astype(F32)[None, None, :, None]
    tap_rows = (tap_rows * on_core).reshape(3, width)
    own_gain = jnp.concatenate([grad_gain_mix[None], grad_gain_ffn[None]], 0)
    terms = jnp.concatenate([own_gain, tap_rows], 0)
    first_hop, first_got, second_hop, blocks, mix_keep, mix_send, near_fed_send, terms = fence(
        first_hop, first_got, second_hop, blocks, mix_keep, mix_send, near_fed_send, terms
    )

    second_got = [ay.shift(summed(blocks[0][3], second_hop).astype(BF))]
    for n, by in enumerate(ax.steps):
        block = blocks[n + 1]
        first_got.append(ax.shift(summed(block[0], [first_hop[n]]).astype(BF), by))
        second_got.append(ax.shift(block[2], by))
    mix_got = [ac.shift(part) for part in mix_send]
    near_fed_got = [ac.shift(part) for part in near_fed_send]
    (grad_inputs,), _ = norm_back(
        [[mix_keep], mix_got], block_input, gain_mix, grad_hidden, (BF,), tokens // 4
    )
    for axis in (ac, ax):
        terms = summed(terms, [axis.shift(terms, by) for by in axis.steps])
    terms = terms.reshape(5, 2 * nx, nz, 2 * rows).transpose(2, 0, 1, 3).reshape(nz, -1)
    high = lax.reduce_precision(terms, 8, 7)
    terms = jnp.concatenate([high, terms - high], 1).astype(BF)
    extra = -(-terms.shape[1] // (2 * rows * 128)) * 128
    terms = jnp.pad(terms, ((0, 0), (0, 2 * rows * extra - terms.shape[1])))
    terms = terms.reshape(nz, 2, rows, extra).transpose(1, 0, 2, 3)
    first_got, second_got, blocks, grad_inputs, terms, near_fed_got = fence(
        first_got, second_got, blocks, grad_inputs, terms, near_fed_got
    )

    own_z = jnp.concatenate(
        [summed(blocks[0][0], first_got).astype(BF), summed(blocks[0][2], second_got).astype(BF)], 1
    )
    own_z = jnp.concatenate([own_z, terms], 3)
    mix_own, mix_send = cut(own_z, az, 1)
    mix_parts = shifted(mix_send, az)
    quad = quad.reshape(4, rows, 2 * hidden)
    quad = [pick(quad, (2 * ap.here + core) ^ step, 0) for step in range(4)]
    quad[1:] = [
        lax.ppermute(part, ("x", "core"), [(i, i ^ step) for i in range(4)])
        for step, part in enumerate(quad[1:], 1)
    ]
    mix_parts, mix_own, quad = fence(mix_parts, mix_own, quad)
    if far == 1 and hidden % 128 == 0 and rows % 16 == 0:
        joined = join_columns(quad, here)
    else:
        sides = [ordered(quad[n], quad[n + 1], core, 0) for n in (0, 2)]
        quads = ordered(*sides, ap.here, 0).astype(F32)
        joined = []
        for part in (quads[..., :hidden], quads[..., hidden:]):
            part = part.reshape(2, 2, rows, far, hidden // far)
            joined.append(jnp.transpose(part, (2, 3, 0, 1, 4)).reshape(rows, 4 * hidden))
    part_gate, part_rise = joined
    mix_sum = summed(mix_own, mix_parts)
    terms = mix_sum[..., wide_cols + feats :].reshape(-1)
    count = 5 * 4 * nx * rows
    terms = (terms[:count] + terms[count : 2 * count]).reshape(5, 4 * nx * rows)

    terms = terms + ay.shift(terms)
    at = ((ax.here * 2 + core) * 2 + ay.here) * rows
    part_down = summed(down_own, down_got)
    if far > 1:
        part_down = lax.psum_scatter(part_down, "far", scatter_dimension=0, tiled=True)
    part_down = part_down[0]
    block_output = (h + (near_fed + jnp.concatenate(near_fed_got, 0) + fed_x.astype(F32))).astype(BF)
    part_out = mix_sum[..., wide_cols : wide_cols + feats].transpose(1, 0, 2).reshape(rows, width)
    in_mine, in_send = cut(mix_sum[..., :wide_cols], ac, 0)
    in_got = shifted(in_send, ac)[0]
    blocks = (rows, 3 * nx, feats // nx)
    part_in = ordered(in_mine.reshape(blocks), in_got.reshape(blocks), core, 2)
    own_terms = lax.dynamic_slice_in_dim(terms, at, rows, 1)
    return (
        block_output,
        grad_inputs,
        part_in.reshape(rows, 3 * width),
        part_out,
        part_gate,
        part_rise,
        part_down,
        own_terms[0],
        own_terms[1],
        own_terms[2:].T,
    )


def solution(mesh):
    nd, nf = mesh.shape["dp"], mesh.shape["fsdp"]
    rows, line = P(AXES, None), P(AXES)
    return jax.shard_map(
        per_device,
        mesh=Mesh(mesh.devices.reshape(nd // 4, 2, 2, nf // 2, 2), AXES),
        in_specs=(rows,) * 6 + (line, line, rows, P(AXES[:3], None), rows),
        out_specs=(rows,) * 7 + (line, line, rows),
        check_vma=False,
    )
```
